128 devices in a mesh: ent: 8 (over z, x_lo), qry: 16 (over y, x_hi, core).
Axes of the slice: x: 4 (x_hi: 2, x_lo: 2; x = x_hi * 2 + x_lo), y: 4, z: 4, core: 2. Of those that a mesh axis runs over, the one named last changes fastest.
Arguments:
- anchor_ids: int32 [16384, 20], P(('ent', 'qry')), may hold values from 0 to 19999
- relation_ids: int32 [16384, 5], P(('ent', 'qry')), may hold values from 0 to 821
- head_anchors: int32 [65536, 20], P(('ent', 'qry')), may hold values from 0 to 19999
- head_relations: int32 [65536, 5], P(('ent', 'qry')), may hold values from 0 to 821
- query_relation: int32 [65536], P(('ent', 'qry')), may hold values from 0 to 821
- targets: int32 [65536, 4], P(('ent', 'qry')), may hold values from 0 to 16383
- anchor_table: bfloat16 [20000, 200], replicated, may hold values from -6 to 6
- relation_table: bfloat16 [822, 200], replicated, may hold values from -6 to 6
- enc_weight: bfloat16 [5000, 200], replicated, may hold values from -0.078125 to 0.078125
- fc_weight: bfloat16 [200, 200], replicated, may hold values from -0.4375 to 0.4375
Outputs:
- entity_grad: float32 [200, 16384], P(None, ('ent', 'qry'))
- query_grad: float32 [65536, 200], P(('ent', 'qry'))
The draws below stay inside these ranges and needn't reach their ends.
All inputs are finite; a program needn't handle non-finite values.
Results may differ from the reference program's by a relative error of at most 0.019.
Values may be sent and summed in bfloat16 or wider, within the bound.
No kernel may reach another device: no remote copies, remote signals or barrier semaphores. Data moves between devices by JAX's collectives and lax.ppermute only.
A program may use at most 128 MiB of HBM per device.

```python
import math
import jax
import jax.numpy as jnp
import numpy as np
from jax import lax

D = 200
ANCHORS = 20000
RELS = 822
NANC = 20
NRT = 5
TARGETS = 4
ENTITIES = 16384
QUERIES = 65536
N_ENT = 8


def with_ends(result, rng, low, top_value):
    place = [jax.random.randint(jax.random.fold_in(rng, axis), (), 0, length) for axis, length in enumerate(result.shape)]
    longest = result.shape.index(max(result.shape))
    neighbour = place[:longest] + [(place[longest] + 1) % result.shape[longest]] + place[longest + 1:]
    return result.at[tuple(place)].set(low).at[tuple(neighbour)].set(top_value)


def rank_table(number_of, lean):
    portions = [(1 << 20) // math.isqrt(grade ** lean) + 1 for grade in range(1, number_of + 1)]
    deviation = 1 + sum(portions) // (1 << 30)
    return np.cumsum(np.array([max(1, weight // deviation) for weight in portions]))


def skewed_ids(key, shape, number_of, slope):
    grid = rank_table(number_of, slope)
    lot = jax.random.randint(jax.random.fold_in(key, 1), shape, 0, int(grid[number_of - 1]))
    grade = jnp.searchsorted(jnp.asarray(grid, jnp.int32), lot, side="right")
    return jax.random.permutation(jax.random.fold_in(key, 2), number_of)[grade].astype(jnp.int32)


def scatter_about(rng, extent, spread, bound, kind=jnp.bfloat16):
    values = spread * jax.random.normal(rng, extent, jnp.float32)
    return jnp.clip(values, min=-bound, max=bound).astype(kind)


def setup_inputs(seed: int = 0) -> dict:
    key_list = jax.random.split(jax.random.key(seed), 11)
    anchor_ids = with_ends(jax.random.randint(key_list[0], (ENTITIES, NANC), 0, ANCHORS), jax.random.fold_in(key_list[0], 1), 0, ANCHORS - 1).astype(jnp.int32)
    relation_ids = with_ends(jax.random.randint(key_list[1], (ENTITIES, NRT), 0, RELS), jax.random.fold_in(key_list[1], 1), 0, RELS - 1).astype(jnp.int32)
    head_anchors = with_ends(jax.random.randint(key_list[2], (QUERIES, NANC), 0, ANCHORS), jax.random.fold_in(key_list[2], 1), 0, ANCHORS - 1).astype(jnp.int32)
    head_relations = with_ends(jax.random.randint(key_list[3], (QUERIES, NRT), 0, RELS), jax.random.fold_in(key_list[3], 1), 0, RELS - 1).astype(jnp.int32)
    query_relation = with_ends(jax.random.randint(key_list[4], (QUERIES,), 0, RELS), jax.random.fold_in(key_list[4], 1), 0, RELS - 1).astype(jnp.int32)
    targets = with_ends(skewed_ids(key_list[5], (QUERIES, TARGETS), ENTITIES, 1), jax.random.fold_in(key_list[5], 3), 0, ENTITIES - 1).astype(jnp.int32)
    anchor_table = scatter_about(key_list[6], (ANCHORS, D), 1.0, 6.0)
    relation_table = scatter_about(key_list[7], (RELS, D), 1.0, 6.0)
    enc_weight = jnp.clip(jax.random.uniform(key_list[8], ((NANC + NRT) * D, D), jnp.float32, -0.078125, 0.078125), -0.078125, 0.078125).astype(jnp.bfloat16)
    fc_weight = scatter_about(key_list[9], (D, D), D ** -0.5, 0.4375)
    return {"anchor_ids": anchor_ids, "relation_ids": relation_ids, "head_anchors": head_anchors, "head_relations": head_relations, "query_relation": query_relation, "targets": targets, "anchor_table": anchor_table, "relation_table": relation_table, "enc_weight": enc_weight, "fc_weight": fc_weight}


def encode(anchor_ids, relation_ids, anchor_table, relation_table, enc_weight):
    rows = jnp.concatenate([jnp.take(anchor_table, anchor_ids, axis=0), jnp.take(relation_table, relation_ids, axis=0)], axis=1)
    flat = rows.reshape(rows.shape[0], -1)
    return lax.dot_general(enc_weight, flat, (((0,), (1,)), ((), ())), preferred_element_type=jnp.float32).astype(jnp.bfloat16)

def make_query(head_anchors, head_relations, query_relation, anchor_table, relation_table, enc_weight, fc_weight):
    head_cols = encode(head_anchors, head_relations, anchor_table, relation_table, enc_weight)
    relation_rows = jnp.take(relation_table, query_relation, axis=0)
    mixed = (head_cols.T.astype(jnp.float32) * relation_rows.astype(jnp.float32)).astype(jnp.bfloat16)
    return jnp.tanh(jnp.dot(mixed, fc_weight, preferred_element_type=jnp.float32)).astype(jnp.bfloat16)

def score_terms(query, chosen, block_cols, first, total_entities):
    ident = first + jnp.arange(block_cols.shape[1], dtype=jnp.int32)
    scores = jnp.dot(query, block_cols, preferred_element_type=jnp.float32) * float(block_cols.shape[0]) ** (-0.5)
    struck = jnp.any(chosen[:, :, None] == ident[None, None, :], axis=1)
    floor_label = 0.1 / total_entities
    labels = jnp.where(struck, 0.9 + floor_label, floor_label)
    residual = (jax.nn.sigmoid(scores) - labels).astype(jnp.bfloat16)
    ent_part = lax.dot_general(query, residual, (((0,), (0,)), ((), ())), preferred_element_type=jnp.float32)
    query_part = lax.dot_general(residual, block_cols, (((1,), (1,)), ((), ())), preferred_element_type=jnp.float32)
    return (ent_part, query_part)

def reference(anchor_ids, relation_ids, head_anchors, head_relations, query_relation, targets, anchor_table, relation_table, enc_weight, fc_weight):
    encoded = encode(anchor_ids, relation_ids, anchor_table, relation_table, enc_weight)
    block = QUERIES // N_ENT

    def step(total, index):
        start = (index * block).astype(jnp.int32)
        h_anc = lax.dynamic_slice_in_dim(head_anchors, start, block, 0)
        h_rel = lax.dynamic_slice_in_dim(head_relations, start, block, 0)
        q_rel = lax.dynamic_slice_in_dim(query_relation, start, block, 0)
        chosen = lax.dynamic_slice_in_dim(targets, start, block, 0)
        query = make_query(h_anc, h_rel, q_rel, anchor_table, relation_table, enc_weight, fc_weight)
        ent_part, query_part = score_terms(query, chosen, encoded, jnp.int32(0), ENTITIES)
        return (total + ent_part, query_part)
    start_total = jnp.zeros((D, ENTITIES), jnp.float32)
    total, query_parts = lax.scan(step, start_total, jnp.arange(N_ENT, dtype=jnp.int32))
    entity_grad = total / math.sqrt(QUERIES)
    query_grad = query_parts.reshape(QUERIES, D) / math.sqrt(ENTITIES)
    return (entity_grad, query_grad)
```

```python
import math

import jax
import jax.numpy as jnp
from jax import lax
from jax.sharding import PartitionSpec as P

AXES = ("ent", "qry")
BF16 = jnp.bfloat16
F32 = jnp.float32


def flat_of(x, y, z, core):
    return z * 32 + (x % 2) * 16 + y * 4 + (x // 2) * 2 + core


def coords_of(flat):
    x = ((flat // 2) % 2) * 2 + (flat // 16) % 2
    return x, (flat // 4) % 4, flat // 32, flat % 2


def moved(block, dx=0, dy=0, dz=0, dcore=0):
    route = []
    for to in range(128):
        x, y, z, core = coords_of(to)
        route.append((flat_of((x + dx) % 4, (y + dy) % 4, (z + dz) % 4, (core + dcore) % 2), to))
    return lax.ppermute(block, AXES, route)


def place():
    ent, qry = lax.axis_index("ent"), lax.axis_index("qry")
    return coords_of(ent * 16 + qry)


def encode(anchor_ids, relation_ids, anchor_table, relation_table, enc_weight):
    rows = jnp.concatenate(
        [
            anchor_table.at[anchor_ids].get(mode="promise_in_bounds"),
            relation_table.at[relation_ids].get(mode="promise_in_bounds"),
        ],
        axis=1,
    )
    flat = rows.reshape(rows.shape[0], -1)
    return lax.dot_general(
        enc_weight, flat, (((0,), (1,)), ((), ())), preferred_element_type=F32
    ).astype(BF16)


def make_query(head_cols, query_relation, relation_table, fc_weight):
    relation_rows = relation_table.at[query_relation].get(mode="promise_in_bounds")
    mixed = (head_cols.astype(F32) * relation_rows.T.astype(F32)).astype(BF16)
    return jnp.tanh(
        lax.dot_general(fc_weight, mixed, (((0,), (0,)), ((), ())), preferred_element_type=F32)
    ).astype(BF16)


def score_terms(query, chosen, slab, ident, total_entities):
    scores = lax.dot_general(
        query, slab, (((0,), (0,)), ((), ())), preferred_element_type=F32
    ) * float(slab.shape[0]) ** (-0.5)
    struck = jnp.zeros(scores.shape, jnp.bool_)
    for k in range(chosen.shape[0]):
        struck = struck | (chosen[k][:, None] == ident[None, :])
    floor_label = 0.1 / total_entities
    labels = jnp.where(struck, 0.9 + floor_label, floor_label)
    residual = (jax.nn.sigmoid(scores) - labels).astype(BF16)
    ent_part = jnp.dot(query, residual, preferred_element_type=F32)
    query_part = lax.dot_general(
        slab, residual, (((1,), (1,)), ((), ())), preferred_element_type=F32
    )
    return (ent_part, query_part)


FAR = (1, 3, 2)


def body(
    anchor_ids,
    relation_ids,
    head_anchors,
    head_relations,
    query_relation,
    targets,
    anchor_table,
    relation_table,
    enc_weight,
    fc_weight,
):
    total = 128
    entities = anchor_ids.shape[0] * total
    queries = head_anchors.shape[0] * total
    x, y, z, core = place()
    wanted = targets.T
    wanted = jnp.concatenate([wanted, moved(wanted, dcore=1)], axis=1)
    wanted = [wanted] + [moved(wanted, dz=d) for d in FAR]
    own_cols = encode(anchor_ids, relation_ids, anchor_table, relation_table, enc_weight)
    width = own_cols.shape[1]
    row = jnp.concatenate([own_cols] + [moved(own_cols, dx=d) for d in FAR], axis=1)
    slab = jnp.concatenate([row] + [moved(row, dy=d) for d in FAR], axis=1)
    within = jnp.arange(width, dtype=jnp.int32)
    ident = jnp.concatenate(
        [
            flat_of((x + dx) % 4, (y + dy) % 4, z, core) * width + within
            for dy in (0,) + FAR
            for dx in (0,) + FAR
        ]
    )
    head_cols = encode(head_anchors, head_relations, anchor_table, relation_table, enc_weight)
    query = make_query(head_cols, query_relation, relation_table, fc_weight)
    far = [moved(query, dz=d) for d in FAR]
    pairs = [jnp.concatenate([q, moved(q, dcore=1)], axis=1) for q in [query] + far]
    count = query.shape[1]
    ent_total = jnp.zeros(slab.shape, F32)
    kept = []
    for k in (1, 2, 3, 0):
        ent_part, query_part = score_terms(pairs[k], wanted[k], slab, ident, entities)
        ent_total = ent_total + ent_part
        away = query_part[:, count:].astype(BF16)
        mine = query_part[:, :count] + moved(away, dcore=1).astype(F32)
        if k:
            mine = moved(mine.astype(BF16), dz=-FAR[k - 1]).astype(F32)
        kept.append(mine)
    query_total = kept[3] + kept[0] + kept[1] + kept[2]
    w4 = 4 * width
    ent_row = ent_total[:, :w4]
    for k, d in enumerate(FAR):
        block = ent_total[:, (k + 1) * w4 : (k + 2) * w4].astype(BF16)
        ent_row = ent_row + moved(block, dy=-d).astype(F32)
    ent_share = ent_row[:, :width]
    for k, d in enumerate(FAR):
        block = ent_row[:, (k + 1) * width : (k + 2) * width].astype(BF16)
        ent_share = ent_share + moved(block, dx=-d).astype(F32)
    return (ent_share / math.sqrt(queries), query_total.T / math.sqrt(entities))


def solution(mesh):
    spread = P(AXES, None)
    placed = (spread, spread, spread, spread, P(AXES), spread, P(), P(), P(), P())
    return jax.shard_map(
        body,
        mesh=mesh,
        in_specs=placed,
        out_specs=(P(None, AXES), spread),
        check_vma=False,
    )
```

```python
import math

import jax
import jax.numpy as jnp
from jax import lax
from jax.experimental import pallas as pl
from jax.experimental.pallas import tpu as pltpu
from jax.sharding import PartitionSpec as P

AXES = ("ent", "qry")
BF16 = jnp.bfloat16
F32 = jnp.float32


def flat_of(x, y, z, core):
    return z * 32 + (x % 2) * 16 + y * 4 + (x // 2) * 2 + core


def coords_of(flat):
    x = ((flat // 2) % 2) * 2 + (flat // 16) % 2
    return x, (flat // 4) % 4, flat // 32, flat % 2


def moved(block, dx=0, dy=0, dz=0, dcore=0):
    route = []
    for to in range(128):
        x, y, z, core = coords_of(to)
        route.append((flat_of((x + dx) % 4, (y + dy) % 4, (z + dz) % 4, (core + dcore) % 2), to))
    return lax.ppermute(block, AXES, route)


def place():
    ent, qry = lax.axis_index("ent"), lax.axis_index("qry")
    return coords_of(ent * 16 + qry)


LANES = 128
CHUNK = 2048
UNROLL = 32


def gather_rows(ids, table, rows, count):
    def some(step, carry):
        first = step * UNROLL
        picked = [table[pl.ds(ids[first + k], 2), :] for k in range(UNROLL)]
        for k in range(UNROLL):
            rows[pl.ds(pl.multiple_of(first * 2, 2 * UNROLL) + 2 * k, 2), :] = picked[k]
        return carry

    lax.fori_loop(0, count // UNROLL, some, 0)


def encoded(anchors, rel_ids, weights, rel_table, rows, width):
    n_rel = rel_ids.shape[0]
    total = jnp.zeros((weights.shape[0], width), F32)
    for t in range(anchors):
        halves = [rows[pl.ds(t * 2 * width + h, width, stride=2), :] for h in range(2)]
        part = jnp.concatenate(halves, axis=1).astype(BF16)
        total = total + lax.dot_general(
            weights[:, t * 256 : (t + 1) * 256], part, (((1,), (1,)), ((), ())),
            preferred_element_type=F32,
        )
    for t in range(n_rel):
        part = relation_rows(rel_ids[t : t + 1, :], rel_table).astype(BF16)
        first = (anchors + t) * 256
        total = total + jnp.dot(weights[:, first : first + 256], part, preferred_element_type=F32)
    return total.astype(BF16)


def relation_rows(ids, rel_table):
    shape = (rel_table.shape[1], ids.shape[1])
    hot = lax.broadcasted_iota(jnp.int32, shape, 0) == jnp.broadcast_to(ids, shape)
    hot = jnp.where(hot, 1.0, 0.0).astype(BF16)
    return jnp.dot(rel_table[...], hot, preferred_element_type=F32)


def encode_kernel(
    own_ids, head_ids, tab_t, w_t, rel_table, own_rel, head_rel, asked, fc_t,
    own_out, query_out, table, rows, weights,
):
    step = pl.program_id(0)
    depth = tab_t.shape[0]
    tokens = weights.shape[1] // 256

    @pl.when(step == 0)
    def _():
        lane = lax.broadcasted_iota(jnp.int32, (depth, 256), 1)
        for t in range(tokens):
            start = t * depth
            base = start // LANES * LANES
            piece = w_t[:, base : base + 384].astype(F32)
            if start > base:
                piece = pltpu.roll(piece, 384 - (start - base), 1)
            weights[:, t * 256 : (t + 1) * 256] = jnp.where(
                lane < depth, piece[:, :256], 0.0
            ).astype(BF16)

    top = tab_t[:LANES, :].astype(F32).T
    rest = jnp.concatenate(
        [tab_t[LANES:, :].astype(F32), jnp.zeros((2 * LANES - depth, CHUNK), F32)], axis=0
    ).T
    table[pl.ds(step * 2 * CHUNK, CHUNK, stride=2), :] = top
    table[pl.ds(step * 2 * CHUNK + 1, CHUNK, stride=2), :] = rest

    @pl.when(step == pl.num_programs(0) - 1)
    def _():
        anchors = tokens - own_rel.shape[0]
        gather_rows(own_ids, table, rows, own_ids.shape[0])
        own_out[...] = encoded(anchors, own_rel, weights, rel_table, rows, own_rel.shape[1])
        gather_rows(head_ids, table, rows, head_ids.shape[0])
        head = encoded(anchors, head_rel, weights, rel_table, rows, head_rel.shape[1])
        mixed = head.astype(F32) * relation_rows(asked[...], rel_table)[:depth, :]
        query_out[...] = jnp.tanh(
            jnp.dot(fc_t[...], mixed.astype(BF16), preferred_element_type=F32)
        ).astype(BF16)


def encode_all(anchor_ids, relation_ids, head_anchors, head_relations, query_relation,
               anchor_table, relation_table, enc_weight, fc_weight):
    own, anchors = anchor_ids.shape
    heads = head_anchors.shape[0]
    depth = anchor_table.shape[1]
    steps = pl.cdiv(anchor_table.shape[0], CHUNK)
    tokens = anchors + relation_ids.shape[1]
    rels = pl.cdiv(relation_table.shape[0], LANES) * LANES
    rel_table = jnp.pad(
        relation_table.T, ((0, 256 - depth), (0, rels - relation_table.shape[0]))
    )
    w_lanes = pl.cdiv(tokens * depth + 256, LANES) * LANES
    whole = pl.BlockSpec(memory_space=pltpu.VMEM)
    smem = pl.BlockSpec(memory_space=pltpu.SMEM)
    return pl.pallas_call(
        encode_kernel,
        grid=(steps,),
        in_specs=[
            smem, smem,
            pl.BlockSpec((depth, CHUNK), lambda i: (0, i)),
            whole, whole, whole, whole, whole, whole,
        ],
        out_specs=[whole, whole],
        out_shape=[
            jax.ShapeDtypeStruct((depth, own), BF16),
            jax.ShapeDtypeStruct((depth, heads), BF16),
        ],
        scratch_shapes=[
            pltpu.VMEM((2 * steps * CHUNK, LANES), F32),
            pltpu.VMEM((2 * heads * anchors, LANES), F32),
            pltpu.VMEM((depth, tokens * 256), BF16),
        ],
        compiler_params=pltpu.CompilerParams(vmem_limit_bytes=56 * 1024 * 1024),
    )(
        (anchor_ids.T * 2).reshape(-1), (head_anchors.T * 2).reshape(-1),
        anchor_table.T, jnp.pad(enc_weight.T, ((0, 0), (0, w_lanes - tokens * depth))),
        rel_table, relation_ids.T, head_relations.T, query_relation[None, :], fc_weight.T,
    )


def score_terms(query, chosen, slab, ident, total_entities):
    scores = lax.dot_general(
        query, slab, (((0,), (0,)), ((), ())), preferred_element_type=F32
    ) * float(slab.shape[0]) ** (-0.5)
    struck = jnp.zeros(scores.shape, jnp.bool_)
    for k in range(chosen.shape[0]):
        struck = struck | (chosen[k][:, None] == ident[None, :])
    floor_label = 0.1 / total_entities
    labels = jnp.where(struck, 0.9 + floor_label, floor_label)
    residual = (jax.nn.sigmoid(scores) - labels).astype(BF16)
    ent_part = jnp.dot(query, residual, preferred_element_type=F32)
    query_part = lax.dot_general(
        slab, residual, (((1,), (1,)), ((), ())), preferred_element_type=F32
    )
    return (ent_part, query_part)


FAR = (1, 3, 2)


def body(
    anchor_ids,
    relation_ids,
    head_anchors,
    head_relations,
    query_relation,
    targets,
    anchor_table,
    relation_table,
    enc_weight,
    fc_weight,
):
    total = 128
    entities = anchor_ids.shape[0] * total
    queries = head_anchors.shape[0] * total
    x, y, z, core = place()
    wanted = targets.T
    wanted = jnp.concatenate([wanted, moved(wanted, dcore=1)], axis=1)
    wanted = [wanted] + [moved(wanted, dz=d) for d in FAR]
    own_cols, query = encode_all(
        anchor_ids,
        relation_ids,
        head_anchors,
        head_relations,
        query_relation,
        anchor_table,
        relation_table,
        enc_weight,
        fc_weight,
    )
    width = own_cols.shape[1]
    row = jnp.concatenate([own_cols] + [moved(own_cols, dx=d) for d in FAR], axis=1)
    slab = jnp.concatenate([row] + [moved(row, dy=d) for d in FAR], axis=1)
    within = jnp.arange(width, dtype=jnp.int32)
    ident = jnp.concatenate(
        [
            flat_of((x + dx) % 4, (y + dy) % 4, z, core) * width + within
            for dy in (0,) + FAR
            for dx in (0,) + FAR
        ]
    )
    far = [moved(query, dz=d) for d in FAR]
    pairs = [jnp.concatenate([q, moved(q, dcore=1)], axis=1) for q in [query] + far]
    count = query.shape[1]
    ent_total = jnp.zeros(slab.shape, F32)
    kept = []
    for k in (1, 2, 3, 0):
        ent_part, query_part = score_terms(pairs[k], wanted[k], slab, ident, entities)
        ent_total = ent_total + ent_part
        away = query_part[:, count:].astype(BF16)
        mine = query_part[:, :count] + moved(away, dcore=1).astype(F32)
        if k:
            mine = moved(mine.astype(BF16), dz=-FAR[k - 1]).astype(F32)
        kept.append(mine)
    query_total = kept[3] + kept[0] + kept[1] + kept[2]
    w4 = 4 * width
    ent_row = ent_total[:, :w4]
    for k, d in enumerate(FAR):
        block = ent_total[:, (k + 1) * w4 : (k + 2) * w4].astype(BF16)
        ent_row = ent_row + moved(block, dy=-d).astype(F32)
    ent_share = ent_row[:, :width]
    for k, d in enumerate(FAR):
        block = ent_row[:, (k + 1) * width : (k + 2) * width].astype(BF16)
        ent_share = ent_share + moved(block, dx=-d).astype(F32)
    return (ent_share / math.sqrt(queries), query_total.T / math.sqrt(entities))


def solution(mesh):
    spread = P(AXES, None)
    placed = (spread, spread, spread, spread, P(AXES), spread, P(), P(), P(), P())
    return jax.shard_map(
        body,
        mesh=mesh,
        in_specs=placed,
        out_specs=(P(None, AXES), spread),
        check_vma=False,
    )
```

```python
import functools
import math

import jax
import jax.numpy as jnp
from jax import lax
from jax.experimental import pallas as pl
from jax.experimental.pallas import tpu as pltpu
from jax.sharding import PartitionSpec as P

AXES = ("ent", "qry")
BF16 = jnp.bfloat16
F32 = jnp.float32
LANES = 128
WIDE = 256
CHUNK = 4096
UNROLL = 64
SPAN = 512
VMEM_BYTES = 58 * 1024 * 1024
FAR = (1, 3, 2)


def flat_of(x, y, z, core):
    return z * 32 + (x % 2) * 16 + y * 4 + (x // 2) * 2 + core


def coords_of(flat):
    x = ((flat // 2) % 2) * 2 + (flat // 16) % 2
    return x, (flat // 4) % 4, flat // 32, flat % 2


def moved(block, dx=0, dy=0, dz=0, dcore=0):
    route = []
    for to in range(128):
        x, y, z, core = coords_of(to)
        route.append((flat_of((x + dx) % 4, (y + dy) % 4, (z + dz) % 4, (core + dcore) % 2), to))
    return lax.ppermute(block, AXES, route)


def place():
    return coords_of(lax.axis_index("ent") * 16 + lax.axis_index("qry"))


def gather_rows(ids, table, rows):
    def some(step, carry):
        first = step * UNROLL
        place = pl.multiple_of(step * (2 * UNROLL), 2 * UNROLL)
        picked = [table[pl.ds(ids[first + k], 2), :] for k in range(UNROLL)]
        for k in range(UNROLL):
            rows[pl.ds(place + 2 * k, 2), :] = picked[k]
        return carry

    lax.fori_loop(0, ids.shape[0] // UNROLL, some, 0)


def relation_rows(ids, rel_table):
    shape = (rel_table.shape[1], ids.shape[1])
    hot = lax.broadcasted_iota(jnp.int32, shape, 0) == jnp.broadcast_to(ids, shape)
    hot = jnp.where(hot, 1.0, 0.0).astype(BF16)
    return jnp.dot(rel_table[...], hot, preferred_element_type=F32)


def encoded(rows, rel_ids, weights, rel_table):
    n_rel, width = rel_ids.shape
    anchors = weights.shape[1] // WIDE - n_rel
    total = jnp.zeros((weights.shape[0], width), F32)
    for t in range(anchors):
        halves = [rows[pl.ds(t * 2 * width + h, width, stride=2), :] for h in range(2)]
        part = jnp.concatenate(halves, axis=1).astype(BF16)
        total = total + lax.dot_general(
            weights[:, t * WIDE : (t + 1) * WIDE],
            part,
            (((1,), (1,)), ((), ())),
            preferred_element_type=F32,
        )
    for t in range(n_rel):
        part = relation_rows(rel_ids[t : t + 1, :], rel_table).astype(BF16)
        first = (anchors + t) * WIDE
        total = total + jnp.dot(weights[:, first : first + WIDE], part, preferred_element_type=F32)
    return total


def prepare(tab_t, w_t, rel_t, table, weights, rel_table, relations):
    step = pl.program_id(0)
    depth = tab_t.shape[0]

    @pl.when(step == 0)
    def _():
        lane = lax.broadcasted_iota(jnp.int32, (depth, WIDE), 1)
        for t in range(weights.shape[1] // WIDE):
            start = t * depth
            base = start // LANES * LANES
            piece = w_t[:, base : base + 3 * LANES].astype(F32)
            if start > base:
                piece = pltpu.roll(piece, 3 * LANES - (start - base), 1)
            weights[:, t * WIDE : (t + 1) * WIDE] = jnp.where(
                lane < depth, piece[:, :WIDE], 0.0
            ).astype(BF16)
        known = lax.broadcasted_iota(jnp.int32, rel_t.shape, 1) < relations
        rel = jnp.where(known, rel_t[...].astype(F32), 0.0)
        rel_table[...] = jnp.concatenate(
            [rel, jnp.zeros((WIDE - depth, rel.shape[1]), F32)], axis=0
        ).astype(BF16)

    chunk = tab_t.shape[1]
    top = tab_t[:LANES, :].astype(F32).T
    rest = jnp.concatenate(
        [tab_t[LANES:, :].astype(F32), jnp.zeros((WIDE - depth, chunk), F32)], axis=0
    ).T
    table[pl.ds(step * 2 * chunk, chunk, stride=2), :] = top
    table[pl.ds(step * 2 * chunk + 1, chunk, stride=2), :] = rest


def encode_kernel(
    relations, scale, own_ids, head_ids, tab_t, w_t, rel_t, own_rel, head_rel, asked, wanted, fc,
    own_out, query_out, table, rows, weights, rel_table,
):
    prepare(tab_t, w_t, rel_t, table, weights, rel_table, relations)

    @pl.when(pl.program_id(0) == pl.num_programs(0) - 1)
    def _():
        gather_rows(own_ids, table, rows)
        own_out[...] = (encoded(rows, own_rel, weights, rel_table) * scale).astype(BF16)
        gather_rows(head_ids, table, rows)
        head = encoded(rows, head_rel, weights, rel_table).astype(BF16)
        mixed = head.astype(F32) * relation_rows(asked[...], rel_table)[: head.shape[0], :]
        query = jnp.tanh(
            lax.dot_general(
                fc[...], mixed.astype(BF16), (((0,), (0,)), ((), ())), preferred_element_type=F32
            )
        )
        digits = []
        for t in range(wanted.shape[0]):
            target = wanted[t : t + 1, :]
            digits += [target // LANES, target % LANES]
        query_out[...] = jnp.concatenate(
            [query, jnp.concatenate(digits, axis=0).astype(F32)], axis=0
        ).astype(BF16)


def encode_all(
    anchor_ids, relation_ids, head_anchors, head_relations, query_relation,
    targets, anchor_table, relation_table, enc_weight, fc_weight, scale,
):
    own, anchors = anchor_ids.shape
    heads = head_anchors.shape[0]
    count, depth = anchor_table.shape
    relations = relation_table.shape[0]
    steps = pl.cdiv(count, CHUNK)
    tokens = anchors + relation_ids.shape[1]
    rel_lanes = pl.cdiv(relations, LANES) * LANES
    w_lanes = pl.cdiv((tokens - 1) * depth // LANES * LANES + 3 * LANES, LANES) * LANES
    whole = pl.BlockSpec(memory_space=pltpu.VMEM)
    smem = pl.BlockSpec(memory_space=pltpu.SMEM)
    once = pl.Buffered(1)
    return pl.pallas_call(
        functools.partial(encode_kernel, relations, scale),
        grid=(steps,),
        in_specs=[
            smem,
            smem,
            pl.BlockSpec((depth, CHUNK), lambda i: (0, i)),
            pl.BlockSpec((depth, w_lanes), lambda i: (0, 0), pipeline_mode=once),
            pl.BlockSpec((depth, rel_lanes), lambda i: (0, 0), pipeline_mode=once),
            whole, whole, whole, whole, whole,
        ],
        out_specs=[whole, whole],
        out_shape=[
            jax.ShapeDtypeStruct((depth, own), BF16),
            jax.ShapeDtypeStruct((depth + 2 * targets.shape[1], heads), BF16),
        ],
        scratch_shapes=[
            pltpu.VMEM((2 * steps * CHUNK, LANES), F32),
            pltpu.VMEM((2 * heads * anchors, LANES), F32),
            pltpu.VMEM((depth, tokens * WIDE), BF16),
            pltpu.VMEM((WIDE, rel_lanes), BF16),
        ],
        compiler_params=pltpu.CompilerParams(vmem_limit_bytes=VMEM_BYTES),
    )(
        (anchor_ids.T * 2).reshape(-1), (head_anchors.T * 2).reshape(-1), anchor_table.T, enc_weight.T, relation_table.T,
        relation_ids.T, head_relations.T, query_relation[None, :], targets.T, fc_weight,
    )


def score_kernel(plain, struck_value, depth, count, started, last, *refs):
    spots, rows = refs[0], refs[1:5]
    blocks = refs[5 : 5 + count]
    refs = refs[5 + count :]
    if started:
        before, refs = refs[0], refs[1:]
    mine, away, refs = refs[: count // 2], refs[count // 2], refs[count // 2 + 1 :]
    if last:
        kept, sent, refs = refs[0], refs[1:4], refs[4:]
        totals, *refs = refs
    else:
        totals, *refs = refs
    slab, tall, queries, marks, asked, *held = refs
    width = blocks[0].shape[1]
    entities = slab.shape[1]
    tiles = SPAN // LANES

    row = entities // 4
    for k in range(4):
        at = slice(k * row, (k + 1) * row)
        slab[:, at] = rows[k][...]
        wide = jnp.concatenate(
            [rows[k][...].astype(F32), jnp.zeros((WIDE - depth, row), F32)], axis=0
        )
        tall[at, :] = wide.T.astype(BF16)
    within = lax.broadcasted_iota(jnp.int32, (LANES, width), 0)
    for b in range(count):
        query = blocks[b][...].astype(F32)
        queries[b] = jnp.concatenate(
            [query[:depth, :], jnp.zeros((WIDE - depth, width), F32)], axis=0
        ).astype(BF16)
        digits = query[depth:, :].astype(jnp.int32)
        marked = jnp.zeros((LANES, width), jnp.int32)
        for t in range(4):
            owner = digits[2 * t : 2 * t + 1, :]
            low = digits[2 * t + 1 : 2 * t + 2, :]
            bit = jnp.zeros(owner.shape, jnp.int32)
            for k in range(entities // LANES):
                bit = jnp.where(owner == spots[k], 1 << k, bit)
            marked = marked | jnp.where(within == low, bit, 0)
        marks[b] = marked

    per = entities // SPAN

    def residual_of(b, part):
        first = part * SPAN
        score = jnp.dot(tall[first : first + SPAN, :], queries[b], preferred_element_type=F32)
        marked = marks[b]
        for j in range(tiles):
            hit = (marked & (1 << (part * tiles + j))) != 0
            label = jnp.where(hit, struck_value, plain)
            held[part % 2][j * LANES : (j + 1) * LANES, :] = (
                jnp.tanh(score[j * LANES : (j + 1) * LANES, :]) + label
            ).astype(BF16)

    def use(b, part, fresh):
        first = part * SPAN
        residual = held[part % 2][...]
        ent = lax.dot_general(
            residual, queries[b], (((1,), (1,)), ((), ())), preferred_element_type=F32
        )
        at = slice(first, first + SPAN)
        if not fresh:
            totals[at, :] += ent
        elif started:
            totals[at, :] = before[at, :] + ent
        else:
            totals[at, :] = ent
        return jnp.dot(slab[:, at], residual, preferred_element_type=F32)

    residual_of(0, 0)
    for b in range(count):
        for part in range(per):
            following = b * per + part + 1
            if following < count * per:
                residual_of(following // per, following % per)
            ask = use(b, part, b == 0)
            if part == 0:
                asked[...] = ask
            elif part < per - 1:
                asked[...] += ask
            else:
                if b % 2:
                    away[:, b // 2 * width : (b // 2 + 1) * width] = (asked[...] + ask).astype(BF16)
                else:
                    mine[b // 2][...] = asked[...] + ask
    if last:
        kept[...] = totals[:row, :].T[:depth, :]
        for k in range(3):
            sent[k][...] = totals[(k + 1) * row : (k + 2) * row, :].T[:depth, :].astype(BF16)


def score(spots, rows, blocks, total_entities, before=None, last=False):
    depth, row = rows[0].shape
    entities = 4 * row
    count, width = len(blocks), blocks[0].shape[1]
    plain = 1.0 - 2.0 * (0.1 / total_entities)
    shape = jax.ShapeDtypeStruct
    outs = [shape((depth, width), F32)] * (count // 2)
    outs.append(shape((depth, width * (count // 2)), BF16))
    scratch = [
        pltpu.VMEM((depth, entities), BF16),
        pltpu.VMEM((entities, WIDE), BF16),
        pltpu.VMEM((count, WIDE, width), BF16),
        pltpu.VMEM((count, LANES, width), jnp.int32),
        pltpu.VMEM((depth, width), F32),
        pltpu.VMEM((SPAN, width), BF16),
        pltpu.VMEM((SPAN, width), BF16),
    ]
    if last:
        outs += [shape((depth, row), F32)] + [shape((depth, row), BF16)] * 3
        scratch.insert(0, pltpu.VMEM((entities, WIDE), F32))
    else:
        outs.append(shape((entities, WIDE), F32))
    whole = pl.BlockSpec(memory_space=pltpu.VMEM)
    extra = [] if before is None else [before]
    return pl.pallas_call(
        functools.partial(
            score_kernel, plain, plain - 1.8, depth, count, before is not None, last
        ),
        in_specs=[pl.BlockSpec(memory_space=pltpu.SMEM)] + [whole] * (4 + count + len(extra)),
        out_specs=[whole] * len(outs),
        out_shape=outs,
        scratch_shapes=scratch,
        compiler_params=pltpu.CompilerParams(vmem_limit_bytes=VMEM_BYTES),
    )(spots, *rows, *blocks, *extra)


def body(
    anchor_ids,
    relation_ids,
    head_anchors,
    head_relations,
    query_relation,
    targets,
    anchor_table,
    relation_table,
    enc_weight,
    fc_weight,
):
    width = anchor_ids.shape[0]
    entities = width * 128
    queries = head_anchors.shape[0] * 128
    scale = 0.5 * float(anchor_table.shape[1]) ** (-0.5)
    x, y, z, core = place()
    own_cols, query = encode_all(
        anchor_ids,
        relation_ids,
        head_anchors,
        head_relations,
        query_relation,
        targets,
        anchor_table,
        relation_table,
        enc_weight,
        fc_weight,
        scale,
    )
    spots = jnp.stack(
        [
            flat_of((x + dx) % 4, (y + dy) % 4, z, core)
            for dy in (0,) + FAR
            for dx in (0,) + FAR
        ]
    ).astype(jnp.int32)
    row = jnp.concatenate([own_cols] + [moved(own_cols, dx=d) for d in FAR], axis=1)
    far = [moved(query, dz=d) for d in FAR]
    rows = [row] + [moved(row, dy=d) for d in FAR]
    pairs = [[q, moved(q, dcore=1)] for q in [query] + far]
    mine0, away0, totals = score(spots, rows, pairs[0], entities)
    kept = [mine0 + moved(away0, dcore=1).astype(F32)]
    mine1, mine2, away12, totals = score(spots, rows, pairs[1] + pairs[2], entities, totals)
    back12 = moved(away12, dcore=1).astype(F32)
    mine3, away3, ent_row, *ent_sent = score(spots, rows, pairs[3], entities, totals, True)
    count = mine1.shape[1]
    ready = [
        mine1 + back12[:, :count],
        mine2 + back12[:, count:],
        mine3 + moved(away3, dcore=1).astype(F32),
    ]
    for d, block in zip(FAR, ent_sent):
        ent_row = ent_row + moved(block, dy=-d).astype(F32)
    kept += [moved(q.astype(BF16), dz=-d).astype(F32) for d, q in zip(FAR, ready)]
    ent_share = ent_row[:, :width]
    for k, d in enumerate(FAR):
        block = ent_row[:, (k + 1) * width : (k + 2) * width].astype(BF16)
        ent_share = ent_share + moved(block, dx=-d).astype(F32)
    query_total = kept[0] + kept[1] + kept[2] + kept[3]
    return (
        ent_share * (0.5 / math.sqrt(queries)),
        query_total.T * (0.5 / scale / math.sqrt(entities)),
    )


def solution(mesh):
    spread = P(AXES, None)
    placed = (spread, spread, spread, spread, P(AXES), spread, P(), P(), P(), P())
    return jax.shard_map(
        body,
        mesh=mesh,
        in_specs=placed,
        out_specs=(P(None, AXES), spread),
        check_vma=False,
    )
```

```python
import functools
import math

import jax
import jax.numpy as jnp
from jax import lax
from jax.experimental import pallas as pl
from jax.experimental.pallas import tpu as pltpu
from jax.sharding import PartitionSpec as P

AXES = ("ent", "qry")
BF16 = jnp.bfloat16
F32 = jnp.float32
LANES = 128
WIDE = 256
CHUNK = 4096
UNROLL = 64
SPAN = 512
VMEM_BYTES = 8 * 1024 * 1024
SCORE_BYTES = 40 * 1024 * 1024
CHUNKS = 2
FAR = (1, 3, 2)


def flat_of(x, y, z, core):
    return z * 32 + (x % 2) * 16 + y * 4 + (x // 2) * 2 + core


def coords_of(flat):
    x = ((flat // 2) % 2) * 2 + (flat // 16) % 2
    return x, (flat // 4) % 4, flat // 32, flat % 2


def moved(block, dx=0, dy=0, dz=0, dcore=0):
    route = []
    for to in range(128):
        x, y, z, core = coords_of(to)
        route.append((flat_of((x + dx) % 4, (y + dy) % 4, (z + dz) % 4, (core + dcore) % 2), to))
    return lax.ppermute(block, AXES, route)


def gather_rows(ids, table, rows, width, count, start, total):
    per = width // UNROLL

    def some(step, carry):
        first = step // per * count + start + step % per * UNROLL
        place = pl.multiple_of(step * (2 * UNROLL), 2 * UNROLL)
        picked = [table[pl.ds(ids[first + k], 2), :] for k in range(UNROLL)]
        for k in range(UNROLL):
            rows[pl.ds(place + 2 * k, 2), :] = picked[k]
        return carry

    lax.fori_loop(0, total // count * per, some, 0)


def relation_rows(ids, rel_table):
    shape = (rel_table.shape[1], ids.shape[1])
    hot = lax.broadcasted_iota(jnp.int32, shape, 0) == jnp.broadcast_to(ids, shape)
    hot = jnp.where(hot, 1.0, 0.0).astype(BF16)
    return jnp.dot(rel_table[...], hot, preferred_element_type=F32)


def encoded(rows, rel_ids, weights, rel_table):
    n_rel, width = rel_ids.shape
    anchors = weights.shape[1] // WIDE - n_rel
    total = jnp.zeros((weights.shape[0], width), F32)
    for t in range(anchors):
        halves = [rows[pl.ds(t * 2 * width + h, width, stride=2), :] for h in range(2)]
        part = jnp.concatenate(halves, axis=1).astype(BF16)
        total = total + lax.dot_general(
            weights[:, t * WIDE : (t + 1) * WIDE],
            part,
            (((1,), (1,)), ((), ())),
            preferred_element_type=F32,
        )
    for t in range(n_rel):
        part = relation_rows(rel_ids[t : t + 1, :], rel_table).astype(BF16)
        first = (anchors + t) * WIDE
        total = total + jnp.dot(weights[:, first : first + WIDE], part, preferred_element_type=F32)
    return total


def prepare(tab_t, w_t, rel_t, table, weights, rel_table, relations):
    step = pl.program_id(0)
    depth = tab_t.shape[0]

    @pl.when(step == 0)
    def _():
        lane = lax.broadcasted_iota(jnp.int32, (depth, WIDE), 1)
        for t in range(weights.shape[1] // WIDE):
            start = t * depth
            base = start // LANES * LANES
            piece = w_t[:, base : base + 3 * LANES].astype(F32)
            if start > base:
                piece = pltpu.roll(piece, 3 * LANES - (start - base), 1)
            weights[:, t * WIDE : (t + 1) * WIDE] = jnp.where(
                lane < depth, piece[:, :WIDE], 0.0
            ).astype(BF16)
        known = lax.broadcasted_iota(jnp.int32, rel_t.shape, 1) < relations
        rel = jnp.where(known, rel_t[...].astype(F32), 0.0)
        rel_table[...] = jnp.concatenate(
            [rel, jnp.zeros((WIDE - depth, rel.shape[1]), F32)], axis=0
        ).astype(BF16)

    chunk = tab_t.shape[1]
    top = tab_t[:LANES, :].astype(F32).T
    rest = jnp.concatenate(
        [tab_t[LANES:, :].astype(F32), jnp.zeros((WIDE - depth, chunk), F32)], axis=0
    ).T
    table[pl.ds(step * 2 * chunk, chunk, stride=2), :] = top
    table[pl.ds(step * 2 * chunk + 1, chunk, stride=2), :] = rest


def entity_kernel(
    relations, scale, own_ids, tab_t, w_t, rel_t, own_rel,
    own_out, table, weights, rel_table, rows,
):
    prepare(tab_t, w_t, rel_t, table, weights, rel_table, relations)

    @pl.when(pl.program_id(0) == pl.num_programs(0) - 1)
    def _():
        width = own_rel.shape[1]
        gather_rows(own_ids, table, rows, width, width, 0, own_ids.shape[0])
        own_out[...] = (encoded(rows, own_rel, weights, rel_table) * scale).astype(BF16)


def head_kernel(
    start, width, head_ids, head_rel, asked, wanted, fc, echo, table, weights, rel_table, *refs
):
    query_out, echo_out, rows = refs[-6], refs[-5], refs[-1]
    if start:
        query_out[:, :start] = refs[0][...]
    echo_out[...] = echo[...]
    part = slice(start, start + width)
    gather_rows(head_ids, table, rows, width, head_rel.shape[1], start, head_ids.shape[0])
    head = encoded(rows, head_rel[:, part], weights, rel_table).astype(BF16)
    mixed = head.astype(F32) * relation_rows(asked[:, part], rel_table)[: head.shape[0], :]
    query = jnp.tanh(
        lax.dot_general(
            fc[...], mixed.astype(BF16), (((0,), (0,)), ((), ())), preferred_element_type=F32
        )
    )
    digits = []
    for t in range(wanted.shape[0]):
        target = wanted[t : t + 1, part]
        digits += [target // LANES, target % LANES]
    query_out[:, query_out.shape[1] - width :] = jnp.concatenate(
        [query, jnp.concatenate(digits, axis=0).astype(F32)], axis=0
    ).astype(BF16)


def encode_entities(anchor_ids, relation_ids, anchor_table, relation_table, enc_weight, scale):
    own, anchors = anchor_ids.shape
    count, depth = anchor_table.shape
    relations = relation_table.shape[0]
    steps = pl.cdiv(count, CHUNK)
    tokens = anchors + relation_ids.shape[1]
    rel_lanes = pl.cdiv(relations, LANES) * LANES
    w_lanes = pl.cdiv((tokens - 1) * depth // LANES * LANES + 3 * LANES, LANES) * LANES
    whole = pl.BlockSpec(memory_space=pltpu.VMEM)
    once = pl.Buffered(1)
    return pl.pallas_call(
        functools.partial(entity_kernel, relations, scale),
        grid=(steps,),
        in_specs=[
            pl.BlockSpec(memory_space=pltpu.SMEM),
            pl.BlockSpec((depth, CHUNK), lambda i: (0, i)),
            pl.BlockSpec((depth, w_lanes), lambda i: (0, 0), pipeline_mode=once),
            pl.BlockSpec((depth, rel_lanes), lambda i: (0, 0), pipeline_mode=once),
            whole,
        ],
        out_specs=[whole] * 4,
        out_shape=[
            jax.ShapeDtypeStruct((depth, own), BF16),
            pltpu.VMEM((2 * steps * CHUNK, LANES), F32),
            pltpu.VMEM((depth, tokens * WIDE), BF16),
            pltpu.VMEM((WIDE, rel_lanes), BF16),
        ],
        scratch_shapes=[pltpu.VMEM((2 * own * anchors, LANES), F32)],
        compiler_params=pltpu.CompilerParams(vmem_limit_bytes=VMEM_BYTES),
    )(
        (anchor_ids.T * 2).reshape(-1), anchor_table.T, enc_weight.T, relation_table.T,
        relation_ids.T,
    )


def encode_heads(
    chunk, head_ids, head_relations, query_relation, targets, fc_weight, echo,
    table, weights, rel_table, earlier,
):
    heads = head_relations.shape[1] // CHUNKS
    depth = fc_weight.shape[0]
    anchors = weights.shape[1] // WIDE - head_relations.shape[0]
    whole = pl.BlockSpec(memory_space=pltpu.VMEM)
    return pl.pallas_call(
        functools.partial(head_kernel, chunk * heads, heads),
        in_specs=[pl.BlockSpec(memory_space=pltpu.SMEM)] + [whole] * (8 + len(earlier)),
        out_specs=[whole] * 5,
        out_shape=[
            jax.ShapeDtypeStruct((depth + 2 * targets.shape[0], heads * (chunk + 1)), BF16),
            jax.ShapeDtypeStruct(echo.shape, BF16),
            pltpu.VMEM(table.shape, F32),
            pltpu.VMEM(weights.shape, BF16),
            pltpu.VMEM(rel_table.shape, BF16),
        ],
        input_output_aliases={6: 2, 7: 3, 8: 4},
        scratch_shapes=[pltpu.VMEM((2 * heads * anchors, LANES), F32)],
        compiler_params=pltpu.CompilerParams(vmem_limit_bytes=VMEM_BYTES),
    )(
        head_ids, head_relations, query_relation, targets, fc_weight, echo,
        table, weights, rel_table, *earlier,
    )


def score_kernel(plain, struck_value, depth, parts, stage, me, slab, *refs):
    blocks, refs = refs[:4], refs[4:]
    if stage:
        before, refs = refs[0], refs[1:]
    if stage == 2:
        kept, sent, refs = refs[0], refs[1:4], refs[4:]
    else:
        asks, refs = refs[0], refs[1:]
    ent_outs, refs = refs[: len(parts)] if stage else refs[:1], refs[len(parts) if stage else 1 :]
    tall, queries, marks, totals, *held = refs[:6]
    if stage == 2:
        asks = refs[6]
    width = SPAN
    tiles = SPAN // LANES

    x, y, z, core = coords_of(me[0])
    if not stage:
        core = 1 - core
    spots = [
        flat_of((x + dx) % 4, (y + ((0,) + FAR)[part]) % 4, z, core)
        for part in parts
        for dx in (0,) + FAR
    ]
    for k, part in enumerate(parts):
        wide = jnp.concatenate(
            [
                slab[:, part * SPAN : (part + 1) * SPAN].astype(F32),
                jnp.zeros((WIDE - depth, SPAN), F32),
            ],
            axis=0,
        )
        tall[k * SPAN : (k + 1) * SPAN, :] = wide.T.astype(BF16)
    within = lax.broadcasted_iota(jnp.int32, (LANES, width), 0)
    for b in range(4):
        query = blocks[b][...].astype(F32)
        queries[b] = jnp.concatenate(
            [query[:depth, :], jnp.zeros((WIDE - depth, width), F32)], axis=0
        ).astype(BF16)
        digits = query[depth:, :].astype(jnp.int32)
        marked = jnp.zeros((LANES, width), jnp.int32)
        for t in range(digits.shape[0] // 2):
            owner = digits[2 * t : 2 * t + 1, :]
            low = digits[2 * t + 1 : 2 * t + 2, :]
            bit = jnp.zeros(owner.shape, jnp.int32)
            for k, spot in enumerate(spots):
                bit = jnp.where(owner == spot, 1 << k, bit)
            marked = marked | jnp.where(within == low, bit, 0)
        marks[b] = marked

    def residual_of(step):
        k, b = step // 4, step % 4
        score = jnp.dot(
            tall[k * SPAN : (k + 1) * SPAN, :], queries[b], preferred_element_type=F32
        )
        marked = marks[b]
        for j in range(tiles):
            hit = (marked & (1 << (k * tiles + j))) != 0
            label = jnp.where(hit, struck_value, plain)
            at = slice(j * LANES, (j + 1) * LANES)
            held[step % 2][at, :] = (jnp.tanh(score[at, :]) + label).astype(BF16)

    def use(step):
        k, b = step // 4, step % 4
        first = parts[k] * SPAN
        residual = held[step % 2][...]
        ent = lax.dot_general(
            residual, queries[b], (((1,), (1,)), ((), ())), preferred_element_type=F32
        )
        ask = jnp.dot(slab[:, first : first + SPAN], residual, preferred_element_type=F32)
        if b == 0:
            totals[...] = ent
        elif b < 3:
            totals[...] += ent
        else:
            ent = (totals[...] + ent).T[:depth, :]
            if stage:
                ent_outs[k][...] = ent
            else:
                ent_outs[0][:, k * SPAN : (k + 1) * SPAN] = ent.astype(BF16)
        if k:
            ask = asks[b] + ask
        elif stage:
            ask = before[b] + ask
        if stage == 2 and k == len(parts) - 1:
            if b:
                sent[b - 1][...] = ask.astype(BF16)
            else:
                kept[...] = ask
        else:
            asks[b] = ask

    steps = 4 * len(parts)
    residual_of(0)
    for step in range(steps):
        if step + 1 < steps:
            residual_of(step + 1)
        use(step)


def score(me, slab, blocks, parts, stage, total_entities, before=None):
    depth, entities = slab.shape
    plain = 1.0 - 2.0 * (0.1 / total_entities)
    shape = jax.ShapeDtypeStruct
    total = pltpu.VMEM((4, depth, SPAN), F32)
    outs = [total]
    if stage == 2:
        outs = [shape((depth, SPAN), F32)] + [shape((depth, SPAN), BF16)] * 3
    outs += [shape((depth, SPAN), F32)] * len(parts) if stage else [shape((depth, entities), BF16)]
    scratch = [
        pltpu.VMEM((len(parts) * SPAN, WIDE), BF16),
        pltpu.VMEM((4, WIDE, SPAN), BF16),
        pltpu.VMEM((4, LANES, SPAN), jnp.int32),
        pltpu.VMEM((SPAN, WIDE), F32),
        pltpu.VMEM((SPAN, SPAN), BF16),
        pltpu.VMEM((SPAN, SPAN), BF16),
    ]
    if stage == 2:
        scratch.append(total)
    whole = pl.BlockSpec(memory_space=pltpu.VMEM)
    extra = [before] if stage else []
    return pl.pallas_call(
        functools.partial(score_kernel, plain, plain - 1.8, depth, parts, stage),
        in_specs=[pl.BlockSpec(memory_space=pltpu.SMEM)] + [whole] * (1 + len(blocks) + len(extra)),
        out_specs=[whole] * len(outs),
        out_shape=outs,
        input_output_aliases={2 + len(blocks): 0} if stage == 1 else {},
        scratch_shapes=scratch,
        compiler_params=pltpu.CompilerParams(vmem_limit_bytes=SCORE_BYTES),
    )(me, slab, *blocks, *extra)


def body(
    anchor_ids,
    relation_ids,
    head_anchors,
    head_relations,
    query_relation,
    targets,
    anchor_table,
    relation_table,
    enc_weight,
    fc_weight,
):
    width = anchor_ids.shape[0]
    entities = width * 128
    queries = head_anchors.shape[0] * 128
    scale = 0.5 * float(anchor_table.shape[1]) ** (-0.5)
    me = (lax.axis_index("ent") * 16 + lax.axis_index("qry")).astype(jnp.int32)[None]
    own_cols, *shared = encode_entities(
        anchor_ids, relation_ids, anchor_table, relation_table, enc_weight, scale
    )
    head_ids = (head_anchors.T * 2).reshape(-1)
    query = []
    piece = own_cols
    for chunk in range(CHUNKS):
        axis = ("dx", "dy")[chunk]
        sent = [moved(piece, **{axis: d}) for d in FAR]
        part, piece, *shared = encode_heads(
            chunk,
            head_ids,
            head_relations.T,
            query_relation[None, :],
            targets.T,
            fc_weight,
            piece,
            *shared,
            query,
        )
        query = [part]
        piece = jnp.concatenate([piece] + sent, axis=1)
    slab = piece
    other = moved(slab, dcore=1)
    blocks = query + [moved(part, dz=d) for part in query for d in FAR]
    asks, away = score(me, other, blocks, (0, 1, 2, 3), 0, entities)
    back = moved(away, dcore=1).astype(F32)
    asks, *ents = score(me, slab, blocks, (1, 2, 3), 1, entities, asks)
    span = slab.shape[1] // 4
    ents = [
        moved((ent + back[:, (k + 1) * span : (k + 2) * span]).astype(BF16), dy=-d)
        for k, (d, ent) in enumerate(zip(FAR, ents))
    ]
    query_total, *far, ent_row = score(me, slab, blocks, (0,), 2, entities, asks)
    ent_row = ent_row + back[:, :span]
    for ent in ents:
        ent_row = ent_row + ent.astype(F32)
    for d, part in zip(FAR, far):
        query_total = query_total + moved(part, dz=-d).astype(F32)
    ent_share = ent_row[:, :width]
    for k, d in enumerate(FAR):
        block = ent_row[:, (k + 1) * width : (k + 2) * width].astype(BF16)
        ent_share = ent_share + moved(block, dx=-d).astype(F32)
    return (
        ent_share * (0.5 / math.sqrt(queries)),
        query_total.T * (0.5 / scale / math.sqrt(entities)),
    )


def solution(mesh):
    spread = P(AXES, None)
    placed = (spread, spread, spread, spread, P(AXES), spread, P(), P(), P(), P())
    return jax.shard_map(
        body,
        mesh=mesh,
        in_specs=placed,
        out_specs=(P(None, AXES), spread),
        check_vma=False,
    )
```

```python
import functools
import math

import jax
import jax.numpy as jnp
from jax import lax
from jax.experimental import pallas as pl
from jax.experimental.pallas import tpu as pltpu
from jax.sharding import PartitionSpec as P

AXES = ("ent", "qry")
BF16 = jnp.bfloat16
F32 = jnp.float32
LANES = 128
WIDE = 256
CHUNK = 4096
UNROLL = 64
SPAN = 512
VMEM_BYTES = 12 * 1024 * 1024
CHUNKS = 2
FAR = (1, 3, 2)


def flat_of(x, y, z, core):
    return z * 32 + (x % 2) * 16 + y * 4 + (x // 2) * 2 + core


def coords_of(flat):
    x = ((flat // 2) % 2) * 2 + (flat // 16) % 2
    return x, (flat // 4) % 4, flat // 32, flat % 2


def moved(block, dx=0, dy=0, dz=0, dcore=0):
    route = []
    for to in range(128):
        x, y, z, core = coords_of(to)
        route.append((flat_of((x + dx) % 4, (y + dy) % 4, (z + dz) % 4, (core + dcore) % 2), to))
    return lax.ppermute(block, AXES, route)


def gather_rows(ids, table, rows, width, count, start, anchors):
    per = width // UNROLL

    def some(step, carry):
        first = step // per * count + start + step % per * UNROLL
        place = pl.multiple_of(step * (2 * UNROLL), 2 * UNROLL)
        picked = [table[pl.ds(ids[first + k], 2), :] for k in range(UNROLL)]
        for k in range(UNROLL):
            rows[pl.ds(place + 2 * k, 2), :] = picked[k]
        return carry

    lax.fori_loop(0, anchors * per, some, 0)


def relation_rows(ids, rel_table):
    shape = (rel_table.shape[1], ids.shape[1])
    hot = lax.broadcasted_iota(jnp.int32, shape, 0) == jnp.broadcast_to(ids, shape)
    hot = jnp.where(hot, 1.0, 0.0).astype(BF16)
    return jnp.dot(rel_table[...], hot, preferred_element_type=F32)


def encoded(rows, rel_ids, weights, rel_table):
    n_rel, width = rel_ids.shape
    anchors = weights.shape[1] // WIDE - n_rel
    total = jnp.zeros((weights.shape[0], width), F32)
    for t in range(anchors):
        halves = [rows[pl.ds(t * 2 * width + h, width, stride=2), :] for h in range(2)]
        part = jnp.concatenate(halves, axis=1).astype(BF16)
        total = total + lax.dot_general(
            weights[:, t * WIDE : (t + 1) * WIDE],
            part,
            (((1,), (1,)), ((), ())),
            preferred_element_type=F32,
        )
    for t in range(n_rel):
        part = relation_rows(rel_ids[t : t + 1, :], rel_table).astype(BF16)
        first = (anchors + t) * WIDE
        total = total + jnp.dot(weights[:, first : first + WIDE], part, preferred_element_type=F32)
    return total


def prepare(tab_t, w_t, rel_t, table, weights, rel_table, relations):
    step = pl.program_id(0)
    depth = tab_t.shape[0]

    @pl.when(step == 0)
    def _():
        lane = lax.broadcasted_iota(jnp.int32, (depth, WIDE), 1)
        for t in range(weights.shape[1] // WIDE):
            start = t * depth
            base = start // LANES * LANES
            piece = w_t[:, base : base + 3 * LANES].astype(F32)
            if start > base:
                piece = pltpu.roll(piece, 3 * LANES - (start - base), 1)
            weights[:, t * WIDE : (t + 1) * WIDE] = jnp.where(
                lane < depth, piece[:, :WIDE], 0.0
            ).astype(BF16)
        known = lax.broadcasted_iota(jnp.int32, rel_t.shape, 1) < relations
        rel = jnp.where(known, rel_t[...].astype(F32), 0.0)
        rel_table[...] = jnp.concatenate(
            [rel, jnp.zeros((WIDE - depth, rel.shape[1]), F32)], axis=0
        ).astype(BF16)

    chunk = tab_t.shape[1]
    top = tab_t[:LANES, :].astype(F32).T
    rest = jnp.concatenate(
        [tab_t[LANES:, :].astype(F32), jnp.zeros((WIDE - depth, chunk), F32)], axis=0
    ).T
    table[pl.ds(step * 2 * chunk, chunk, stride=2), :] = top
    table[pl.ds(step * 2 * chunk + 1, chunk, stride=2), :] = rest


def entity_kernel(
    relations, scale, own_ids, tab_t, w_t, rel_t, own_rel,
    own_out, table, weights, rel_table, rows,
):
    prepare(tab_t, w_t, rel_t, table, weights, rel_table, relations)

    @pl.when(pl.program_id(0) == pl.num_programs(0) - 1)
    def _():
        width = own_rel.shape[1]
        anchors = weights.shape[1] // WIDE - own_rel.shape[0]
        gather_rows(own_ids, table, rows, width, width, 0, anchors)
        own_out[...] = (encoded(rows, own_rel, weights, rel_table) * scale).astype(BF16)


def head_kernel(
    start, width, head_ids, head_rel, asked, wanted, fc, echo, table, weights, rel_table, *refs
):
    query_out, echo_out, rows = refs[-6], refs[-5], refs[-1]
    if start:
        query_out[:, :start] = refs[0][...]
    echo_out[...] = echo[...]
    part = slice(start, start + width)
    tokens, heads = head_rel.shape
    anchors = weights.shape[1] // WIDE - tokens
    before = head_ids.shape[0] - anchors * heads
    gather_rows(head_ids, table, rows, width, heads, before + start, anchors)
    head = encoded(rows, head_rel[:, part], weights, rel_table).astype(BF16)
    mixed = head.astype(F32) * relation_rows(asked[:, part], rel_table)[: head.shape[0], :]
    query = jnp.tanh(
        lax.dot_general(
            fc[...], mixed.astype(BF16), (((0,), (0,)), ((), ())), preferred_element_type=F32
        )
    )
    digits = []
    for t in range(wanted.shape[0]):
        target = wanted[t : t + 1, part]
        digits += [target // LANES, target % LANES]
    query_out[:, query_out.shape[1] - width :] = jnp.concatenate(
        [query, jnp.concatenate(digits, axis=0).astype(F32)], axis=0
    ).astype(BF16)


def encode_entities(ids, anchors, relation_ids, anchor_table, relation_table, enc_weight, scale):
    own = relation_ids.shape[0]
    count, depth = anchor_table.shape
    relations = relation_table.shape[0]
    steps = pl.cdiv(count, CHUNK)
    tokens = anchors + relation_ids.shape[1]
    rel_lanes = pl.cdiv(relations, LANES) * LANES
    w_lanes = pl.cdiv((tokens - 1) * depth // LANES * LANES + 3 * LANES, LANES) * LANES
    whole = pl.BlockSpec(memory_space=pltpu.VMEM)
    once = pl.Buffered(1)
    return pl.pallas_call(
        functools.partial(entity_kernel, relations, scale),
        grid=(steps,),
        in_specs=[
            pl.BlockSpec(memory_space=pltpu.SMEM),
            pl.BlockSpec((depth, CHUNK), lambda i: (0, i)),
            pl.BlockSpec((depth, w_lanes), lambda i: (0, 0), pipeline_mode=once),
            pl.BlockSpec((depth, rel_lanes), lambda i: (0, 0), pipeline_mode=once),
            whole,
        ],
        out_specs=[whole] * 4,
        out_shape=[
            jax.ShapeDtypeStruct((depth, own), BF16),
            pltpu.VMEM((2 * steps * CHUNK, LANES), F32),
            pltpu.VMEM((depth, tokens * WIDE), BF16),
            pltpu.VMEM((WIDE, rel_lanes), BF16),
        ],
        scratch_shapes=[pltpu.VMEM((2 * own * anchors, LANES), F32)],
        compiler_params=pltpu.CompilerParams(vmem_limit_bytes=VMEM_BYTES),
    )(
        ids,
        pltpu.with_memory_space_constraint(anchor_table.T, pltpu.HBM), enc_weight.T, relation_table.T,
        relation_ids.T,
    )


def encode_heads(
    chunk, head_ids, head_relations, query_relation, targets, fc_weight, echo,
    table, weights, rel_table, earlier,
):
    heads = head_relations.shape[1] // CHUNKS
    depth = fc_weight.shape[0]
    anchors = weights.shape[1] // WIDE - head_relations.shape[0]
    whole = pl.BlockSpec(memory_space=pltpu.VMEM)
    return pl.pallas_call(
        functools.partial(head_kernel, chunk * heads, heads),
        in_specs=[pl.BlockSpec(memory_space=pltpu.SMEM)] + [whole] * (8 + len(earlier)),
        out_specs=[whole] * 5,
        out_shape=[
            jax.ShapeDtypeStruct((depth + 2 * targets.shape[0], heads * (chunk + 1)), BF16),
            jax.ShapeDtypeStruct(echo.shape, BF16),
            pltpu.VMEM(table.shape, F32),
            pltpu.VMEM(weights.shape, BF16),
            pltpu.VMEM(rel_table.shape, BF16),
        ],
        input_output_aliases={6: 2, 7: 3, 8: 4},
        scratch_shapes=[pltpu.VMEM((2 * heads * anchors, LANES), F32)],
        compiler_params=pltpu.CompilerParams(vmem_limit_bytes=VMEM_BYTES),
    )(
        head_ids, head_relations, query_relation, targets, fc_weight, echo,
        table, weights, rel_table, *earlier,
    )


def score_kernel(plain, struck_value, depth, parts, stage, me, slab, *refs):
    blocks, refs = refs[:4], refs[4:]
    if stage:
        before, refs = refs[0], refs[1:]
    if stage == 2:
        kept, sent, refs = refs[0], refs[1:4], refs[4:]
    else:
        asks, refs = refs[0], refs[1:]
    ent_outs, refs = refs[: len(parts)] if stage else refs[:1], refs[len(parts) if stage else 1 :]
    tall, queries, marks, totals, *held = refs[:6]
    if stage == 2:
        asks = refs[6]
    width = SPAN
    tiles = SPAN // LANES

    x, y, z, core = coords_of(me[0])
    if not stage:
        core = 1 - core
    spots = [
        flat_of((x + dx) % 4, (y + ((0,) + FAR)[part]) % 4, z, core)
        for part in parts
        for dx in (0,) + FAR
    ]
    for k, part in enumerate(parts):
        wide = jnp.concatenate(
            [
                slab[:, part * SPAN : (part + 1) * SPAN].astype(F32),
                jnp.zeros((WIDE - depth, SPAN), F32),
            ],
            axis=0,
        )
        tall[k * SPAN : (k + 1) * SPAN, :] = wide.T.astype(BF16)
    within = lax.broadcasted_iota(jnp.int32, (LANES, width), 0)
    for b in range(4):
        query = blocks[b][...].astype(F32)
        queries[b] = jnp.concatenate(
            [query[:depth, :], jnp.zeros((WIDE - depth, width), F32)], axis=0
        ).astype(BF16)
        digits = query[depth:, :].astype(jnp.int32)
        marked = jnp.zeros((LANES, width), jnp.int32)
        for t in range(digits.shape[0] // 2):
            owner = digits[2 * t : 2 * t + 1, :]
            low = digits[2 * t + 1 : 2 * t + 2, :]
            bit = jnp.zeros(owner.shape, jnp.int32)
            for k, spot in enumerate(spots):
                bit = jnp.where(owner == spot, 1 << k, bit)
            marked = marked | jnp.where(within == low, bit, 0)
        marks[b] = marked

    def residual_of(step):
        k, b = step // 4, step % 4
        score = jnp.dot(
            tall[k * SPAN : (k + 1) * SPAN, :], queries[b], preferred_element_type=F32
        )
        marked = marks[b]
        for j in range(tiles):
            hit = (marked & (1 << (k * tiles + j))) != 0
            label = jnp.where(hit, struck_value, plain)
            at = slice(j * LANES, (j + 1) * LANES)
            held[step % 2][at, :] = (jnp.tanh(score[at, :]) + label).astype(BF16)

    def use(step):
        k, b = step // 4, step % 4
        first = parts[k] * SPAN
        residual = held[step % 2][...]
        ent = lax.dot_general(
            residual, queries[b], (((1,), (1,)), ((), ())), preferred_element_type=F32
        )
        ask = jnp.dot(slab[:, first : first + SPAN], residual, preferred_element_type=F32)
        if b == 0:
            totals[...] = ent
        elif b < 3:
            totals[...] += ent
        else:
            ent = (totals[...] + ent).T[:depth, :]
            if stage:
                ent_outs[k][...] = ent
            else:
                ent_outs[0][:, k * SPAN : (k + 1) * SPAN] = ent.astype(BF16)
        if k:
            ask = asks[b] + ask
        elif stage:
            ask = before[b] + ask
        if stage == 2 and k == len(parts) - 1:
            if b:
                sent[b - 1][...] = ask.astype(BF16)
            else:
                kept[...] = ask
        else:
            asks[b] = ask

    steps = 4 * len(parts)
    residual_of(0)
    for step in range(steps):
        if step + 1 < steps:
            residual_of(step + 1)
        use(step)


def score(me, slab, blocks, parts, stage, total_entities, before=None):
    depth, entities = slab.shape
    plain = 1.0 - 2.0 * (0.1 / total_entities)
    shape = jax.ShapeDtypeStruct
    total = pltpu.VMEM((4, depth, SPAN), F32)
    outs = [total]
    if stage == 2:
        outs = [shape((depth, SPAN), F32)] + [shape((depth, SPAN), BF16)] * 3
    outs += [shape((depth, SPAN), F32)] * len(parts) if stage else [shape((depth, entities), BF16)]
    scratch = [
        pltpu.VMEM((len(parts) * SPAN, WIDE), BF16),
        pltpu.VMEM((4, WIDE, SPAN), BF16),
        pltpu.VMEM((4, LANES, SPAN), jnp.int32),
        pltpu.VMEM((SPAN, WIDE), F32),
        pltpu.VMEM((SPAN, SPAN), BF16),
        pltpu.VMEM((SPAN, SPAN), BF16),
    ]
    if stage == 2:
        scratch.append(total)
    whole = pl.BlockSpec(memory_space=pltpu.VMEM)
    extra = [before] if stage else []
    return pl.pallas_call(
        functools.partial(score_kernel, plain, plain - 1.8, depth, parts, stage),
        in_specs=[pl.BlockSpec(memory_space=pltpu.SMEM)] + [whole] * (1 + len(blocks) + len(extra)),
        out_specs=[whole] * len(outs),
        out_shape=outs,
        input_output_aliases={2 + len(blocks): 0} if stage == 1 else {},
        scratch_shapes=scratch,
        compiler_params=pltpu.CompilerParams(vmem_limit_bytes=VMEM_BYTES),
    )(me, slab, *blocks, *extra)


def body(
    anchor_ids,
    relation_ids,
    head_anchors,
    head_relations,
    query_relation,
    targets,
    anchor_table,
    relation_table,
    enc_weight,
    fc_weight,
):
    width = anchor_ids.shape[0]
    entities = width * 128
    queries = head_anchors.shape[0] * 128
    scale = 0.5 * float(anchor_table.shape[1]) ** (-0.5)
    me = (lax.axis_index("ent") * 16 + lax.axis_index("qry")).astype(jnp.int32)[None]
    ids = jnp.concatenate([anchor_ids.T.reshape(-1), head_anchors.T.reshape(-1)]) * 2
    own_cols, *shared = encode_entities(
        ids,
        anchor_ids.shape[1],
        relation_ids,
        anchor_table,
        relation_table,
        enc_weight,
        scale,
    )
    query = []
    piece = own_cols
    for chunk in range(CHUNKS):
        axis = ("dx", "dy")[chunk]
        sent = [moved(piece, **{axis: d}) for d in FAR]
        part, piece, *shared = encode_heads(
            chunk,
            ids,
            head_relations.T,
            query_relation[None, :],
            targets.T,
            fc_weight,
            piece,
            *shared,
            query,
        )
        query = [part]
        piece = jnp.concatenate([piece] + sent, axis=1)
    slab = piece
    other = moved(slab, dcore=1)
    blocks = query + [moved(part, dz=d) for part in query for d in FAR]
    asks, away = score(me, other, blocks, (0, 1, 2, 3), 0, entities)
    back = moved(away, dcore=1).astype(F32)
    asks, *ents = score(me, slab, blocks, (1, 2, 3), 1, entities, asks)
    span = slab.shape[1] // 4
    ents = [
        moved((ent + back[:, (k + 1) * span : (k + 2) * span]).astype(BF16), dy=-d)
        for k, (d, ent) in enumerate(zip(FAR, ents))
    ]
    query_total, *far, ent_row = score(me, slab, blocks, (0,), 2, entities, asks)
    ent_row = ent_row + back[:, :span]
    for ent in ents:
        ent_row = ent_row + ent.astype(F32)
    for d, part in zip(FAR, far):
        query_total = query_total + moved(part, dz=-d).astype(F32)
    ent_share = ent_row[:, :width]
    for k, d in enumerate(FAR):
        block = ent_row[:, (k + 1) * width : (k + 2) * width].astype(BF16)
        ent_share = ent_share + moved(block, dx=-d).astype(F32)
    return (
        ent_share * (0.5 / math.sqrt(queries)),
        query_total.T * (0.5 / scale / math.sqrt(entities)),
    )


def solution(mesh):
    spread = P(AXES, None)
    placed = (spread, spread, spread, spread, P(AXES), spread, P(), P(), P(), P())
    return jax.shard_map(
        body,
        mesh=mesh,
        in_specs=placed,
        out_specs=(P(None, AXES), spread),
        check_vma=False,
    )
```

```python
import functools
import math

import jax
import jax.numpy as jnp
from jax import lax
from jax.experimental import pallas as pl
from jax.experimental.pallas import tpu as pltpu
from jax.sharding import PartitionSpec as P

AXES = ("ent", "qry")
BF16 = jnp.bfloat16
F32 = jnp.float32
LANES = 128
WIDE = 256
CHUNK = 4096
UNROLL = 64
SPAN = 512
VMEM_BYTES = 12 * 1024 * 1024
CHUNKS = 2
FAR = (1, 3, 2)


def flat_of(x, y, z, core):
    return z * 32 + (x % 2) * 16 + y * 4 + (x // 2) * 2 + core


def coords_of(flat):
    x = ((flat // 2) % 2) * 2 + (flat // 16) % 2
    return x, (flat // 4) % 4, flat // 32, flat % 2


def moved(block, dx=0, dy=0, dz=0, dcore=0):
    route = []
    for to in range(128):
        x, y, z, core = coords_of(to)
        route.append((flat_of((x + dx) % 4, (y + dy) % 4, (z + dz) % 4, (core + dcore) % 2), to))
    return lax.ppermute(block, AXES, route)


def gather_rows(ids, table, rows, width, count, start, anchors):
    per = width // UNROLL

    def some(step, carry):
        first = step // per * count + start + step % per * UNROLL
        place = pl.multiple_of(step * (2 * UNROLL), 2 * UNROLL)
        picked = [table[pl.ds(ids[first + k], 2), :] for k in range(UNROLL)]
        for k in range(UNROLL):
            rows[pl.ds(place + 2 * k, 2), :] = picked[k]
        return carry

    lax.fori_loop(0, anchors * per, some, 0)


def relation_rows(ids, rel_table):
    shape = (rel_table.shape[1], ids.shape[1])
    hot = lax.broadcasted_iota(jnp.int32, shape, 0) == jnp.broadcast_to(ids, shape)
    hot = jnp.where(hot, 1.0, 0.0).astype(BF16)
    return jnp.dot(rel_table[...], hot, preferred_element_type=F32)


def encoded(rows, rel_ids, weights, rel_table):
    n_rel, width = rel_ids.shape
    anchors = weights.shape[1] // WIDE - n_rel
    total = jnp.zeros((weights.shape[0], width), F32)
    for t in range(anchors):
        halves = [rows[pl.ds(t * 2 * width + h, width, stride=2), :] for h in range(2)]
        part = jnp.concatenate(halves, axis=1).astype(BF16)
        total = total + lax.dot_general(
            weights[:, t * WIDE : (t + 1) * WIDE],
            part,
            (((1,), (1,)), ((), ())),
            preferred_element_type=F32,
        )
    for t in range(n_rel):
        part = relation_rows(rel_ids[t : t + 1, :], rel_table).astype(BF16)
        first = (anchors + t) * WIDE
        total = total + jnp.dot(weights[:, first : first + WIDE], part, preferred_element_type=F32)
    return total


def prepare(tab_t, w_t, rel_t, table, weights, rel_table, relations):
    step = pl.program_id(0)
    depth = tab_t.shape[0]

    @pl.when(step == 0)
    def _():
        lane = lax.broadcasted_iota(jnp.int32, (depth, WIDE), 1)
        for t in range(weights.shape[1] // WIDE):
            start = t * depth
            base = start // LANES * LANES
            piece = w_t[:, base : base + 3 * LANES].astype(F32)
            if start > base:
                piece = pltpu.roll(piece, 3 * LANES - (start - base), 1)
            weights[:, t * WIDE : (t + 1) * WIDE] = jnp.where(
                lane < depth, piece[:, :WIDE], 0.0
            ).astype(BF16)
        known = lax.broadcasted_iota(jnp.int32, rel_t.shape, 1) < relations
        rel = jnp.where(known, rel_t[...].astype(F32), 0.0)
        rel_table[...] = jnp.concatenate(
            [rel, jnp.zeros((WIDE - depth, rel.shape[1]), F32)], axis=0
        ).astype(BF16)

    chunk = tab_t.shape[1]
    top = tab_t[:LANES, :].astype(F32).T
    rest = jnp.concatenate(
        [tab_t[LANES:, :].astype(F32), jnp.zeros((WIDE - depth, chunk), F32)], axis=0
    ).T
    table[pl.ds(step * 2 * chunk, chunk, stride=2), :] = top
    table[pl.ds(step * 2 * chunk + 1, chunk, stride=2), :] = rest


def entity_kernel(
    relations, scale, own_ids, tab_t, w_t, rel_t, own_rel,
    own_out, table, weights, rel_table, rows,
):
    prepare(tab_t, w_t, rel_t, table, weights, rel_table, relations)

    @pl.when(pl.program_id(0) == pl.num_programs(0) - 1)
    def _():
        width = own_rel.shape[1]
        anchors = weights.shape[1] // WIDE - own_rel.shape[0]
        gather_rows(own_ids, table, rows, width, width, 0, anchors)
        own_out[...] = (encoded(rows, own_rel, weights, rel_table) * scale).astype(BF16)


def head_kernel(
    start, width, head_ids, head_rel, asked, wanted, fc, echo, table, weights, rel_table, *refs
):
    query_out, echo_out, rows = refs[-6], refs[-5], refs[-1]
    if start:
        query_out[:, :start] = refs[0][...]
    echo_out[...] = echo[...]
    part = slice(start, start + width)
    tokens, heads = head_rel.shape
    anchors = weights.shape[1] // WIDE - tokens
    before = head_ids.shape[0] - anchors * heads
    gather_rows(head_ids, table, rows, width, heads, before + start, anchors)
    head = encoded(rows, head_rel[:, part], weights, rel_table).astype(BF16)
    mixed = head.astype(F32) * relation_rows(asked[:, part], rel_table)[: head.shape[0], :]
    query = jnp.tanh(
        lax.dot_general(
            fc[...], mixed.astype(BF16), (((0,), (0,)), ((), ())), preferred_element_type=F32
        )
    )
    digits = []
    for t in range(wanted.shape[0]):
        target = wanted[t : t + 1, part]
        digits += [target // LANES, target % LANES]
    query_out[:, query_out.shape[1] - width :] = jnp.concatenate(
        [query, jnp.concatenate(digits, axis=0).astype(F32)], axis=0
    ).astype(BF16)


def encode_entities(ids, anchors, relation_ids, anchor_table, relation_table, enc_weight, scale):
    own = relation_ids.shape[0]
    count, depth = anchor_table.shape
    relations = relation_table.shape[0]
    steps = pl.cdiv(count, CHUNK)
    tokens = anchors + relation_ids.shape[1]
    rel_lanes = pl.cdiv(relations, LANES) * LANES
    w_lanes = pl.cdiv((tokens - 1) * depth // LANES * LANES + 3 * LANES, LANES) * LANES
    whole = pl.BlockSpec(memory_space=pltpu.VMEM)
    once = pl.Buffered(1)
    return pl.pallas_call(
        functools.partial(entity_kernel, relations, scale),
        grid=(steps,),
        in_specs=[
            pl.BlockSpec(memory_space=pltpu.SMEM),
            pl.BlockSpec((depth, CHUNK), lambda i: (0, i)),
            pl.BlockSpec((depth, w_lanes), lambda i: (0, 0), pipeline_mode=once),
            pl.BlockSpec((depth, rel_lanes), lambda i: (0, 0), pipeline_mode=once),
            whole,
        ],
        out_specs=[whole] * 4,
        out_shape=[
            jax.ShapeDtypeStruct((depth, own), BF16),
            pltpu.VMEM((2 * steps * CHUNK, LANES), F32),
            pltpu.VMEM((depth, tokens * WIDE), BF16),
            pltpu.VMEM((WIDE, rel_lanes), BF16),
        ],
        scratch_shapes=[pltpu.VMEM((2 * own * anchors, LANES), F32)],
        compiler_params=pltpu.CompilerParams(vmem_limit_bytes=VMEM_BYTES),
    )(
        ids,
        pltpu.with_memory_space_constraint(anchor_table.T, pltpu.HBM), enc_weight.T, relation_table.T,
        relation_ids.T,
    )


def encode_heads(
    chunk, head_ids, head_relations, query_relation, targets, fc_weight, echo,
    table, weights, rel_table, earlier,
):
    heads = head_relations.shape[1] // CHUNKS
    depth = fc_weight.shape[0]
    anchors = weights.shape[1] // WIDE - head_relations.shape[0]
    whole = pl.BlockSpec(memory_space=pltpu.VMEM)
    return pl.pallas_call(
        functools.partial(head_kernel, chunk * heads, heads),
        in_specs=[pl.BlockSpec(memory_space=pltpu.SMEM)] + [whole] * (8 + len(earlier)),
        out_specs=[whole] * 5,
        out_shape=[
            jax.ShapeDtypeStruct((depth + 2 * targets.shape[0], heads * (chunk + 1)), BF16),
            jax.ShapeDtypeStruct(echo.shape, BF16),
            pltpu.VMEM(table.shape, F32),
            pltpu.VMEM(weights.shape, BF16),
            pltpu.VMEM(rel_table.shape, BF16),
        ],
        input_output_aliases={6: 2, 7: 3, 8: 4},
        scratch_shapes=[pltpu.VMEM((2 * heads * anchors, LANES), F32)],
        compiler_params=pltpu.CompilerParams(vmem_limit_bytes=VMEM_BYTES),
    )(
        head_ids, head_relations, query_relation, targets, fc_weight, echo,
        table, weights, rel_table, *earlier,
    )


def leave(out, which, block, base):
    half = SPAN // 2
    places = ((0, half), (base + 4 * half, base + half), (base + 3 * half, base + 5 * half))
    places += ((base, base + 2 * half),)
    for k, at in enumerate(places[which]):
        out[:, at : at + half] = block[:, k * half : (k + 1) * half].astype(out.dtype)


def score_kernel(plain, struck_value, depth, parts, stage, me, slab, *refs):
    blocks, refs = refs[:5], refs[5:]
    if stage:
        before, refs = refs[0], refs[1:]
    if stage == 2:
        kept, sent, refs = refs[0], refs[1], refs[2:]
    else:
        asks, refs = refs[0], refs[1:]
    ents, refs = refs[0], refs[1:]
    tall, queries, marks, totals, *held = refs[:6]
    if stage == 2:
        asks = refs[6]
    width = SPAN
    tiles = SPAN // LANES

    x, y, z, core = coords_of(me[0])
    if not stage:
        core = 1 - core
    spots = [
        flat_of((x + dx) % 4, (y + ((0,) + FAR)[part]) % 4, z, core)
        for part in parts
        for dx in (0,) + FAR
    ]
    for k, part in enumerate(parts):
        wide = jnp.concatenate(
            [
                slab[:, part * SPAN : (part + 1) * SPAN].astype(F32),
                jnp.zeros((WIDE - depth, SPAN), F32),
            ],
            axis=0,
        )
        tall[k * SPAN : (k + 1) * SPAN, :] = wide.T.astype(BF16)
    within = lax.broadcasted_iota(jnp.int32, (LANES, width), 0)
    for b in range(4):
        query = blocks[b][...] if b < 3 else jnp.concatenate([blocks[3][...], blocks[4][...]], axis=1)
        query = query.astype(F32)
        queries[b] = jnp.concatenate(
            [query[:depth, :], jnp.zeros((WIDE - depth, width), F32)], axis=0
        ).astype(BF16)
        digits = query[depth:, :].astype(jnp.int32)
        marked = jnp.zeros((LANES, width), jnp.int32)
        for t in range(digits.shape[0] // 2):
            owner = digits[2 * t : 2 * t + 1, :]
            low = digits[2 * t + 1 : 2 * t + 2, :]
            bit = jnp.zeros(owner.shape, jnp.int32)
            for k, spot in enumerate(spots):
                bit = jnp.where(owner == spot, 1 << k, bit)
            marked = marked | jnp.where(within == low, bit, 0)
        marks[b] = marked

    def residual_of(step):
        k, b = step // 4, step % 4
        score = jnp.dot(
            tall[k * SPAN : (k + 1) * SPAN, :], queries[b], preferred_element_type=F32
        )
        marked = marks[b]
        for j in range(tiles):
            hit = (marked & (1 << (k * tiles + j))) != 0
            label = jnp.where(hit, struck_value, plain)
            at = slice(j * LANES, (j + 1) * LANES)
            held[step % 2][at, :] = (jnp.tanh(score[at, :]) + label).astype(BF16)

    def use(step):
        k, b = step // 4, step % 4
        first = parts[k] * SPAN
        residual = held[step % 2][...]
        ent = lax.dot_general(
            residual, queries[b], (((1,), (1,)), ((), ())), preferred_element_type=F32
        )
        ask = jnp.dot(slab[:, first : first + SPAN], residual, preferred_element_type=F32)
        if b == 0:
            totals[...] = ent
        elif b < 3:
            totals[...] += ent
        else:
            ent = (totals[...] + ent).T[:depth, :]
            leave(ents, parts[k], ent, 0 if stage else SPAN)
        if k:
            ask = asks[b] + ask
        elif stage:
            ask = before[b] + ask
        if stage == 2 and k == len(parts) - 1:
            if b:
                leave(sent, b, ask, 0)
            else:
                kept[...] = ask
        else:
            asks[b] = ask

    steps = 4 * len(parts)
    residual_of(0)
    for step in range(steps):
        if step + 1 < steps:
            residual_of(step + 1)
        use(step)


def score(me, slab, blocks, parts, stage, total_entities, before=None):
    depth, entities = slab.shape
    plain = 1.0 - 2.0 * (0.1 / total_entities)
    shape = jax.ShapeDtypeStruct
    total = pltpu.VMEM((4, depth, SPAN), F32)
    outs = [total]
    if stage == 2:
        outs = [shape((depth, SPAN), F32), shape((depth, 3 * SPAN), F32)]
    outs.append(shape((depth, len(parts) * SPAN), F32 if stage else BF16))
    scratch = [
        pltpu.VMEM((len(parts) * SPAN, WIDE), BF16),
        pltpu.VMEM((4, WIDE, SPAN), BF16),
        pltpu.VMEM((4, LANES, SPAN), jnp.int32),
        pltpu.VMEM((SPAN, WIDE), F32),
        pltpu.VMEM((SPAN, SPAN), BF16),
        pltpu.VMEM((SPAN, SPAN), BF16),
    ]
    if stage == 2:
        scratch.append(total)
    whole = pl.BlockSpec(memory_space=pltpu.VMEM)
    extra = [before] if stage else []
    return pl.pallas_call(
        functools.partial(score_kernel, plain, plain - 1.8, depth, parts, stage),
        in_specs=[pl.BlockSpec(memory_space=pltpu.SMEM)] + [whole] * (1 + len(blocks) + len(extra)),
        out_specs=[whole] * len(outs),
        out_shape=outs,
        input_output_aliases={2 + len(blocks): 0} if stage == 1 else {},
        scratch_shapes=scratch,
        compiler_params=pltpu.CompilerParams(vmem_limit_bytes=VMEM_BYTES),
    )(me, slab, *blocks, *extra)


def first_hop(axis, sent):
    half = sent.shape[1] // 6
    up = moved(sent[:, : 2 * half].astype(BF16), **{axis: -1})
    down = moved(sent[:, 2 * half : 4 * half].astype(BF16), **{axis: 1})
    return up, down


def second_hop(axis, sent, up, down):
    half = sent.shape[1] // 6
    up, down = up.astype(F32), down.astype(F32)
    far_up = moved((sent[:, 4 * half : 5 * half] + up[:, :half]).astype(BF16), **{axis: -1})
    far_down = moved((sent[:, 5 * half :] + down[:, :half]).astype(BF16), **{axis: 1})
    return jnp.concatenate(
        [down[:, half:] + far_up.astype(F32), up[:, half:] + far_down.astype(F32)], axis=1
    )


def body(
    anchor_ids,
    relation_ids,
    head_anchors,
    head_relations,
    query_relation,
    targets,
    anchor_table,
    relation_table,
    enc_weight,
    fc_weight,
):
    width = anchor_ids.shape[0]
    entities = width * 128
    queries = head_anchors.shape[0] * 128
    scale = 0.5 * float(anchor_table.shape[1]) ** (-0.5)
    me = (lax.axis_index("ent") * 16 + lax.axis_index("qry")).astype(jnp.int32)[None]
    ids = jnp.concatenate([anchor_ids.T.reshape(-1), head_anchors.T.reshape(-1)]) * 2
    own_cols, *shared = encode_entities(
        ids,
        anchor_ids.shape[1],
        relation_ids,
        anchor_table,
        relation_table,
        enc_weight,
        scale,
    )
    query = []
    piece = own_cols
    for chunk in range(CHUNKS):
        axis = ("dx", "dy")[chunk]
        sent = [moved(piece, **{axis: d}) for d in FAR]
        part, piece, *shared = encode_heads(
            chunk,
            ids,
            head_relations.T,
            query_relation[None, :],
            targets.T,
            fc_weight,
            piece,
            *shared,
            query,
        )
        query = [part]
        piece = jnp.concatenate([piece] + sent, axis=1)
    slab = piece
    other = moved(slab, dcore=1)
    up, down = moved(query[0], dz=1), moved(query[0], dz=-1)
    half = up.shape[1] // 2
    blocks = [query[0], up, down, moved(up[:, :half], dz=1), moved(down[:, half:], dz=-1)]
    asks, away = score(me, other, blocks, (0, 1, 2, 3), 0, entities)
    back = moved(away, dcore=1).astype(F32)
    asks, ents = score(me, slab, blocks, (1, 2, 3), 1, entities, asks)
    span = slab.shape[1] // 4
    ents = ents + back[:, span:]
    ent_hop = first_hop("dy", ents)
    query_total, sent, ent_row = score(me, slab, blocks, (0,), 2, entities, asks)
    sent, ent_row, *ent_hop = lax.optimization_barrier((sent, ent_row, *ent_hop))
    query_hop = first_hop("dz", sent)
    ent_row = ent_row + back[:, :span] + second_hop("dy", ents, *ent_hop)
    query_total = query_total + second_hop("dz", sent, *query_hop)
    ent_share = ent_row[:, :width]
    for k, d in enumerate(FAR):
        block = ent_row[:, (k + 1) * width : (k + 2) * width].astype(BF16)
        ent_share = ent_share + moved(block, dx=-d).astype(F32)
    return (
        ent_share * (0.5 / math.sqrt(queries)),
        query_total.T * (0.5 / scale / math.sqrt(entities)),
    )


def solution(mesh):
    spread = P(AXES, None)
    placed = (spread, spread, spread, spread, P(AXES), spread, P(), P(), P(), P())
    return jax.shard_map(
        body,
        mesh=mesh,
        in_specs=placed,
        out_specs=(P(None, AXES), spread),
        check_vma=False,
    )
```

```python
import functools
import math

import jax
import jax.numpy as jnp
from jax import lax
from jax.experimental import pallas as pl
from jax.experimental.pallas import tpu as pltpu
from jax.sharding import PartitionSpec as P

AXES = ("ent", "qry")
BF16 = jnp.bfloat16
F32 = jnp.float32
LANES = 128
WIDE = 256
CHUNK = 4096
UNROLL = 64
SPAN = 512
VMEM_BYTES = 12 * 1024 * 1024
CHUNKS = 2
FAR = (1, 3, 2)


def flat_of(x, y, z, core):
    return z * 32 + (x % 2) * 16 + y * 4 + (x // 2) * 2 + core


def coords_of(flat):
    x = ((flat // 2) % 2) * 2 + (flat // 16) % 2
    return x, (flat // 4) % 4, flat // 32, flat % 2


def moved(block, dx=0, dy=0, dz=0, dcore=0):
    route = []
    for to in range(128):
        x, y, z, core = coords_of(to)
        route.append((flat_of((x + dx) % 4, (y + dy) % 4, (z + dz) % 4, (core + dcore) % 2), to))
    return lax.ppermute(block, AXES, route)


def gather_rows(ids, table, rows, width, count, start, anchors):
    per = width // UNROLL

    def some(step, carry):
        first = step // per * count + start + step % per * UNROLL
        place = pl.multiple_of(step * (2 * UNROLL), 2 * UNROLL)
        picked = [table[pl.ds(ids[first + k], 2), :] for k in range(UNROLL)]
        for k in range(UNROLL):
            rows[pl.ds(place + 2 * k, 2), :] = picked[k]
        return carry

    lax.fori_loop(0, anchors * per, some, 0)


def relation_rows(ids, rel_table):
    shape = (rel_table.shape[1], ids.shape[1])
    hot = lax.broadcasted_iota(jnp.int32, shape, 0) == jnp.broadcast_to(ids, shape)
    hot = jnp.where(hot, 1.0, 0.0).astype(BF16)
    return jnp.dot(rel_table[...], hot, preferred_element_type=F32)


def encoded(rows, rel_ids, weights, rel_table):
    n_rel, width = rel_ids.shape
    anchors = weights.shape[1] // WIDE - n_rel
    total = jnp.zeros((weights.shape[0], width), F32)
    for t in range(anchors):
        halves = [rows[pl.ds(t * 2 * width + h, width, stride=2), :] for h in range(2)]
        part = jnp.concatenate(halves, axis=1).astype(BF16)
        total = total + lax.dot_general(
            weights[:, t * WIDE : (t + 1) * WIDE],
            part,
            (((1,), (1,)), ((), ())),
            preferred_element_type=F32,
        )
    for t in range(n_rel):
        part = relation_rows(rel_ids[t : t + 1, :], rel_table).astype(BF16)
        first = (anchors + t) * WIDE
        total = total + jnp.dot(weights[:, first : first + WIDE], part, preferred_element_type=F32)
    return total


def prepare(tab_t, w_t, rel_t, table, weights, rel_table, relations):
    step = pl.program_id(0)
    depth = tab_t.shape[0]

    @pl.when(step == 0)
    def _():
        lane = lax.broadcasted_iota(jnp.int32, (depth, WIDE), 1)
        for t in range(weights.shape[1] // WIDE):
            start = t * depth
            base = start // LANES * LANES
            piece = w_t[:, base : base + 3 * LANES].astype(F32)
            if start > base:
                piece = pltpu.roll(piece, 3 * LANES - (start - base), 1)
            weights[:, t * WIDE : (t + 1) * WIDE] = jnp.where(
                lane < depth, piece[:, :WIDE], 0.0
            ).astype(BF16)
        known = lax.broadcasted_iota(jnp.int32, rel_t.shape, 1) < relations
        rel = jnp.where(known, rel_t[...].astype(F32), 0.0)
        rel_table[...] = jnp.concatenate(
            [rel, jnp.zeros((WIDE - depth, rel.shape[1]), F32)], axis=0
        ).astype(BF16)

    chunk = tab_t.shape[1]
    top = tab_t[:LANES, :].astype(F32).T
    rest = jnp.concatenate(
        [tab_t[LANES:, :].astype(F32), jnp.zeros((WIDE - depth, chunk), F32)], axis=0
    ).T
    table[pl.ds(step * 2 * chunk, chunk, stride=2), :] = top
    table[pl.ds(step * 2 * chunk + 1, chunk, stride=2), :] = rest


def entity_kernel(
    relations, scale, own_ids, tab_t, w_t, rel_t, own_rel,
    own_out, table, weights, rel_table, rows,
):
    prepare(tab_t, w_t, rel_t, table, weights, rel_table, relations)

    @pl.when(pl.program_id(0) == pl.num_programs(0) - 1)
    def _():
        width = own_rel.shape[1]
        anchors = weights.shape[1] // WIDE - own_rel.shape[0]
        gather_rows(own_ids, table, rows, width, width, 0, anchors)
        own_out[...] = (encoded(rows, own_rel, weights, rel_table) * scale).astype(BF16)


def head_kernel(
    start, width, head_ids, head_rel, asked, wanted, fc, echo, table, weights, rel_table, *refs
):
    rows = refs[-1]
    if start:
        earlier, query_out, echo_out, whole_out = refs[:4]
        whole_out[:, :start] = earlier[...]
    else:
        query_out, echo_out = refs[:2]
    echo_out[...] = echo[...]
    part = slice(start, start + width)
    tokens, heads = head_rel.shape
    anchors = weights.shape[1] // WIDE - tokens
    before = head_ids.shape[0] - anchors * heads
    gather_rows(head_ids, table, rows, width, heads, before + start, anchors)
    head = encoded(rows, head_rel[:, part], weights, rel_table).astype(BF16)
    mixed = head.astype(F32) * relation_rows(asked[:, part], rel_table)[: head.shape[0], :]
    query = jnp.tanh(
        lax.dot_general(
            fc[...], mixed.astype(BF16), (((0,), (0,)), ((), ())), preferred_element_type=F32
        )
    )
    digits = []
    for t in range(wanted.shape[0]):
        target = wanted[t : t + 1, part]
        digits += [target // LANES, target % LANES]
    query = jnp.concatenate(
        [query, jnp.concatenate(digits, axis=0).astype(F32)], axis=0
    ).astype(BF16)
    query_out[...] = query
    if start:
        whole_out[:, start:] = query


def encode_entities(ids, anchors, relation_ids, anchor_table, relation_table, enc_weight, scale):
    own = relation_ids.shape[0]
    count, depth = anchor_table.shape
    relations = relation_table.shape[0]
    steps = pl.cdiv(count, CHUNK)
    tokens = anchors + relation_ids.shape[1]
    rel_lanes = pl.cdiv(relations, LANES) * LANES
    w_lanes = pl.cdiv((tokens - 1) * depth // LANES * LANES + 3 * LANES, LANES) * LANES
    whole = pl.BlockSpec(memory_space=pltpu.VMEM)
    once = pl.Buffered(1)
    return pl.pallas_call(
        functools.partial(entity_kernel, relations, scale),
        grid=(steps,),
        in_specs=[
            pl.BlockSpec(memory_space=pltpu.SMEM),
            pl.BlockSpec((depth, CHUNK), lambda i: (0, i)),
            pl.BlockSpec((depth, w_lanes), lambda i: (0, 0), pipeline_mode=once),
            pl.BlockSpec((depth, rel_lanes), lambda i: (0, 0), pipeline_mode=once),
            whole,
        ],
        out_specs=[whole] * 4,
        out_shape=[
            jax.ShapeDtypeStruct((depth, own), BF16),
            pltpu.VMEM((2 * steps * CHUNK, LANES), F32),
            pltpu.VMEM((depth, tokens * WIDE), BF16),
            pltpu.VMEM((WIDE, rel_lanes), BF16),
        ],
        scratch_shapes=[pltpu.VMEM((2 * own * anchors, LANES), F32)],
        compiler_params=pltpu.CompilerParams(vmem_limit_bytes=VMEM_BYTES),
    )(
        ids,
        pltpu.with_memory_space_constraint(anchor_table.T, pltpu.HBM),
        pltpu.with_memory_space_constraint(enc_weight.T, pltpu.HBM),
        pltpu.with_memory_space_constraint(relation_table.T, pltpu.HBM),
        relation_ids.T,
    )


def encode_heads(
    chunk, head_ids, head_relations, query_relation, targets, fc_weight, echo,
    table, weights, rel_table, *earlier,
):
    heads = head_relations.shape[1] // CHUNKS
    depth = fc_weight.shape[0]
    anchors = weights.shape[1] // WIDE - head_relations.shape[0]
    whole = pl.BlockSpec(memory_space=pltpu.VMEM)
    return pl.pallas_call(
        functools.partial(head_kernel, chunk * heads, heads),
        in_specs=[pl.BlockSpec(memory_space=pltpu.SMEM)] + [whole] * (8 + chunk),
        out_specs=[whole] * (5 + chunk),
        out_shape=[
            jax.ShapeDtypeStruct((depth + 2 * targets.shape[0], heads), BF16),
            jax.ShapeDtypeStruct(echo.shape, BF16),
            *[jax.ShapeDtypeStruct((depth + 2 * targets.shape[0], 2 * heads), BF16)] * chunk,
            pltpu.VMEM(table.shape, F32),
            pltpu.VMEM(weights.shape, BF16),
            pltpu.VMEM(rel_table.shape, BF16),
        ],
        input_output_aliases={6 + k: 2 + chunk + k for k in range(3)},
        scratch_shapes=[pltpu.VMEM((2 * heads * anchors, LANES), F32)],
        compiler_params=pltpu.CompilerParams(vmem_limit_bytes=VMEM_BYTES),
    )(
        head_ids, head_relations, query_relation, targets, fc_weight, echo,
        table, weights, rel_table, *earlier,
    )


def score_kernel(plain, struck_value, depth, parts, stage, me, slab, *refs):
    blocks, refs = (refs[:1], refs[1:3], refs[3:4], refs[4:6]), refs[6:]
    if stage:
        before, refs = refs[0], refs[1:]
    if stage == 2:
        kept, sent, refs = refs[0], refs[1:4], refs[4:]
    else:
        asks, refs = refs[0], refs[1:]
    ent_outs, refs = refs[: len(parts)] if stage else refs[:1], refs[len(parts) if stage else 1 :]
    tall, queries, marks, totals, *held = refs[:6]
    if stage == 2:
        asks = refs[6]
    width = SPAN
    tiles = SPAN // LANES

    x, y, z, core = coords_of(me[0])
    if not stage:
        core = 1 - core
    spots = [
        flat_of((x + dx) % 4, (y + ((0,) + FAR)[part]) % 4, z, core)
        for part in parts
        for dx in (0,) + FAR
    ]
    for k, part in enumerate(parts):
        wide = jnp.concatenate(
            [
                slab[:, part * SPAN : (part + 1) * SPAN].astype(F32),
                jnp.zeros((WIDE - depth, SPAN), F32),
            ],
            axis=0,
        )
        tall[k * SPAN : (k + 1) * SPAN, :] = wide.T.astype(BF16)
    within = lax.broadcasted_iota(jnp.int32, (LANES, width), 0)
    for b in range(4):
        query = jnp.concatenate([piece[...] for piece in blocks[b]], axis=1).astype(F32)
        queries[b] = jnp.concatenate(
            [query[:depth, :], jnp.zeros((WIDE - depth, width), F32)], axis=0
        ).astype(BF16)
        digits = query[depth:, :].astype(jnp.int32)
        marked = jnp.zeros((LANES, width), jnp.int32)
        for t in range(digits.shape[0] // 2):
            owner = digits[2 * t : 2 * t + 1, :]
            low = digits[2 * t + 1 : 2 * t + 2, :]
            bit = jnp.zeros(owner.shape, jnp.int32)
            for k, spot in enumerate(spots):
                bit = jnp.where(owner == spot, 1 << k, bit)
            marked = marked | jnp.where(within == low, bit, 0)
        marks[b] = marked

    def residual_of(step):
        k, b = step // 4, step % 4
        score = jnp.dot(
            tall[k * SPAN : (k + 1) * SPAN, :], queries[b], preferred_element_type=F32
        )
        marked = marks[b]
        for j in range(tiles):
            hit = (marked & (1 << (k * tiles + j))) != 0
            label = jnp.where(hit, struck_value, plain)
            at = slice(j * LANES, (j + 1) * LANES)
            held[step % 2][at, :] = (jnp.tanh(score[at, :]) + label).astype(BF16)

    def use(step):
        k, b = step // 4, step % 4
        first = parts[k] * SPAN
        residual = held[step % 2][...]
        ent = lax.dot_general(
            residual, queries[b], (((1,), (1,)), ((), ())), preferred_element_type=F32
        )
        ask = jnp.dot(slab[:, first : first + SPAN], residual, preferred_element_type=F32)
        if b == 0:
            totals[...] = ent
        elif b < 3:
            totals[...] += ent
        else:
            ent = (totals[...] + ent).T[:depth, :]
            if stage:
                ent_outs[k][...] = ent
            else:
                ent_outs[0][:, k * SPAN : (k + 1) * SPAN] = ent.astype(BF16)
        if k:
            ask = asks[b] + ask
        elif stage:
            ask = before[b] + ask
        if stage == 2 and k == len(parts) - 1:
            if b:
                sent[b - 1][...] = ask.astype(BF16)
            else:
                kept[...] = ask
        else:
            asks[b] = ask

    steps = 4 * len(parts)
    residual_of(0)
    for step in range(steps):
        if step + 1 < steps:
            residual_of(step + 1)
        use(step)


def score(me, slab, blocks, parts, stage, total_entities, before=None):
    depth, entities = slab.shape
    plain = 1.0 - 2.0 * (0.1 / total_entities)
    shape = jax.ShapeDtypeStruct
    total = pltpu.VMEM((4, depth, SPAN), F32)
    outs = [total]
    if stage == 2:
        outs = [shape((depth, SPAN), F32)] + [shape((depth, SPAN), BF16)] * 3
    outs += [shape((depth, SPAN), F32)] * len(parts) if stage else [shape((depth, entities), BF16)]
    scratch = [
        pltpu.VMEM((len(parts) * SPAN, WIDE), BF16),
        pltpu.VMEM((4, WIDE, SPAN), BF16),
        pltpu.VMEM((4, LANES, SPAN), jnp.int32),
        pltpu.VMEM((SPAN, WIDE), F32),
        pltpu.VMEM((SPAN, SPAN), BF16),
        pltpu.VMEM((SPAN, SPAN), BF16),
    ]
    if stage == 2:
        scratch.append(total)
    whole = pl.BlockSpec(memory_space=pltpu.VMEM)
    extra = [before] if stage else []
    return pl.pallas_call(
        functools.partial(score_kernel, plain, plain - 1.8, depth, parts, stage),
        in_specs=[pl.BlockSpec(memory_space=pltpu.SMEM)] + [whole] * (1 + len(blocks) + len(extra)),
        out_specs=[whole] * len(outs),
        out_shape=outs,
        input_output_aliases={2 + len(blocks): 0} if stage == 1 else {},
        scratch_shapes=scratch,
        compiler_params=pltpu.CompilerParams(vmem_limit_bytes=VMEM_BYTES),
    )(me, slab, *blocks, *extra)


def body(
    anchor_ids,
    relation_ids,
    head_anchors,
    head_relations,
    query_relation,
    targets,
    anchor_table,
    relation_table,
    enc_weight,
    fc_weight,
):
    width = anchor_ids.shape[0]
    entities = width * 128
    queries = head_anchors.shape[0] * 128
    scale = 0.5 * float(anchor_table.shape[1]) ** (-0.5)
    me = (lax.axis_index("ent") * 16 + lax.axis_index("qry")).astype(jnp.int32)[None]
    ids = jnp.concatenate([anchor_ids.T.reshape(-1), head_anchors.T.reshape(-1)]) * 2
    own_cols, *shared = encode_entities(
        ids,
        anchor_ids.shape[1],
        relation_ids,
        anchor_table,
        relation_table,
        enc_weight,
        scale,
    )
    heads = (head_relations.T, query_relation[None, :], targets.T, fc_weight)
    sent = [moved(own_cols, dx=d) for d in FAR]
    early, own_cols, *shared = encode_heads(0, ids, *heads, own_cols, *shared)
    row = jnp.concatenate([own_cols] + sent, axis=1)
    first = [moved(early, dz=d) for d in (1, 2)]
    sent = [moved(row, dy=d) for d in FAR]
    late, row, query, *shared = encode_heads(1, ids, *heads, row, *shared, early)
    late, query, row, *first = lax.optimization_barrier((late, query, row, *first))
    slab = jnp.concatenate([row] + sent, axis=1)
    other = moved(slab, dcore=1)
    second = [moved(late, dz=d) for d in (1, 2)]
    blocks = [query, first[0], second[0], moved(query, dz=3), first[1], second[1]]
    asks, away = score(me, other, blocks, (0, 1, 2, 3), 0, entities)
    back = moved(away, dcore=1).astype(F32)
    asks, *ents = score(me, slab, blocks, (1, 2, 3), 1, entities, asks)
    span = slab.shape[1] // 4
    ents = [
        moved((ent + back[:, (k + 1) * span : (k + 2) * span]).astype(BF16), dy=-d)
        for k, (d, ent) in enumerate(zip(FAR, ents))
    ]
    query_total, *sums, ent_row = score(me, slab, blocks, (0,), 2, entities, asks)
    ent_row = ent_row + back[:, :span]
    for ent in ents:
        ent_row = ent_row + ent.astype(F32)
    for d, part in zip(FAR, sums):
        query_total = query_total + moved(part, dz=-d).astype(F32)
    ent_share = ent_row[:, :width]
    for k, d in enumerate(FAR):
        block = ent_row[:, (k + 1) * width : (k + 2) * width].astype(BF16)
        ent_share = ent_share + moved(block, dx=-d).astype(F32)
    return (
        ent_share * (0.5 / math.sqrt(queries)),
        query_total.T * (0.5 / scale / math.sqrt(entities)),
    )


def solution(mesh):
    spread = P(AXES, None)
    placed = (spread, spread, spread, spread, P(AXES), spread, P(), P(), P(), P())
    return jax.shard_map(
        body,
        mesh=mesh,
        in_specs=placed,
        out_specs=(P(None, AXES), spread),
        check_vma=False,
    )
```

```python
import functools
import math

import jax
import jax.numpy as jnp
from jax import lax
from jax.experimental import pallas as pl
from jax.experimental.pallas import tpu as pltpu
from jax.sharding import PartitionSpec as P

AXES = ("ent", "qry")
BF16 = jnp.bfloat16
F32 = jnp.float32
LANES = 128
WIDE = 256
CHUNK = 4096
UNROLL = 64
SPAN = 512
VMEM_BYTES = 12 * 1024 * 1024
CHUNKS = 2
FAR = (1, 3, 2)


def flat_of(x, y, z, core):
    return z * 32 + (x % 2) * 16 + y * 4 + (x // 2) * 2 + core


def coords_of(flat):
    x = ((flat // 2) % 2) * 2 + (flat // 16) % 2
    return x, (flat // 4) % 4, flat // 32, flat % 2


def moved(block, dx=0, dy=0, dz=0, dcore=0):
    route = []
    for to in range(128):
        x, y, z, core = coords_of(to)
        route.append((flat_of((x + dx) % 4, (y + dy) % 4, (z + dz) % 4, (core + dcore) % 2), to))
    return lax.ppermute(block, AXES, route)


def gather_rows(ids, table, rows, width, count, start, anchors):
    per = width // UNROLL

    def some(step, carry):
        first = step // per * count + start + step % per * UNROLL
        place = pl.multiple_of(step * (2 * UNROLL), 2 * UNROLL)
        picked = [table[pl.ds(ids[first + k], 2), :] for k in range(UNROLL)]
        for k in range(UNROLL):
            rows[pl.ds(place + 2 * k, 2), :] = picked[k]
        return carry

    lax.fori_loop(0, anchors * per, some, 0)


def relation_rows(ids, rel_table):
    shape = (rel_table.shape[1], ids.shape[1])
    hot = lax.broadcasted_iota(jnp.int32, shape, 0) == jnp.broadcast_to(ids, shape)
    hot = jnp.where(hot, 1.0, 0.0).astype(BF16)
    return jnp.dot(rel_table[...], hot, preferred_element_type=F32)


def encoded(rows, rel_ids, weights, rel_table):
    n_rel, width = rel_ids.shape
    anchors = weights.shape[1] // WIDE - n_rel
    total = jnp.zeros((weights.shape[0], width), F32)
    for t in range(anchors):
        halves = [rows[pl.ds(t * 2 * width + h, width, stride=2), :] for h in range(2)]
        part = jnp.concatenate(halves, axis=1).astype(BF16)
        total = total + lax.dot_general(
            weights[:, t * WIDE : (t + 1) * WIDE],
            part,
            (((1,), (1,)), ((), ())),
            preferred_element_type=F32,
        )
    for t in range(n_rel):
        part = relation_rows(rel_ids[t : t + 1, :], rel_table).astype(BF16)
        first = (anchors + t) * WIDE
        total = total + jnp.dot(weights[:, first : first + WIDE], part, preferred_element_type=F32)
    return total


def prepare(tab_t, w_t, rel_t, table, weights, rel_table, relations, steps):
    step = pl.program_id(0)
    depth = tab_t.shape[0]

    tokens = weights.shape[1] // WIDE
    share = pl.cdiv(tokens, steps)
    for turn in range(steps):

        @pl.when(step == turn)
        def _(turn=turn):
            lane = lax.broadcasted_iota(jnp.int32, (depth, WIDE), 1)
            for t in range(turn * share, min((turn + 1) * share, tokens)):
                start = t * depth
                base = start // LANES * LANES
                piece = w_t[:, base : base + 3 * LANES].astype(F32)
                if start > base:
                    piece = pltpu.roll(piece, 3 * LANES - (start - base), 1)
                weights[:, t * WIDE : (t + 1) * WIDE] = jnp.where(
                    lane < depth, piece[:, :WIDE], 0.0
                ).astype(BF16)

    @pl.when(step == 0)
    def _():
        known = lax.broadcasted_iota(jnp.int32, rel_t.shape, 1) < relations
        rel = jnp.where(known, rel_t[...].astype(F32), 0.0)
        rel_table[...] = jnp.concatenate(
            [rel, jnp.zeros((WIDE - depth, rel.shape[1]), F32)], axis=0
        ).astype(BF16)

    chunk = tab_t.shape[1]
    top = tab_t[:LANES, :].astype(F32).T
    rest = jnp.concatenate(
        [tab_t[LANES:, :].astype(F32), jnp.zeros((WIDE - depth, chunk), F32)], axis=0
    ).T
    table[pl.ds(step * 2 * chunk, chunk, stride=2), :] = top
    table[pl.ds(step * 2 * chunk + 1, chunk, stride=2), :] = rest


def entity_kernel(
    relations, steps, scale, own_ids, tab_t, w_t, rel_t, own_rel,
    own_out, table, weights, rel_table, rows,
):
    prepare(tab_t, w_t, rel_t, table, weights, rel_table, relations, steps)

    @pl.when(pl.program_id(0) == pl.num_programs(0) - 1)
    def _():
        width = own_rel.shape[1]
        anchors = weights.shape[1] // WIDE - own_rel.shape[0]
        gather_rows(own_ids, table, rows, width, width, 0, anchors)
        own_out[...] = (encoded(rows, own_rel, weights, rel_table) * scale).astype(BF16)


def head_kernel(
    start, width, head_ids, head_rel, asked, wanted, fc, echo, table, weights, rel_table, *refs
):
    rows = refs[-1]
    if start:
        earlier, query_out, echo_out, whole_out = refs[:4]
        whole_out[:, :start] = earlier[...]
    else:
        query_out, echo_out = refs[:2]
    echo_out[...] = echo[...]
    part = slice(start, start + width)
    tokens, heads = head_rel.shape
    anchors = weights.shape[1] // WIDE - tokens
    before = head_ids.shape[0] - anchors * heads
    gather_rows(head_ids, table, rows, width, heads, before + start, anchors)
    head = encoded(rows, head_rel[:, part], weights, rel_table).astype(BF16)
    mixed = head.astype(F32) * relation_rows(asked[:, part], rel_table)[: head.shape[0], :]
    query = jnp.tanh(
        lax.dot_general(
            fc[...], mixed.astype(BF16), (((0,), (0,)), ((), ())), preferred_element_type=F32
        )
    )
    digits = []
    for t in range(wanted.shape[0]):
        target = wanted[t : t + 1, part]
        digits += [target // LANES, target % LANES]
    query = jnp.concatenate(
        [query, jnp.concatenate(digits, axis=0).astype(F32)], axis=0
    ).astype(BF16)
    query_out[...] = query
    if start:
        whole_out[:, start:] = query


def encode_entities(ids, anchors, relation_ids, anchor_table, relation_table, enc_weight, scale):
    own = relation_ids.shape[0]
    count, depth = anchor_table.shape
    relations = relation_table.shape[0]
    steps = pl.cdiv(count, CHUNK)
    tokens = anchors + relation_ids.shape[1]
    rel_lanes = pl.cdiv(relations, LANES) * LANES
    w_lanes = pl.cdiv((tokens - 1) * depth // LANES * LANES + 3 * LANES, LANES) * LANES
    whole = pl.BlockSpec(memory_space=pltpu.VMEM)
    once = pl.Buffered(1)
    return pl.pallas_call(
        functools.partial(entity_kernel, relations, steps, scale),
        grid=(steps,),
        in_specs=[
            pl.BlockSpec(memory_space=pltpu.SMEM),
            pl.BlockSpec((depth, CHUNK), lambda i: (0, i)),
            pl.BlockSpec((depth, w_lanes), lambda i: (0, 0), pipeline_mode=once),
            pl.BlockSpec((depth, rel_lanes), lambda i: (0, 0), pipeline_mode=once),
            whole,
        ],
        out_specs=[whole] * 4,
        out_shape=[
            jax.ShapeDtypeStruct((depth, own), BF16),
            pltpu.VMEM((2 * steps * CHUNK, LANES), F32),
            pltpu.VMEM((depth, tokens * WIDE), BF16),
            pltpu.VMEM((WIDE, rel_lanes), BF16),
        ],
        scratch_shapes=[pltpu.VMEM((2 * own * anchors, LANES), F32)],
        compiler_params=pltpu.CompilerParams(vmem_limit_bytes=VMEM_BYTES),
    )(
        ids,
        pltpu.with_memory_space_constraint(anchor_table.T, pltpu.HBM),
        pltpu.with_memory_space_constraint(enc_weight.T, pltpu.HBM),
        pltpu.with_memory_space_constraint(relation_table.T, pltpu.HBM),
        relation_ids.T,
    )


def encode_heads(
    chunk, head_ids, head_relations, query_relation, targets, fc_weight, echo,
    table, weights, rel_table, *earlier,
):
    heads = head_relations.shape[1] // CHUNKS
    depth = fc_weight.shape[0]
    anchors = weights.shape[1] // WIDE - head_relations.shape[0]
    whole = pl.BlockSpec(memory_space=pltpu.VMEM)
    return pl.pallas_call(
        functools.partial(head_kernel, chunk * heads, heads),
        in_specs=[pl.BlockSpec(memory_space=pltpu.SMEM)] + [whole] * (8 + chunk),
        out_specs=[whole] * (5 + chunk),
        out_shape=[
            jax.ShapeDtypeStruct((depth + 2 * targets.shape[0], heads), BF16),
            jax.ShapeDtypeStruct(echo.shape, BF16),
            *[jax.ShapeDtypeStruct((depth + 2 * targets.shape[0], 2 * heads), BF16)] * chunk,
            pltpu.VMEM(table.shape, F32),
            pltpu.VMEM(weights.shape, BF16),
            pltpu.VMEM(rel_table.shape, BF16),
        ],
        input_output_aliases={6 + k: 2 + chunk + k for k in range(3)},
        scratch_shapes=[pltpu.VMEM((2 * heads * anchors, LANES), F32)],
        compiler_params=pltpu.CompilerParams(vmem_limit_bytes=VMEM_BYTES),
    )(
        head_ids, head_relations, query_relation, targets, fc_weight, echo,
        table, weights, rel_table, *earlier,
    )


def score_kernel(plain, struck_value, depth, parts, pieces, stage, me, slab, *refs):
    blocks = []
    for count in pieces:
        blocks.append(refs[:count])
        refs = refs[count:]
    before = None
    if stage > 1:
        before, refs = refs[0], refs[1:]
    if stage == 3:
        kept, sent, refs = refs[0], refs[1:4], refs[4:]
        kept[...] = before[0]
    else:
        asks, refs = refs[0], refs[1:]
    ents, tall, queries, marks, totals, *held = refs[:7]
    if stage == 3:
        asks = refs[7]
    if stage == 2:
        asks[0] = before[0]
    number = len(blocks)
    base = 1 if stage > 1 else 0
    width = SPAN
    tiles = SPAN // LANES

    x, y, z, core = coords_of(me[0])
    if stage == 1:
        core = 1 - core
    spots = [
        flat_of((x + dx) % 4, (y + ((0,) + FAR)[part]) % 4, z, core)
        for part in parts
        for dx in (0,) + FAR
    ]
    for k, part in enumerate(parts):
        wide = jnp.concatenate(
            [
                slab[:, part * SPAN : (part + 1) * SPAN].astype(F32),
                jnp.zeros((WIDE - depth, SPAN), F32),
            ],
            axis=0,
        )
        tall[k * SPAN : (k + 1) * SPAN, :] = wide.T.astype(BF16)
    within = lax.broadcasted_iota(jnp.int32, (LANES, width), 0)
    for b in range(number):
        query = jnp.concatenate([piece[...] for piece in blocks[b]], axis=1).astype(F32)
        queries[b] = jnp.concatenate(
            [query[:depth, :], jnp.zeros((WIDE - depth, width), F32)], axis=0
        ).astype(BF16)
        digits = query[depth:, :].astype(jnp.int32)
        marked = jnp.zeros((LANES, width), jnp.int32)
        for t in range(digits.shape[0] // 2):
            owner = digits[2 * t : 2 * t + 1, :]
            low = digits[2 * t + 1 : 2 * t + 2, :]
            bit = jnp.zeros(owner.shape, jnp.int32)
            for k, spot in enumerate(spots):
                bit = jnp.where(owner == spot, 1 << k, bit)
            marked = marked | jnp.where(within == low, bit, 0)
        marks[b] = marked

    def residual_of(step):
        k, b = step // number, step % number
        score = jnp.dot(
            tall[k * SPAN : (k + 1) * SPAN, :], queries[b], preferred_element_type=F32
        )
        marked = marks[b]
        for j in range(tiles):
            hit = (marked & (1 << (k * tiles + j))) != 0
            label = jnp.where(hit, struck_value, plain)
            at = slice(j * LANES, (j + 1) * LANES)
            held[step % 2][at, :] = (jnp.tanh(score[at, :]) + label).astype(BF16)

    def use(step):
        k, b = step // number, step % number
        first = parts[k] * SPAN
        residual = held[step % 2][...]
        ent = lax.dot_general(
            residual, queries[b], (((1,), (1,)), ((), ())), preferred_element_type=F32
        )
        ask = jnp.dot(slab[:, first : first + SPAN], residual, preferred_element_type=F32)
        if b:
            ent = totals[...] + ent
        if b < number - 1:
            totals[...] = ent
        else:
            ents[:, k * SPAN : (k + 1) * SPAN] = ent.T[:depth, :].astype(ents.dtype)
        if k:
            ask = asks[base + b] + ask
        elif stage > 1:
            ask = before[base + b] + ask
        if stage == 3 and k == len(parts) - 1:
            sent[b][...] = ask.astype(BF16)
        else:
            asks[base + b] = ask

    steps = number * len(parts)
    residual_of(0)
    for step in range(steps):
        if step + 1 < steps:
            residual_of(step + 1)
        use(step)


def score(me, slab, blocks, parts, stage, total_entities, before=None):
    depth = slab.shape[0]
    plain = 1.0 - 2.0 * (0.1 / total_entities)
    shape = jax.ShapeDtypeStruct
    number = len(blocks)
    total = pltpu.VMEM((1 if stage == 0 else 4, depth, SPAN), F32)
    outs = [total]
    if stage == 3:
        outs = [shape((depth, SPAN), F32)] + [shape((depth, SPAN), BF16)] * 3
    outs.append(shape((depth, len(parts) * SPAN), BF16 if stage == 1 else F32))
    scratch = [
        pltpu.VMEM((len(parts) * SPAN, WIDE), BF16),
        pltpu.VMEM((number, WIDE, SPAN), BF16),
        pltpu.VMEM((number, LANES, SPAN), jnp.int32),
        pltpu.VMEM((SPAN, WIDE), F32),
        pltpu.VMEM((SPAN, SPAN), BF16),
        pltpu.VMEM((SPAN, SPAN), BF16),
    ]
    if stage == 3:
        scratch.append(total)
    whole = pl.BlockSpec(memory_space=pltpu.VMEM)
    given = [piece for block in blocks for piece in block] + ([before] if stage > 1 else [])
    return pl.pallas_call(
        functools.partial(
            score_kernel, plain, plain - 1.8, depth, parts, [len(b) for b in blocks], stage
        ),
        in_specs=[pl.BlockSpec(memory_space=pltpu.SMEM)] + [whole] * (1 + len(given)),
        out_specs=[whole] * len(outs),
        out_shape=outs,
        input_output_aliases={1 + len(given): 0} if stage == 2 else {},
        scratch_shapes=scratch,
        compiler_params=pltpu.CompilerParams(vmem_limit_bytes=VMEM_BYTES),
    )(me, slab, *given)


def body(
    anchor_ids,
    relation_ids,
    head_anchors,
    head_relations,
    query_relation,
    targets,
    anchor_table,
    relation_table,
    enc_weight,
    fc_weight,
):
    width = anchor_ids.shape[0]
    entities = width * 128
    queries = head_anchors.shape[0] * 128
    scale = 0.5 * float(anchor_table.shape[1]) ** (-0.5)
    me = (lax.axis_index("ent") * 16 + lax.axis_index("qry")).astype(jnp.int32)[None]
    ids = jnp.concatenate([anchor_ids.T.reshape(-1), head_anchors.T.reshape(-1)]) * 2
    own_cols, *shared = encode_entities(
        ids,
        anchor_ids.shape[1],
        relation_ids,
        anchor_table,
        relation_table,
        enc_weight,
        scale,
    )
    heads = (head_relations.T, query_relation[None, :], targets.T, fc_weight)
    sent = [moved(own_cols, dx=d) for d in FAR]
    early, own_cols, *shared = encode_heads(0, ids, *heads, own_cols, *shared)
    row = jnp.concatenate([own_cols] + sent, axis=1)
    first = [moved(early, dz=d) for d in (1, 2)]
    sent = [moved(row, dy=d) for d in FAR]
    late, row, query, *shared = encode_heads(1, ids, *heads, row, *shared, early)
    late, query, row, *first = lax.optimization_barrier((late, query, row, *first))
    slab = jnp.concatenate([row] + sent, axis=1)
    other = moved(slab, dcore=1)
    second = [moved(late, dz=d) for d in (1, 2)]
    own_asks, own_ents = score(me, slab, [[query]], (0, 1, 2, 3), 0, entities)
    own_asks, own_ents, last, *second = lax.optimization_barrier(
        (own_asks, own_ents, moved(query, dz=3), *second)
    )
    blocks = [[query], [first[0], second[0]], [last], [first[1], second[1]]]
    asks, away = score(me, other, blocks, (0, 1, 2, 3), 1, entities)
    back = moved(away, dcore=1)
    asks, ents = score(me, slab, blocks[1:], (1, 2, 3), 2, entities, asks)
    span = slab.shape[1] // 4

    def slab_sum(part, k):
        at = slice(k * span, (k + 1) * span)
        return part + own_ents[:, at] + back[:, at].astype(F32)

    ents = [ents[:, k * span : (k + 1) * span] for k in range(3)]
    ents = [slab_sum(part, k + 1).astype(BF16) for k, part in enumerate(ents)]
    ents = [moved(part, dy=-d) for d, part in zip(FAR, ents)]
    query_total, *sums, ent_row = score(me, slab, blocks[1:], (0,), 3, entities, asks)
    query_total = query_total + own_asks[0]
    ent_row = slab_sum(ent_row, 0)
    for ent in ents:
        ent_row = ent_row + ent.astype(F32)
    for d, part in zip(FAR, sums):
        query_total = query_total + moved(part, dz=-d).astype(F32)
    ent_share = ent_row[:, :width]
    for k, d in enumerate(FAR):
        block = ent_row[:, (k + 1) * width : (k + 2) * width].astype(BF16)
        ent_share = ent_share + moved(block, dx=-d).astype(F32)
    return (
        ent_share * (0.5 / math.sqrt(queries)),
        query_total.T * (0.5 / scale / math.sqrt(entities)),
    )


def solution(mesh):
    spread = P(AXES, None)
    placed = (spread, spread, spread, spread, P(AXES), spread, P(), P(), P(), P())
    return jax.shard_map(
        body,
        mesh=mesh,
        in_specs=placed,
        out_specs=(P(None, AXES), spread),
        check_vma=False,
    )
```

```python
import functools
import math

import jax
import jax.numpy as jnp
from jax import lax
from jax.experimental import pallas as pl
from jax.experimental.pallas import tpu as pltpu
from jax.sharding import PartitionSpec as P

AXES = ("ent", "qry")
BF16 = jnp.bfloat16
F32 = jnp.float32
LANES = 128
WIDE = 256
CHUNK = 4096
UNROLL = 64
SPAN = 512
VMEM_BYTES = 12 * 1024 * 1024
CHUNKS = 2
FAR = (1, 3, 2)


def flat_of(x, y, z, core):
    return z * 32 + (x % 2) * 16 + y * 4 + (x // 2) * 2 + core


def coords_of(flat):
    x = ((flat // 2) % 2) * 2 + (flat // 16) % 2
    return x, (flat // 4) % 4, flat // 32, flat % 2


def moved(block, dx=0, dy=0, dz=0, dcore=0):
    route = []
    for to in range(128):
        x, y, z, core = coords_of(to)
        route.append((flat_of((x + dx) % 4, (y + dy) % 4, (z + dz) % 4, (core + dcore) % 2), to))
    return lax.ppermute(block, AXES, route)


def gather_rows(ids, table, rows, width, count, start, anchors):
    per = width // UNROLL

    def some(step, carry):
        first = step // per * count + start + step % per * UNROLL
        place = pl.multiple_of(step * (2 * UNROLL), 2 * UNROLL)
        picked = [table[pl.ds(ids[first + k], 2), :] for k in range(UNROLL)]
        for k in range(UNROLL):
            rows[pl.ds(place + 2 * k, 2), :] = picked[k]
        return carry

    lax.fori_loop(0, anchors * per, some, 0)


def relation_rows(ids, rel_table):
    shape = (rel_table.shape[1], ids.shape[1])
    hot = lax.broadcasted_iota(jnp.int32, shape, 0) == jnp.broadcast_to(ids, shape)
    hot = jnp.where(hot, 1.0, 0.0).astype(BF16)
    return jnp.dot(rel_table[...], hot, preferred_element_type=F32)


def encoded(rows, rel_ids, weights, rel_table):
    n_rel, width = rel_ids.shape
    anchors = weights.shape[1] // WIDE - n_rel
    total = jnp.zeros((weights.shape[0], width), F32)
    for t in range(anchors):
        halves = [rows[pl.ds(t * 2 * width + h, width, stride=2), :] for h in range(2)]
        part = jnp.concatenate(halves, axis=1).astype(BF16)
        total = total + lax.dot_general(
            weights[:, t * WIDE : (t + 1) * WIDE],
            part,
            (((1,), (1,)), ((), ())),
            preferred_element_type=F32,
        )
    for t in range(n_rel):
        part = relation_rows(rel_ids[t : t + 1, :], rel_table).astype(BF16)
        first = (anchors + t) * WIDE
        total = total + jnp.dot(weights[:, first : first + WIDE], part, preferred_element_type=F32)
    return total


def prepare(tab_t, w_t, rel_t, table, weights, rel_table, relations, steps):
    step = pl.program_id(0)
    depth = tab_t.shape[0]

    tokens = weights.shape[1] // WIDE
    share = pl.cdiv(tokens, steps)
    for turn in range(steps):

        @pl.when(step == turn)
        def _(turn=turn):
            lane = lax.broadcasted_iota(jnp.int32, (depth, WIDE), 1)
            for t in range(turn * share, min((turn + 1) * share, tokens)):
                start = t * depth
                base = start // LANES * LANES
                piece = w_t[:, base : base + 3 * LANES].astype(F32)
                if start > base:
                    piece = pltpu.roll(piece, 3 * LANES - (start - base), 1)
                weights[:, t * WIDE : (t + 1) * WIDE] = jnp.where(
                    lane < depth, piece[:, :WIDE], 0.0
                ).astype(BF16)

    @pl.when(step == 0)
    def _():
        known = lax.broadcasted_iota(jnp.int32, rel_t.shape, 1) < relations
        rel = jnp.where(known, rel_t[...].astype(F32), 0.0)
        rel_table[...] = jnp.concatenate(
            [rel, jnp.zeros((WIDE - depth, rel.shape[1]), F32)], axis=0
        ).astype(BF16)

    chunk = tab_t.shape[1]
    top = tab_t[:LANES, :].astype(F32).T
    rest = jnp.concatenate(
        [tab_t[LANES:, :].astype(F32), jnp.zeros((WIDE - depth, chunk), F32)], axis=0
    ).T
    table[pl.ds(step * 2 * chunk, chunk, stride=2), :] = top
    table[pl.ds(step * 2 * chunk + 1, chunk, stride=2), :] = rest


def entity_kernel(
    relations, steps, scale, own_ids, tab_t, w_t, rel_t, own_rel,
    own_out, table, weights, rel_table, rows,
):
    prepare(tab_t, w_t, rel_t, table, weights, rel_table, relations, steps)

    @pl.when(pl.program_id(0) == pl.num_programs(0) - 1)
    def _():
        width = own_rel.shape[1]
        anchors = weights.shape[1] // WIDE - own_rel.shape[0]
        gather_rows(own_ids, table, rows, width, width, 0, anchors)
        own_out[...] = (encoded(rows, own_rel, weights, rel_table) * scale).astype(BF16)


def head_kernel(
    start, width, head_ids, head_rel, asked, wanted, fc, echo, table, weights, rel_table, *refs
):
    rows = refs[-1]
    if start:
        earlier, query_out, echo_out, whole_out = refs[:4]
        whole_out[:, :start] = earlier[...]
    else:
        query_out, echo_out = refs[:2]
    echo_out[...] = echo[...]
    part = slice(start, start + width)
    tokens, heads = head_rel.shape
    anchors = weights.shape[1] // WIDE - tokens
    before = head_ids.shape[0] - anchors * heads
    gather_rows(head_ids, table, rows, width, heads, before + start, anchors)
    head = encoded(rows, head_rel[:, part], weights, rel_table).astype(BF16)
    mixed = head.astype(F32) * relation_rows(asked[:, part], rel_table)[: head.shape[0], :]
    query = jnp.tanh(
        lax.dot_general(
            fc[...], mixed.astype(BF16), (((0,), (0,)), ((), ())), preferred_element_type=F32
        )
    )
    digits = []
    for t in range(wanted.shape[0]):
        target = wanted[t : t + 1, part]
        digits += [target // LANES, target % LANES]
    query = jnp.concatenate(
        [query, jnp.concatenate(digits, axis=0).astype(F32)], axis=0
    ).astype(BF16)
    query_out[...] = query
    if start:
        whole_out[:, start:] = query


def encode_entities(ids, anchors, relation_ids, anchor_table, relation_table, enc_weight, scale):
    own = relation_ids.shape[0]
    count, depth = anchor_table.shape
    relations = relation_table.shape[0]
    steps = pl.cdiv(count, CHUNK)
    tokens = anchors + relation_ids.shape[1]
    rel_lanes = pl.cdiv(relations, LANES) * LANES
    w_lanes = pl.cdiv((tokens - 1) * depth // LANES * LANES + 3 * LANES, LANES) * LANES
    whole = pl.BlockSpec(memory_space=pltpu.VMEM)
    once = pl.Buffered(1)
    return pl.pallas_call(
        functools.partial(entity_kernel, relations, steps, scale),
        grid=(steps,),
        in_specs=[
            pl.BlockSpec(memory_space=pltpu.SMEM),
            pl.BlockSpec((depth, CHUNK), lambda i: (0, i)),
            pl.BlockSpec((depth, w_lanes), lambda i: (0, 0), pipeline_mode=once),
            pl.BlockSpec((depth, rel_lanes), lambda i: (0, 0), pipeline_mode=once),
            whole,
        ],
        out_specs=[whole] * 4,
        out_shape=[
            jax.ShapeDtypeStruct((depth, own), BF16),
            pltpu.VMEM((2 * steps * CHUNK, LANES), F32),
            pltpu.VMEM((depth, tokens * WIDE), BF16),
            pltpu.VMEM((WIDE, rel_lanes), BF16),
        ],
        scratch_shapes=[pltpu.VMEM((2 * own * anchors, LANES), F32)],
        compiler_params=pltpu.CompilerParams(vmem_limit_bytes=VMEM_BYTES),
    )(
        ids,
        pltpu.with_memory_space_constraint(anchor_table.T, pltpu.HBM),
        pltpu.with_memory_space_constraint(enc_weight.T, pltpu.HBM),
        pltpu.with_memory_space_constraint(relation_table.T, pltpu.HBM),
        relation_ids.T,
    )


def encode_heads(
    chunk, head_ids, head_relations, query_relation, targets, fc_weight, echo,
    table, weights, rel_table, *earlier,
):
    heads = head_relations.shape[1] // CHUNKS
    depth = fc_weight.shape[0]
    anchors = weights.shape[1] // WIDE - head_relations.shape[0]
    whole = pl.BlockSpec(memory_space=pltpu.VMEM)
    return pl.pallas_call(
        functools.partial(head_kernel, chunk * heads, heads),
        in_specs=[pl.BlockSpec(memory_space=pltpu.SMEM)] + [whole] * (8 + chunk),
        out_specs=[whole] * (5 + chunk),
        out_shape=[
            jax.ShapeDtypeStruct((depth + 2 * targets.shape[0], heads), BF16),
            jax.ShapeDtypeStruct(echo.shape, BF16),
            *[jax.ShapeDtypeStruct((depth + 2 * targets.shape[0], 2 * heads), BF16)] * chunk,
            pltpu.VMEM(table.shape, F32),
            pltpu.VMEM(weights.shape, BF16),
            pltpu.VMEM(rel_table.shape, BF16),
        ],
        input_output_aliases={6 + k: 2 + chunk + k for k in range(3)},
        scratch_shapes=[pltpu.VMEM((2 * heads * anchors, LANES), F32)],
        compiler_params=pltpu.CompilerParams(vmem_limit_bytes=VMEM_BYTES),
    )(
        head_ids, head_relations, query_relation, targets, fc_weight, echo,
        table, weights, rel_table, *earlier,
    )


def score_kernel(plain, struck_value, depth, parts, pieces, stage, me, slab, *refs):
    blocks = []
    for count in pieces:
        blocks.append(refs[:count])
        refs = refs[count:]
    before = None
    if stage:
        before, refs = refs[0], refs[1:]
    if stage == 3:
        kept, sent, refs = refs[0], refs[1:4], refs[4:]
        kept[...] = before[0]
    else:
        asks, refs = refs[0], refs[1:]
    ents, tall, queries, marks, totals, *held = refs
    if stage == 2:
        asks[:2] = before[:2]
    number = len(blocks)
    base = 2 if stage > 1 else 0
    width = SPAN
    tiles = SPAN // LANES

    x, y, z, core = coords_of(me[0])
    if stage == 1:
        core = 1 - core
    spots = [
        flat_of((x + dx) % 4, (y + ((0,) + FAR)[part]) % 4, z, core)
        for part in parts
        for dx in (0,) + FAR
    ]
    for k, part in enumerate(parts):
        wide = jnp.concatenate(
            [
                slab[:, part * SPAN : (part + 1) * SPAN].astype(F32),
                jnp.zeros((WIDE - depth, SPAN), F32),
            ],
            axis=0,
        )
        tall[k * SPAN : (k + 1) * SPAN, :] = wide.T.astype(BF16)
    within = lax.broadcasted_iota(jnp.int32, (LANES, width), 0)
    for b in range(number):
        query = jnp.concatenate([piece[...] for piece in blocks[b]], axis=1).astype(F32)
        queries[b] = jnp.concatenate(
            [query[:depth, :], jnp.zeros((WIDE - depth, width), F32)], axis=0
        ).astype(BF16)
        digits = query[depth:, :].astype(jnp.int32)
        marked = jnp.zeros((LANES, width), jnp.int32)
        for t in range(digits.shape[0] // 2):
            owner = digits[2 * t : 2 * t + 1, :]
            low = digits[2 * t + 1 : 2 * t + 2, :]
            bit = jnp.zeros(owner.shape, jnp.int32)
            for k, spot in enumerate(spots):
                bit = jnp.where(owner == spot, 1 << k, bit)
            marked = marked | jnp.where(within == low, bit, 0)
        marks[b] = marked

    def residual_of(step):
        k, b = step // number, step % number
        score = jnp.dot(
            tall[k * SPAN : (k + 1) * SPAN, :], queries[b], preferred_element_type=F32
        )
        marked = marks[b]
        for j in range(tiles):
            hit = (marked & (1 << (k * tiles + j))) != 0
            label = jnp.where(hit, struck_value, plain)
            at = slice(j * LANES, (j + 1) * LANES)
            held[step % 2][at, :] = (jnp.tanh(score[at, :]) + label).astype(BF16)

    def use(step):
        k, b = step // number, step % number
        first = parts[k] * SPAN
        residual = held[step % 2][...]
        ent = lax.dot_general(
            residual, queries[b], (((1,), (1,)), ((), ())), preferred_element_type=F32
        )
        ask = jnp.dot(slab[:, first : first + SPAN], residual, preferred_element_type=F32)
        if b:
            ent = totals[...] + ent
        if b < number - 1:
            totals[...] = ent
        else:
            ents[:, k * SPAN : (k + 1) * SPAN] = ent.T[:depth, :].astype(ents.dtype)
        if k:
            ask = asks[base + b] + ask
        elif stage > 1 or stage == 1 and b < 2:
            ask = before[base + b] + ask
        if stage == 3 and b:
            sent[1][...] = ask.astype(BF16)
        elif stage == 3:
            half = width // 2
            for out, at in ((sent[0], slice(0, half)), (sent[2], slice(half, width))):
                out[:, :half] = before[1, :, at].astype(BF16)
                out[:, half:] = ask[:, at].astype(BF16)
        else:
            asks[base + b] = ask

    steps = number * len(parts)
    residual_of(0)
    for step in range(steps):
        if step + 1 < steps:
            residual_of(step + 1)
        use(step)


def score(me, slab, blocks, parts, stage, total_entities, before=None):
    depth = slab.shape[0]
    plain = 1.0 - 2.0 * (0.1 / total_entities)
    shape = jax.ShapeDtypeStruct
    number = len(blocks)
    outs = [pltpu.VMEM((4 if stage else 2, depth, SPAN), F32)]
    if stage == 3:
        outs = [shape((depth, SPAN), F32)] + [shape((depth, SPAN), BF16)] * 3
    outs.append(shape((depth, len(parts) * SPAN), BF16 if stage == 1 else F32))
    scratch = [
        pltpu.VMEM((len(parts) * SPAN, WIDE), BF16),
        pltpu.VMEM((number, WIDE, SPAN), BF16),
        pltpu.VMEM((number, LANES, SPAN), jnp.int32),
        pltpu.VMEM((SPAN, WIDE), F32),
        pltpu.VMEM((SPAN, SPAN), BF16),
        pltpu.VMEM((SPAN, SPAN), BF16),
    ]
    whole = pl.BlockSpec(memory_space=pltpu.VMEM)
    given = [piece for block in blocks for piece in block] + ([before] if stage else [])
    return pl.pallas_call(
        functools.partial(
            score_kernel, plain, plain - 1.8, depth, parts, [len(b) for b in blocks], stage
        ),
        in_specs=[pl.BlockSpec(memory_space=pltpu.SMEM)] + [whole] * (1 + len(given)),
        out_specs=[whole] * len(outs),
        out_shape=outs,
        input_output_aliases={1 + len(given): 0} if stage == 2 else {},
        scratch_shapes=scratch,
        compiler_params=pltpu.CompilerParams(vmem_limit_bytes=VMEM_BYTES),
    )(me, slab, *given)


def body(
    anchor_ids,
    relation_ids,
    head_anchors,
    head_relations,
    query_relation,
    targets,
    anchor_table,
    relation_table,
    enc_weight,
    fc_weight,
):
    width = anchor_ids.shape[0]
    entities = width * 128
    queries = head_anchors.shape[0] * 128
    scale = 0.5 * float(anchor_table.shape[1]) ** (-0.5)
    me = (lax.axis_index("ent") * 16 + lax.axis_index("qry")).astype(jnp.int32)[None]
    ids = jnp.concatenate([anchor_ids.T.reshape(-1), head_anchors.T.reshape(-1)]) * 2
    own_cols, *shared = encode_entities(
        ids,
        anchor_ids.shape[1],
        relation_ids,
        anchor_table,
        relation_table,
        enc_weight,
        scale,
    )
    heads = (head_relations.T, query_relation[None, :], targets.T, fc_weight)
    sent = [moved(own_cols, dx=d) for d in FAR]
    early, own_cols, *shared = encode_heads(0, ids, *heads, own_cols, *shared)
    row = jnp.concatenate([own_cols] + sent, axis=1)
    first = [moved(early, dz=d) for d in (1, 2)]
    sent = [moved(row, dy=d) for d in FAR]
    late, row, query, *shared = encode_heads(1, ids, *heads, row, *shared, early)
    late, query, row, *first = lax.optimization_barrier((late, query, row, *first))
    slab = jnp.concatenate([row] + sent, axis=1)
    other = moved(slab, dcore=1)
    second = [moved(late, dz=d) for d in (1, 2)]
    asks, own_ents = score(me, slab, [[query], first], (0, 1, 2, 3), 0, entities)
    asks, own_ents, last, *second = lax.optimization_barrier(
        (asks, own_ents, moved(query, dz=3), *second)
    )
    blocks = [[query], first, second, [last]]
    asks, away = score(me, other, blocks, (0, 1, 2, 3), 1, entities, asks)
    back = moved(away, dcore=1)
    asks, ents = score(me, slab, blocks[2:], (1, 2, 3), 2, entities, asks)
    span = slab.shape[1] // 4

    def slab_sum(part, k):
        at = slice(k * span, (k + 1) * span)
        return part + own_ents[:, at] + back[:, at].astype(F32)

    ents = [ents[:, k * span : (k + 1) * span] for k in range(3)]
    ents = [slab_sum(part, k + 1).astype(BF16) for k, part in enumerate(ents)]
    ents = [moved(part, dy=-d) for d, part in zip(FAR, ents)]
    query_total, *sums, ent_row = score(me, slab, blocks[2:], (0,), 3, entities, asks)
    ent_row = slab_sum(ent_row, 0)
    for ent in ents:
        ent_row = ent_row + ent.astype(F32)
    for d, part in zip(FAR, sums):
        query_total = query_total + moved(part, dz=-d).astype(F32)
    ent_share = ent_row[:, :width]
    for k, d in enumerate(FAR):
        block = ent_row[:, (k + 1) * width : (k + 2) * width].astype(BF16)
        ent_share = ent_share + moved(block, dx=-d).astype(F32)
    return (
        ent_share * (0.5 / math.sqrt(queries)),
        query_total.T * (0.5 / scale / math.sqrt(entities)),
    )


def solution(mesh):
    spread = P(AXES, None)
    placed = (spread, spread, spread, spread, P(AXES), spread, P(), P(), P(), P())
    return jax.shard_map(
        body,
        mesh=mesh,
        in_specs=placed,
        out_specs=(P(None, AXES), spread),
        check_vma=False,
    )
```

```python
import functools
import math

import jax
import jax.numpy as jnp
from jax import lax
from jax.experimental import pallas as pl
from jax.experimental.pallas import tpu as pltpu
from jax.sharding import PartitionSpec as P

AXES = ("ent", "qry")
BF16 = jnp.bfloat16
F32 = jnp.float32
LANES = 128
WIDE = 256
CHUNK = 4096
UNROLL = 256
SPAN = 512
VMEM_BYTES = 12 * 1024 * 1024
CHUNKS = 2
FAR = (1, 3, 2)


def flat_of(x, y, z, core):
    return z * 32 + (x % 2) * 16 + y * 4 + (x // 2) * 2 + core


def coords_of(flat):
    x = ((flat // 2) % 2) * 2 + (flat // 16) % 2
    return x, (flat // 4) % 4, flat // 32, flat % 2


def moved(block, dx=0, dy=0, dz=0, dcore=0):
    route = []
    for to in range(128):
        x, y, z, core = coords_of(to)
        route.append((flat_of((x + dx) % 4, (y + dy) % 4, (z + dz) % 4, (core + dcore) % 2), to))
    return lax.ppermute(block, AXES, route)


def gather_rows(ids, table, rows, width, count, start, anchors):
    unroll = min(UNROLL, width)
    per = width // unroll

    def some(step, carry):
        first = step // per * count + start + step % per * unroll
        place = pl.multiple_of(step * (2 * unroll), 2 * unroll)
        picked = [table[pl.ds(ids[first + k], 2), :] for k in range(unroll)]
        for k in range(unroll):
            rows[pl.ds(place + 2 * k, 2), :] = picked[k]
        return carry

    lax.fori_loop(0, anchors * per, some, 0)


def relation_rows(ids, rel_table):
    shape = (rel_table.shape[1], ids.shape[1])
    hot = lax.broadcasted_iota(jnp.int32, shape, 0) == jnp.broadcast_to(ids, shape)
    hot = jnp.where(hot, 1.0, 0.0).astype(BF16)
    return jnp.dot(rel_table[...], hot, preferred_element_type=F32)


def encoded(rows, rel_ids, weights, rel_table):
    n_rel, width = rel_ids.shape
    anchors = weights.shape[1] // WIDE - n_rel
    total = jnp.zeros((weights.shape[0], width), F32)
    for t in range(anchors):
        halves = [rows[pl.ds(t * 2 * width + h, width, stride=2), :] for h in range(2)]
        part = jnp.concatenate(halves, axis=1).astype(BF16)
        total = total + lax.dot_general(
            weights[:, t * WIDE : (t + 1) * WIDE],
            part,
            (((1,), (1,)), ((), ())),
            preferred_element_type=F32,
        )
    for t in range(n_rel):
        part = relation_rows(rel_ids[t : t + 1, :], rel_table).astype(BF16)
        first = (anchors + t) * WIDE
        total = total + jnp.dot(weights[:, first : first + WIDE], part, preferred_element_type=F32)
    return total


def prepare(tab_t, w_t, rel_t, table, weights, rel_table, relations, steps):
    step = pl.program_id(0)
    depth = tab_t.shape[0]

    tokens = weights.shape[1] // WIDE
    share = pl.cdiv(tokens, steps)
    for turn in range(steps):

        @pl.when(step == turn)
        def _(turn=turn):
            lane = lax.broadcasted_iota(jnp.int32, (depth, WIDE), 1)
            for t in range(turn * share, min((turn + 1) * share, tokens)):
                start = t * depth
                base = start // LANES * LANES
                piece = w_t[:, base : base + 3 * LANES].astype(F32)
                if start > base:
                    piece = pltpu.roll(piece, 3 * LANES - (start - base), 1)
                weights[:, t * WIDE : (t + 1) * WIDE] = jnp.where(
                    lane < depth, piece[:, :WIDE], 0.0
                ).astype(BF16)

    @pl.when(step == 0)
    def _():
        known = lax.broadcasted_iota(jnp.int32, rel_t.shape, 1) < relations
        rel = jnp.where(known, rel_t[...].astype(F32), 0.0)
        rel_table[...] = jnp.concatenate(
            [rel, jnp.zeros((WIDE - depth, rel.shape[1]), F32)], axis=0
        ).astype(BF16)

    chunk = tab_t.shape[1]
    top = tab_t[:LANES, :].astype(F32).T
    rest = jnp.concatenate(
        [tab_t[LANES:, :].astype(F32), jnp.zeros((WIDE - depth, chunk), F32)], axis=0
    ).T
    table[pl.ds(step * 2 * chunk, chunk, stride=2), :] = top
    table[pl.ds(step * 2 * chunk + 1, chunk, stride=2), :] = rest


def entity_kernel(
    relations, steps, scale, own_ids, tab_t, w_t, rel_t, own_rel,
    own_out, table, weights, rel_table, rows,
):
    prepare(tab_t, w_t, rel_t, table, weights, rel_table, relations, steps)

    @pl.when(pl.program_id(0) == pl.num_programs(0) - 1)
    def _():
        width = own_rel.shape[1]
        anchors = weights.shape[1] // WIDE - own_rel.shape[0]
        gather_rows(own_ids, table, rows, width, width, 0, anchors)
        own_out[...] = (encoded(rows, own_rel, weights, rel_table) * scale).astype(BF16)


def head_kernel(
    start, width, head_ids, head_rel, asked, wanted, fc, echo, table, weights, rel_table, *refs
):
    rows = refs[-1]
    if start:
        earlier, query_out, echo_out, whole_out = refs[:4]
        whole_out[:, :start] = earlier[...]
    else:
        query_out, echo_out = refs[:2]
    echo_out[...] = echo[...]
    part = slice(start, start + width)
    tokens, heads = head_rel.shape
    anchors = weights.shape[1] // WIDE - tokens
    before = head_ids.shape[0] - anchors * heads
    gather_rows(head_ids, table, rows, width, heads, before + start, anchors)
    head = encoded(rows, head_rel[:, part], weights, rel_table).astype(BF16)
    mixed = head.astype(F32) * relation_rows(asked[:, part], rel_table)[: head.shape[0], :]
    query = jnp.tanh(
        lax.dot_general(
            fc[...], mixed.astype(BF16), (((0,), (0,)), ((), ())), preferred_element_type=F32
        )
    )
    digits = []
    for t in range(wanted.shape[0]):
        target = wanted[t : t + 1, part]
        digits += [target // LANES, target % LANES]
    query = jnp.concatenate(
        [query, jnp.concatenate(digits, axis=0).astype(F32)], axis=0
    ).astype(BF16)
    query_out[...] = query
    if start:
        whole_out[:, start:] = query


def encode_entities(ids, anchors, relation_ids, anchor_table, relation_table, enc_weight, scale):
    own = relation_ids.shape[0]
    count, depth = anchor_table.shape
    relations = relation_table.shape[0]
    steps = pl.cdiv(count, CHUNK)
    tokens = anchors + relation_ids.shape[1]
    rel_lanes = pl.cdiv(relations, LANES) * LANES
    w_lanes = pl.cdiv((tokens - 1) * depth // LANES * LANES + 3 * LANES, LANES) * LANES
    whole = pl.BlockSpec(memory_space=pltpu.VMEM)
    once = pl.Buffered(1)
    return pl.pallas_call(
        functools.partial(entity_kernel, relations, steps, scale),
        grid=(steps,),
        in_specs=[
            pl.BlockSpec(memory_space=pltpu.SMEM),
            pl.BlockSpec((depth, CHUNK), lambda i: (0, i)),
            pl.BlockSpec((depth, w_lanes), lambda i: (0, 0), pipeline_mode=once),
            pl.BlockSpec((depth, rel_lanes), lambda i: (0, 0), pipeline_mode=once),
            whole,
        ],
        out_specs=[whole] * 4,
        out_shape=[
            jax.ShapeDtypeStruct((depth, own), BF16),
            pltpu.VMEM((2 * steps * CHUNK, LANES), F32),
            pltpu.VMEM((depth, tokens * WIDE), BF16),
            pltpu.VMEM((WIDE, rel_lanes), BF16),
        ],
        scratch_shapes=[pltpu.VMEM((2 * own * anchors, LANES), F32)],
        compiler_params=pltpu.CompilerParams(vmem_limit_bytes=VMEM_BYTES),
    )(
        ids,
        pltpu.with_memory_space_constraint(anchor_table.T, pltpu.HBM),
        pltpu.with_memory_space_constraint(enc_weight.T, pltpu.HBM),
        pltpu.with_memory_space_constraint(relation_table.T, pltpu.HBM),
        relation_ids.T,
    )


def encode_heads(
    chunk, head_ids, head_relations, query_relation, targets, fc_weight, echo,
    table, weights, rel_table, *earlier,
):
    heads = head_relations.shape[1] // CHUNKS
    depth = fc_weight.shape[0]
    anchors = weights.shape[1] // WIDE - head_relations.shape[0]
    whole = pl.BlockSpec(memory_space=pltpu.VMEM)
    return pl.pallas_call(
        functools.partial(head_kernel, chunk * heads, heads),
        in_specs=[pl.BlockSpec(memory_space=pltpu.SMEM)] + [whole] * (8 + chunk),
        out_specs=[whole] * (5 + chunk),
        out_shape=[
            jax.ShapeDtypeStruct((depth + 2 * targets.shape[0], heads), BF16),
            jax.ShapeDtypeStruct(echo.shape, BF16),
            *[jax.ShapeDtypeStruct((depth + 2 * targets.shape[0], 2 * heads), BF16)] * chunk,
            pltpu.VMEM(table.shape, F32),
            pltpu.VMEM(weights.shape, BF16),
            pltpu.VMEM(rel_table.shape, BF16),
        ],
        input_output_aliases={6 + k: 2 + chunk + k for k in range(3)},
        scratch_shapes=[pltpu.VMEM((2 * heads * anchors, LANES), F32)],
        compiler_params=pltpu.CompilerParams(vmem_limit_bytes=VMEM_BYTES),
    )(
        head_ids, head_relations, query_relation, targets, fc_weight, echo,
        table, weights, rel_table, *earlier,
    )


def score_kernel(plain, struck_value, depth, parts, pieces, stage, me, slab, *refs):
    blocks = []
    for count in pieces:
        blocks.append(refs[:count])
        refs = refs[count:]
    before = None
    if stage:
        before, refs = refs[0], refs[1:]
    if stage == 3:
        kept, sent, refs = refs[0], refs[1:4], refs[4:]
        kept[...] = before[0]
    else:
        asks, refs = refs[0], refs[1:]
    ents, tall, queries, marks, totals, *held = refs
    if stage == 2:
        asks[:2] = before[:2]
    number = len(blocks)
    base = 2 if stage > 1 else 0
    width = SPAN
    tiles = SPAN // LANES

    x, y, z, core = coords_of(me[0])
    if stage == 1:
        core = 1 - core
    spots = [
        flat_of((x + dx) % 4, (y + ((0,) + FAR)[part]) % 4, z, core)
        for part in parts
        for dx in (0,) + FAR
    ]
    for k, part in enumerate(parts):
        wide = jnp.concatenate(
            [
                slab[:, part * SPAN : (part + 1) * SPAN].astype(F32),
                jnp.zeros((WIDE - depth, SPAN), F32),
            ],
            axis=0,
        )
        tall[k * SPAN : (k + 1) * SPAN, :] = wide.T.astype(BF16)
    within = lax.broadcasted_iota(jnp.int32, (LANES, width), 0)
    for b in range(number):
        query = jnp.concatenate([piece[...] for piece in blocks[b]], axis=1).astype(F32)
        queries[b] = jnp.concatenate(
            [query[:depth, :], jnp.zeros((WIDE - depth, width), F32)], axis=0
        ).astype(BF16)
        digits = query[depth:, :].astype(jnp.int32)
        marked = jnp.zeros((LANES, width), jnp.int32)
        for t in range(digits.shape[0] // 2):
            owner = digits[2 * t : 2 * t + 1, :]
            low = digits[2 * t + 1 : 2 * t + 2, :]
            bit = jnp.zeros(owner.shape, jnp.int32)
            for k, spot in enumerate(spots):
                bit = jnp.where(owner == spot, 1 << k, bit)
            marked = marked | jnp.where(within == low, bit, 0)
        marks[b] = marked

    def residual_of(step):
        k, b = step // number, step % number
        score = jnp.dot(
            tall[k * SPAN : (k + 1) * SPAN, :], queries[b], preferred_element_type=F32
        )
        marked = marks[b]
        for j in range(tiles):
            hit = (marked & (1 << (k * tiles + j))) != 0
            label = jnp.where(hit, struck_value, plain)
            at = slice(j * LANES, (j + 1) * LANES)
            held[step % 2][at, :] = (jnp.tanh(score[at, :]) + label).astype(BF16)

    def use(step):
        k, b = step // number, step % number
        first = parts[k] * SPAN
        residual = held[step % 2][...]
        ent = lax.dot_general(
            residual, queries[b], (((1,), (1,)), ((), ())), preferred_element_type=F32
        )
        ask = jnp.dot(slab[:, first : first + SPAN], residual, preferred_element_type=F32)
        if b:
            ent = totals[...] + ent
        if b < number - 1:
            totals[...] = ent
        else:
            ents[:, k * SPAN : (k + 1) * SPAN] = ent.T[:depth, :].astype(ents.dtype)
        if k:
            ask = asks[base + b] + ask
        elif stage > 1 or stage == 1 and b < 2:
            ask = before[base + b] + ask
        if stage == 3 and b:
            sent[1][...] = ask.astype(BF16)
        elif stage == 3:
            half = width // 2
            for out, at in ((sent[0], slice(0, half)), (sent[2], slice(half, width))):
                out[:, :half] = before[1, :, at].astype(BF16)
                out[:, half:] = ask[:, at].astype(BF16)
        else:
            asks[base + b] = ask

    steps = number * len(parts)
    residual_of(0)
    for step in range(steps):
        if step + 1 < steps:
            residual_of(step + 1)
        use(step)


def score(me, slab, blocks, parts, stage, total_entities, before=None):
    depth = slab.shape[0]
    plain = 1.0 - 2.0 * (0.1 / total_entities)
    shape = jax.ShapeDtypeStruct
    number = len(blocks)
    outs = [pltpu.VMEM((4 if stage else 2, depth, SPAN), F32)]
    if stage == 3:
        outs = [shape((depth, SPAN), F32)] + [shape((depth, SPAN), BF16)] * 3
    outs.append(shape((depth, len(parts) * SPAN), BF16 if stage == 1 else F32))
    scratch = [
        pltpu.VMEM((len(parts) * SPAN, WIDE), BF16),
        pltpu.VMEM((number, WIDE, SPAN), BF16),
        pltpu.VMEM((number, LANES, SPAN), jnp.int32),
        pltpu.VMEM((SPAN, WIDE), F32),
        pltpu.VMEM((SPAN, SPAN), BF16),
        pltpu.VMEM((SPAN, SPAN), BF16),
    ]
    whole = pl.BlockSpec(memory_space=pltpu.VMEM)
    given = [piece for block in blocks for piece in block] + ([before] if stage else [])
    return pl.pallas_call(
        functools.partial(
            score_kernel, plain, plain - 1.8, depth, parts, [len(b) for b in blocks], stage
        ),
        in_specs=[pl.BlockSpec(memory_space=pltpu.SMEM)] + [whole] * (1 + len(given)),
        out_specs=[whole] * len(outs),
        out_shape=outs,
        input_output_aliases={1 + len(given): 0} if stage == 2 else {},
        scratch_shapes=scratch,
        compiler_params=pltpu.CompilerParams(vmem_limit_bytes=VMEM_BYTES),
    )(me, slab, *given)


def body(
    anchor_ids,
    relation_ids,
    head_anchors,
    head_relations,
    query_relation,
    targets,
    anchor_table,
    relation_table,
    enc_weight,
    fc_weight,
):
    width = anchor_ids.shape[0]
    entities = width * 128
    queries = head_anchors.shape[0] * 128
    scale = 0.5 * float(anchor_table.shape[1]) ** (-0.5)
    me = (lax.axis_index("ent") * 16 + lax.axis_index("qry")).astype(jnp.int32)[None]
    ids = jnp.concatenate([anchor_ids.T.reshape(-1), head_anchors.T.reshape(-1)]) * 2
    own_cols, *shared = encode_entities(
        ids,
        anchor_ids.shape[1],
        relation_ids,
        anchor_table,
        relation_table,
        enc_weight,
        scale,
    )
    heads = (head_relations.T, query_relation[None, :], targets.T, fc_weight)
    sent = [moved(own_cols, dx=d) for d in FAR]
    early, own_cols, *shared = encode_heads(0, ids, *heads, own_cols, *shared)
    row = jnp.concatenate([own_cols] + sent, axis=1)
    first = [moved(early, dz=d) for d in (1, 2)]
    sent = [moved(row, dy=d) for d in FAR]
    late, row, query, *shared = encode_heads(1, ids, *heads, row, *shared, early)
    late, query, row, *first = lax.optimization_barrier((late, query, row, *first))
    slab = jnp.concatenate([row] + sent, axis=1)
    other = moved(slab, dcore=1)
    second = [moved(late, dz=d) for d in (1, 2)]
    asks, own_ents = score(me, slab, [[query], first], (0, 1, 2, 3), 0, entities)
    asks, own_ents, last, *second = lax.optimization_barrier(
        (asks, own_ents, moved(query, dz=3), *second)
    )
    blocks = [[query], first, second, [last]]
    asks, away = score(me, other, blocks, (0, 1, 2, 3), 1, entities, asks)
    back = moved(away, dcore=1)
    asks, ents = score(me, slab, blocks[2:], (1, 2, 3), 2, entities, asks)
    span = slab.shape[1] // 4

    def slab_sum(part, k):
        at = slice(k * span, (k + 1) * span)
        return part + own_ents[:, at] + back[:, at].astype(F32)

    ents = [ents[:, k * span : (k + 1) * span] for k in range(3)]
    ents = [slab_sum(part, k + 1).astype(BF16) for k, part in enumerate(ents)]
    ents = [moved(part, dy=-d) for d, part in zip(FAR, ents)]
    query_total, *sums, ent_row = score(me, slab, blocks[2:], (0,), 3, entities, asks)
    ent_row = slab_sum(ent_row, 0)
    for ent in ents:
        ent_row = ent_row + ent.astype(F32)
    for d, part in zip(FAR, sums):
        query_total = query_total + moved(part, dz=-d).astype(F32)
    ent_share = ent_row[:, :width]
    for k, d in enumerate(FAR):
        block = ent_row[:, (k + 1) * width : (k + 2) * width].astype(BF16)
        ent_share = ent_share + moved(block, dx=-d).astype(F32)
    return (
        ent_share * (0.5 / math.sqrt(queries)),
        query_total.T * (0.5 / scale / math.sqrt(entities)),
    )


def solution(mesh):
    spread = P(AXES, None)
    placed = (spread, spread, spread, spread, P(AXES), spread, P(), P(), P(), P())
    return jax.shard_map(
        body,
        mesh=mesh,
        in_specs=placed,
        out_specs=(P(None, AXES), spread),
        check_vma=False,
    )
```

```python
import functools
import math

import jax
import jax.numpy as jnp
from jax import lax
from jax.experimental import pallas as pl
from jax.experimental.pallas import tpu as pltpu
from jax.sharding import PartitionSpec as P

AXES = ("ent", "qry")
BF16 = jnp.bfloat16
F32 = jnp.float32
LANES = 128
WIDE = 256
CHUNK = 5120
UNROLL = 256
SPAN = 512
VMEM_BYTES = 12 * 1024 * 1024
CHUNKS = 2
FAR = (1, 3, 2)


def flat_of(x, y, z, core):
    return z * 32 + (x % 2) * 16 + y * 4 + (x // 2) * 2 + core


def coords_of(flat):
    x = ((flat // 2) % 2) * 2 + (flat // 16) % 2
    return x, (flat // 4) % 4, flat // 32, flat % 2


def moved(block, dx=0, dy=0, dz=0, dcore=0):
    route = []
    for to in range(128):
        x, y, z, core = coords_of(to)
        route.append((flat_of((x + dx) % 4, (y + dy) % 4, (z + dz) % 4, (core + dcore) % 2), to))
    return lax.ppermute(block, AXES, route)


def gather_rows(ids, table, rows, width, count, start, anchors):
    unroll = min(UNROLL, width)
    per = width // unroll

    def some(step, carry):
        first = step // per * count + start + step % per * unroll
        place = pl.multiple_of(step * (2 * unroll), 2 * unroll)
        picked = [table[pl.ds(ids[first + k], 2), :] for k in range(unroll)]
        for k in range(unroll):
            rows[pl.ds(place + 2 * k, 2), :] = picked[k]
        return carry

    lax.fori_loop(0, anchors * per, some, 0)


def relation_rows(ids, rel_table):
    shape = (rel_table.shape[1], ids.shape[1])
    hot = lax.broadcasted_iota(jnp.int32, shape, 0) == jnp.broadcast_to(ids, shape)
    hot = jnp.where(hot, 1.0, 0.0).astype(BF16)
    return jnp.dot(rel_table[...], hot, preferred_element_type=F32)


def encoded(rows, rel_ids, weights, rel_table):
    n_rel, width = rel_ids.shape
    anchors = weights.shape[1] // WIDE - n_rel
    total = jnp.zeros((weights.shape[0], width), F32)
    for t in range(anchors):
        halves = [rows[pl.ds(t * 2 * width + h, width, stride=2), :] for h in range(2)]
        part = jnp.concatenate(halves, axis=1).astype(BF16)
        total = total + lax.dot_general(
            weights[:, t * WIDE : (t + 1) * WIDE],
            part,
            (((1,), (1,)), ((), ())),
            preferred_element_type=F32,
        )
    for t in range(n_rel):
        part = relation_rows(rel_ids[t : t + 1, :], rel_table).astype(BF16)
        first = (anchors + t) * WIDE
        total = total + jnp.dot(weights[:, first : first + WIDE], part, preferred_element_type=F32)
    return total


def prepare(tab_t, w_t, rel_t, table, weights, rel_table, relations, steps):
    step = pl.program_id(0)
    depth = tab_t.shape[0]

    tokens = weights.shape[1] // WIDE
    share = pl.cdiv(tokens, steps)
    for turn in range(steps):

        @pl.when(step == turn)
        def _(turn=turn):
            lane = lax.broadcasted_iota(jnp.int32, (depth, WIDE), 1)
            for t in range(turn * share, min((turn + 1) * share, tokens)):
                start = t * depth
                base = start // LANES * LANES
                piece = w_t[:, base : base + 3 * LANES].astype(F32)
                if start > base:
                    piece = pltpu.roll(piece, 3 * LANES - (start - base), 1)
                weights[:, t * WIDE : (t + 1) * WIDE] = jnp.where(
                    lane < depth, piece[:, :WIDE], 0.0
                ).astype(BF16)

    @pl.when(step == 0)
    def _():
        known = lax.broadcasted_iota(jnp.int32, rel_t.shape, 1) < relations
        rel = jnp.where(known, rel_t[...].astype(F32), 0.0)
        rel_table[...] = jnp.concatenate(
            [rel, jnp.zeros((WIDE - depth, rel.shape[1]), F32)], axis=0
        ).astype(BF16)

    chunk = tab_t.shape[1]
    top = tab_t[:LANES, :].astype(F32).T
    rest = jnp.concatenate(
        [tab_t[LANES:, :].astype(F32), jnp.zeros((WIDE - depth, chunk), F32)], axis=0
    ).T
    table[pl.ds(step * 2 * chunk, chunk, stride=2), :] = top
    table[pl.ds(step * 2 * chunk + 1, chunk, stride=2), :] = rest


def entity_kernel(
    relations, steps, scale, own_ids, tab_t, w_t, rel_t, own_rel,
    own_out, table, weights, rel_table, rows,
):
    prepare(tab_t, w_t, rel_t, table, weights, rel_table, relations, steps)

    @pl.when(pl.program_id(0) == pl.num_programs(0) - 1)
    def _():
        width = own_rel.shape[1]
        anchors = weights.shape[1] // WIDE - own_rel.shape[0]
        gather_rows(own_ids, table, rows, width, width, 0, anchors)
        own_out[...] = (encoded(rows, own_rel, weights, rel_table) * scale).astype(BF16)


def head_kernel(
    start, width, head_ids, head_rel, asked, wanted, fc, echo, table, weights, rel_table, *refs
):
    rows = refs[-1]
    if start:
        earlier, query_out, echo_out, whole_out = refs[:4]
        whole_out[:, :start] = earlier[...]
    else:
        query_out, echo_out = refs[:2]
    echo_out[...] = echo[...]
    part = slice(start, start + width)
    tokens, heads = head_rel.shape
    anchors = weights.shape[1] // WIDE - tokens
    before = head_ids.shape[0] - anchors * heads
    gather_rows(head_ids, table, rows, width, heads, before + start, anchors)
    head = encoded(rows, head_rel[:, part], weights, rel_table).astype(BF16)
    mixed = head.astype(F32) * relation_rows(asked[:, part], rel_table)[: head.shape[0], :]
    query = jnp.tanh(
        lax.dot_general(
            fc[...], mixed.astype(BF16), (((0,), (0,)), ((), ())), preferred_element_type=F32
        )
    )
    digits = []
    for t in range(wanted.shape[0]):
        target = wanted[t : t + 1, part]
        digits += [target // LANES, target % LANES]
    query = jnp.concatenate(
        [query, jnp.concatenate(digits, axis=0).astype(F32)], axis=0
    ).astype(BF16)
    query_out[...] = query
    if start:
        whole_out[:, start:] = query


def encode_entities(ids, anchors, relation_ids, anchor_table, relation_table, enc_weight, scale):
    own = relation_ids.shape[0]
    count, depth = anchor_table.shape
    relations = relation_table.shape[0]
    steps = pl.cdiv(count, CHUNK)
    tokens = anchors + relation_ids.shape[1]
    rel_lanes = pl.cdiv(relations, LANES) * LANES
    w_lanes = pl.cdiv((tokens - 1) * depth // LANES * LANES + 3 * LANES, LANES) * LANES
    whole = pl.BlockSpec(memory_space=pltpu.VMEM)
    once = pl.Buffered(1)
    return pl.pallas_call(
        functools.partial(entity_kernel, relations, steps, scale),
        grid=(steps,),
        in_specs=[
            pl.BlockSpec(memory_space=pltpu.SMEM),
            pl.BlockSpec((depth, CHUNK), lambda i: (0, i)),
            pl.BlockSpec((depth, w_lanes), lambda i: (0, 0), pipeline_mode=once),
            pl.BlockSpec((depth, rel_lanes), lambda i: (0, 0), pipeline_mode=once),
            whole,
        ],
        out_specs=[whole] * 4,
        out_shape=[
            jax.ShapeDtypeStruct((depth, own), BF16),
            pltpu.VMEM((2 * steps * CHUNK, LANES), F32),
            pltpu.VMEM((depth, tokens * WIDE), BF16),
            pltpu.VMEM((WIDE, rel_lanes), BF16),
        ],
        scratch_shapes=[pltpu.VMEM((2 * own * anchors, LANES), F32)],
        compiler_params=pltpu.CompilerParams(vmem_limit_bytes=VMEM_BYTES),
    )(
        ids,
        pltpu.with_memory_space_constraint(anchor_table.T, pltpu.HBM),
        pltpu.with_memory_space_constraint(enc_weight.T, pltpu.HBM),
        pltpu.with_memory_space_constraint(relation_table.T, pltpu.HBM),
        relation_ids.T,
    )


def encode_heads(
    chunk, head_ids, head_relations, query_relation, targets, fc_weight, echo,
    table, weights, rel_table, *earlier,
):
    heads = head_relations.shape[1] // CHUNKS
    depth = fc_weight.shape[0]
    anchors = weights.shape[1] // WIDE - head_relations.shape[0]
    whole = pl.BlockSpec(memory_space=pltpu.VMEM)
    return pl.pallas_call(
        functools.partial(head_kernel, chunk * heads, heads),
        in_specs=[pl.BlockSpec(memory_space=pltpu.SMEM)] + [whole] * (8 + chunk),
        out_specs=[whole] * (5 + chunk),
        out_shape=[
            jax.ShapeDtypeStruct((depth + 2 * targets.shape[0], heads), BF16),
            jax.ShapeDtypeStruct(echo.shape, BF16),
            *[jax.ShapeDtypeStruct((depth + 2 * targets.shape[0], 2 * heads), BF16)] * chunk,
            pltpu.VMEM(table.shape, F32),
            pltpu.VMEM(weights.shape, BF16),
            pltpu.VMEM(rel_table.shape, BF16),
        ],
        input_output_aliases={6 + k: 2 + chunk + k for k in range(3)},
        scratch_shapes=[pltpu.VMEM((2 * heads * anchors, LANES), F32)],
        compiler_params=pltpu.CompilerParams(vmem_limit_bytes=VMEM_BYTES),
    )(
        head_ids, head_relations, query_relation, targets, fc_weight, echo,
        table, weights, rel_table, *earlier,
    )


def score_kernel(plain, struck_value, depth, parts, pieces, stage, me, slab, *refs):
    blocks = []
    for count in pieces:
        blocks.append(refs[:count])
        refs = refs[count:]
    before = None
    if stage:
        before, refs = refs[0], refs[1:]
    if stage == 3:
        kept, sent, refs = refs[0], refs[1:4], refs[4:]
        kept[...] = before[0]
    else:
        asks, refs = refs[0], refs[1:]
    ents, tall, queries, marks, totals, *held = refs
    if stage == 2:
        asks[:2] = before[:2]
    number = len(blocks)
    base = 2 if stage > 1 else 0
    width = SPAN
    tiles = SPAN // LANES

    x, y, z, core = coords_of(me[0])
    if stage == 1:
        core = 1 - core
    spots = [
        flat_of((x + dx) % 4, (y + ((0,) + FAR)[part]) % 4, z, core)
        for part in parts
        for dx in (0,) + FAR
    ]
    for k, part in enumerate(parts):
        wide = jnp.concatenate(
            [
                slab[:, part * SPAN : (part + 1) * SPAN].astype(F32),
                jnp.zeros((WIDE - depth, SPAN), F32),
            ],
            axis=0,
        )
        tall[k * SPAN : (k + 1) * SPAN, :] = wide.T.astype(BF16)
    within = lax.broadcasted_iota(jnp.int32, (LANES, width), 0)
    for b in range(number):
        query = jnp.concatenate([piece[...] for piece in blocks[b]], axis=1).astype(F32)
        queries[b] = jnp.concatenate(
            [query[:depth, :], jnp.zeros((WIDE - depth, width), F32)], axis=0
        ).astype(BF16)
        digits = query[depth:, :].astype(jnp.int32)
        marked = jnp.zeros((LANES, width), jnp.int32)
        for t in range(digits.shape[0] // 2):
            owner = digits[2 * t : 2 * t + 1, :]
            low = digits[2 * t + 1 : 2 * t + 2, :]
            bit = jnp.zeros(owner.shape, jnp.int32)
            for k, spot in enumerate(spots):
                bit = jnp.where(owner == spot, 1 << k, bit)
            marked = marked | jnp.where(within == low, bit, 0)
        marks[b] = marked

    def residual_of(step):
        k, b = step // number, step % number
        score = jnp.dot(
            tall[k * SPAN : (k + 1) * SPAN, :], queries[b], preferred_element_type=F32
        )
        marked = marks[b]
        for j in range(tiles):
            hit = (marked & (1 << (k * tiles + j))) != 0
            label = jnp.where(hit, struck_value, plain)
            at = slice(j * LANES, (j + 1) * LANES)
            held[step % 2][at, :] = (jnp.tanh(score[at, :]) + label).astype(BF16)

    def use(step):
        k, b = step // number, step % number
        first = parts[k] * SPAN
        residual = held[step % 2][...]
        ent = lax.dot_general(
            residual, queries[b], (((1,), (1,)), ((), ())), preferred_element_type=F32
        )
        ask = jnp.dot(slab[:, first : first + SPAN], residual, preferred_element_type=F32)
        if b:
            ent = totals[...] + ent
        if b < number - 1:
            totals[...] = ent
        else:
            ents[:, k * SPAN : (k + 1) * SPAN] = ent.T[:depth, :].astype(ents.dtype)
        if k:
            ask = asks[base + b] + ask
        elif stage > 1 or stage == 1 and b < 2:
            ask = before[base + b] + ask
        if stage == 3 and b:
            sent[1][...] = ask.astype(BF16)
        elif stage == 3:
            half = width // 2
            for out, at in ((sent[0], slice(0, half)), (sent[2], slice(half, width))):
                out[:, :half] = before[1, :, at].astype(BF16)
                out[:, half:] = ask[:, at].astype(BF16)
        else:
            asks[base + b] = ask

    steps = number * len(parts)
    residual_of(0)
    for step in range(steps):
        if step + 1 < steps:
            residual_of(step + 1)
        use(step)


def score(me, slab, blocks, parts, stage, total_entities, before=None):
    depth = slab.shape[0]
    plain = 1.0 - 2.0 * (0.1 / total_entities)
    shape = jax.ShapeDtypeStruct
    number = len(blocks)
    outs = [pltpu.VMEM((4 if stage else 2, depth, SPAN), F32)]
    if stage == 3:
        outs = [shape((depth, SPAN), F32)] + [shape((depth, SPAN), BF16)] * 3
    outs.append(shape((depth, len(parts) * SPAN), BF16 if stage == 1 else F32))
    scratch = [
        pltpu.VMEM((len(parts) * SPAN, WIDE), BF16),
        pltpu.VMEM((number, WIDE, SPAN), BF16),
        pltpu.VMEM((number, LANES, SPAN), jnp.int32),
        pltpu.VMEM((SPAN, WIDE), F32),
        pltpu.VMEM((SPAN, SPAN), BF16),
        pltpu.VMEM((SPAN, SPAN), BF16),
    ]
    whole = pl.BlockSpec(memory_space=pltpu.VMEM)
    given = [piece for block in blocks for piece in block] + ([before] if stage else [])
    return pl.pallas_call(
        functools.partial(
            score_kernel, plain, plain - 1.8, depth, parts, [len(b) for b in blocks], stage
        ),
        in_specs=[pl.BlockSpec(memory_space=pltpu.SMEM)] + [whole] * (1 + len(given)),
        out_specs=[whole] * len(outs),
        out_shape=outs,
        input_output_aliases={1 + len(given): 0} if stage == 2 else {},
        scratch_shapes=scratch,
        compiler_params=pltpu.CompilerParams(vmem_limit_bytes=VMEM_BYTES),
    )(me, slab, *given)


def body(
    anchor_ids,
    relation_ids,
    head_anchors,
    head_relations,
    query_relation,
    targets,
    anchor_table,
    relation_table,
    enc_weight,
    fc_weight,
):
    width = anchor_ids.shape[0]
    entities = width * 128
    queries = head_anchors.shape[0] * 128
    scale = 0.5 * float(anchor_table.shape[1]) ** (-0.5)
    me = (lax.axis_index("ent") * 16 + lax.axis_index("qry")).astype(jnp.int32)[None]
    ids = jnp.concatenate([anchor_ids.T.reshape(-1), head_anchors.T.reshape(-1)]) * 2
    own_cols, *shared = encode_entities(
        ids,
        anchor_ids.shape[1],
        relation_ids,
        anchor_table,
        relation_table,
        enc_weight,
        scale,
    )
    heads = (head_relations.T, query_relation[None, :], targets.T, fc_weight)
    sent = [moved(own_cols, dx=d) for d in FAR]
    early, own_cols, *shared = encode_heads(0, ids, *heads, own_cols, *shared)
    row = jnp.concatenate([own_cols] + sent, axis=1)
    first = [moved(early, dz=d) for d in (1, 2)]
    sent = [moved(row, dy=d) for d in FAR]
    late, row, query, *shared = encode_heads(1, ids, *heads, row, *shared, early)
    late, query, row, *first = lax.optimization_barrier((late, query, row, *first))
    slab = jnp.concatenate([row] + sent, axis=1)
    other = moved(slab, dcore=1)
    second = [moved(late, dz=d) for d in (1, 2)]
    asks, own_ents = score(me, slab, [[query], first], (0, 1, 2, 3), 0, entities)
    asks, own_ents, last, *second = lax.optimization_barrier(
        (asks, own_ents, moved(query, dz=3), *second)
    )
    blocks = [[query], first, second, [last]]
    asks, away = score(me, other, blocks, (0, 1, 2, 3), 1, entities, asks)
    back = moved(away, dcore=1)
    asks, ents = score(me, slab, blocks[2:], (1, 2, 3), 2, entities, asks)
    span = slab.shape[1] // 4

    def slab_sum(part, k):
        at = slice(k * span, (k + 1) * span)
        return part + own_ents[:, at] + back[:, at].astype(F32)

    ents = [ents[:, k * span : (k + 1) * span] for k in range(3)]
    ents = [slab_sum(part, k + 1).astype(BF16) for k, part in enumerate(ents)]
    ents = [moved(part, dy=-d) for d, part in zip((3, 1, 2), (ents[1], ents[0], ents[2]))]
    query_total, *sums, ent_row = score(me, slab, blocks[2:], (0,), 3, entities, asks)
    ent_row = slab_sum(ent_row, 0)
    for ent in ents:
        ent_row = ent_row + ent.astype(F32)
    for d, part in zip((1, 2, 3), (sums[0], sums[2], sums[1])):
        query_total = query_total + moved(part, dz=-d).astype(F32)
    ent_share = ent_row[:, :width]
    for k, d in enumerate(FAR):
        block = ent_row[:, (k + 1) * width : (k + 2) * width].astype(BF16)
        ent_share = ent_share + moved(block, dx=-d).astype(F32)
    return (
        ent_share * (0.5 / math.sqrt(queries)),
        query_total.T * (0.5 / scale / math.sqrt(entities)),
    )


def solution(mesh):
    spread = P(AXES, None)
    placed = (spread, spread, spread, spread, P(AXES), spread, P(), P(), P(), P())
    return jax.shard_map(
        body,
        mesh=mesh,
        in_specs=placed,
        out_specs=(P(None, AXES), spread),
        check_vma=False,
    )
```

```python
import functools
import math

import jax
import jax.numpy as jnp
from jax import lax
from jax.experimental import pallas as pl
from jax.experimental.pallas import tpu as pltpu
from jax.sharding import PartitionSpec as P

AXES = ("ent", "qry")
BF16 = jnp.bfloat16
F32 = jnp.float32
LANES = 128
WIDE = 256
CHUNK = 5120
UNROLL = 256
SPAN = 512
VMEM_BYTES = 12 * 1024 * 1024
CHUNKS = 2
FAR = (1, 3, 2)


def flat_of(x, y, z, core):
    return z * 32 + (x % 2) * 16 + y * 4 + (x // 2) * 2 + core


def coords_of(flat):
    x = ((flat // 2) % 2) * 2 + (flat // 16) % 2
    return x, (flat // 4) % 4, flat // 32, flat % 2


def moved(block, dx=0, dy=0, dz=0, dcore=0):
    route = []
    for to in range(128):
        x, y, z, core = coords_of(to)
        route.append((flat_of((x + dx) % 4, (y + dy) % 4, (z + dz) % 4, (core + dcore) % 2), to))
    return lax.ppermute(block, AXES, route)


def gather_rows(ids, table, rows, width, count, start, anchors):
    unroll = min(UNROLL, width)
    per = width // unroll

    def some(step, carry):
        first = step // per * count + start + step % per * unroll
        place = pl.multiple_of(step * (2 * unroll), 2 * unroll)
        picked = [table[pl.ds(ids[first + k], 2), :] for k in range(unroll)]
        for k in range(unroll):
            rows[pl.ds(place + 2 * k, 2), :] = picked[k]
        return carry

    lax.fori_loop(0, anchors * per, some, 0)


def relation_rows(ids, rel_table):
    shape = (rel_table.shape[1], ids.shape[1])
    hot = lax.broadcasted_iota(jnp.int32, shape, 0) == jnp.broadcast_to(ids, shape)
    hot = jnp.where(hot, 1.0, 0.0).astype(BF16)
    return jnp.dot(rel_table[...], hot, preferred_element_type=F32)


def encoded(rows, rel_ids, weights, rel_table):
    n_rel, width = rel_ids.shape
    anchors = weights.shape[1] // WIDE - n_rel
    total = jnp.zeros((weights.shape[0], width), F32)
    for t in range(anchors):
        halves = [rows[pl.ds(t * 2 * width + h, width, stride=2), :] for h in range(2)]
        part = jnp.concatenate(halves, axis=1).astype(BF16)
        total = total + lax.dot_general(
            weights[:, t * WIDE : (t + 1) * WIDE],
            part,
            (((1,), (1,)), ((), ())),
            preferred_element_type=F32,
        )
    for t in range(n_rel):
        part = relation_rows(rel_ids[t : t + 1, :], rel_table).astype(BF16)
        first = (anchors + t) * WIDE
        total = total + jnp.dot(weights[:, first : first + WIDE], part, preferred_element_type=F32)
    return total


def prepare(tab_t, w_t, rel_t, table, weights, rel_table, relations, steps):
    step = pl.program_id(0)
    depth = tab_t.shape[0]

    tokens = weights.shape[1] // WIDE
    share = pl.cdiv(tokens, steps)
    for turn in range(steps):

        @pl.when(step == turn)
        def _(turn=turn):
            lane = lax.broadcasted_iota(jnp.int32, (depth, WIDE), 1)
            for t in range(turn * share, min((turn + 1) * share, tokens)):
                start = t * depth
                base = start // LANES * LANES
                piece = w_t[:, base : base + 3 * LANES].astype(F32)
                if start > base:
                    piece = pltpu.roll(piece, 3 * LANES - (start - base), 1)
                weights[:, t * WIDE : (t + 1) * WIDE] = jnp.where(
                    lane < depth, piece[:, :WIDE], 0.0
                ).astype(BF16)

    @pl.when(step == 0)
    def _():
        known = lax.broadcasted_iota(jnp.int32, rel_t.shape, 1) < relations
        rel = jnp.where(known, rel_t[...].astype(F32), 0.0)
        rel_table[...] = jnp.concatenate(
            [rel, jnp.zeros((WIDE - depth, rel.shape[1]), F32)], axis=0
        ).astype(BF16)

    chunk = tab_t.shape[1]
    top = tab_t[:LANES, :].astype(F32).T
    rest = jnp.concatenate(
        [tab_t[LANES:, :].astype(F32), jnp.zeros((WIDE - depth, chunk), F32)], axis=0
    ).T
    table[pl.ds(step * 2 * chunk, chunk, stride=2), :] = top
    table[pl.ds(step * 2 * chunk + 1, chunk, stride=2), :] = rest


def entity_kernel(
    relations, steps, scale, own_ids, tab_t, w_t, rel_t, own_rel,
    own_out, table, weights, rel_table, rows,
):
    prepare(tab_t, w_t, rel_t, table, weights, rel_table, relations, steps)

    @pl.when(pl.program_id(0) == pl.num_programs(0) - 1)
    def _():
        width = own_rel.shape[1]
        anchors = weights.shape[1] // WIDE - own_rel.shape[0]
        gather_rows(own_ids, table, rows, width, width, 0, anchors)
        own_out[...] = (encoded(rows, own_rel, weights, rel_table) * scale).astype(BF16)


def head_kernel(
    start, width, head_ids, head_rel, asked, wanted, fc, echo, table, weights, rel_table, *refs
):
    rows = refs[-1]
    if start:
        earlier, query_out, echo_out, whole_out = refs[:4]
        whole_out[:, :start] = earlier[...]
    else:
        query_out, echo_out = refs[:2]
    echo_out[...] = echo[...]
    part = slice(start, start + width)
    tokens, heads = head_rel.shape
    anchors = weights.shape[1] // WIDE - tokens
    before = head_ids.shape[0] - anchors * heads
    gather_rows(head_ids, table, rows, width, heads, before + start, anchors)
    head = encoded(rows, head_rel[:, part], weights, rel_table).astype(BF16)
    mixed = head.astype(F32) * relation_rows(asked[:, part], rel_table)[: head.shape[0], :]
    query = jnp.tanh(
        lax.dot_general(
            fc[...], mixed.astype(BF16), (((0,), (0,)), ((), ())), preferred_element_type=F32
        )
    )
    digits = []
    for t in range(wanted.shape[0]):
        target = wanted[t : t + 1, part]
        digits += [target // LANES, target % LANES]
    query = jnp.concatenate(
        [query, jnp.concatenate(digits, axis=0).astype(F32)], axis=0
    ).astype(BF16)
    query_out[...] = query
    if start:
        whole_out[:, start:] = query


def encode_entities(ids, anchors, relation_ids, anchor_table, relation_table, enc_weight, scale):
    own = relation_ids.shape[0]
    count, depth = anchor_table.shape
    relations = relation_table.shape[0]
    steps = pl.cdiv(count, CHUNK)
    tokens = anchors + relation_ids.shape[1]
    rel_lanes = pl.cdiv(relations, LANES) * LANES
    w_lanes = pl.cdiv((tokens - 1) * depth // LANES * LANES + 3 * LANES, LANES) * LANES
    whole = pl.BlockSpec(memory_space=pltpu.VMEM)
    once = pl.Buffered(1)
    return pl.pallas_call(
        functools.partial(entity_kernel, relations, steps, scale),
        grid=(steps,),
        in_specs=[
            pl.BlockSpec(memory_space=pltpu.SMEM),
            pl.BlockSpec((depth, CHUNK), lambda i: (0, i)),
            pl.BlockSpec((depth, w_lanes), lambda i: (0, 0), pipeline_mode=once),
            pl.BlockSpec((depth, rel_lanes), lambda i: (0, 0), pipeline_mode=once),
            whole,
        ],
        out_specs=[whole] * 4,
        out_shape=[
            jax.ShapeDtypeStruct((depth, own), BF16),
            pltpu.VMEM((2 * steps * CHUNK, LANES), F32),
            pltpu.VMEM((depth, tokens * WIDE), BF16),
            pltpu.VMEM((WIDE, rel_lanes), BF16),
        ],
        scratch_shapes=[pltpu.VMEM((2 * own * anchors, LANES), F32)],
        compiler_params=pltpu.CompilerParams(vmem_limit_bytes=VMEM_BYTES),
    )(
        ids,
        pltpu.with_memory_space_constraint(anchor_table.T, pltpu.HBM),
        pltpu.with_memory_space_constraint(enc_weight.T, pltpu.HBM),
        pltpu.with_memory_space_constraint(relation_table.T, pltpu.HBM),
        relation_ids.T,
    )


def encode_heads(
    chunk, head_ids, head_relations, query_relation, targets, fc_weight, echo,
    table, weights, rel_table, *earlier,
):
    heads = head_relations.shape[1] // CHUNKS
    depth = fc_weight.shape[0]
    anchors = weights.shape[1] // WIDE - head_relations.shape[0]
    whole = pl.BlockSpec(memory_space=pltpu.VMEM)
    return pl.pallas_call(
        functools.partial(head_kernel, chunk * heads, heads),
        in_specs=[pl.BlockSpec(memory_space=pltpu.SMEM)] + [whole] * (8 + chunk),
        out_specs=[whole] * (5 + chunk),
        out_shape=[
            jax.ShapeDtypeStruct((depth + 2 * targets.shape[0], heads), BF16),
            jax.ShapeDtypeStruct(echo.shape, BF16),
            *[jax.ShapeDtypeStruct((depth + 2 * targets.shape[0], 2 * heads), BF16)] * chunk,
            pltpu.VMEM(table.shape, F32),
            pltpu.VMEM(weights.shape, BF16),
            pltpu.VMEM(rel_table.shape, BF16),
        ],
        input_output_aliases={6 + k: 2 + chunk + k for k in range(3)},
        scratch_shapes=[pltpu.VMEM((2 * heads * anchors, LANES), F32)],
        compiler_params=pltpu.CompilerParams(vmem_limit_bytes=VMEM_BYTES),
    )(
        head_ids, head_relations, query_relation, targets, fc_weight, echo,
        table, weights, rel_table, *earlier,
    )


def score_kernel(plain, struck_value, depth, parts, pieces, stage, me, slab, *refs):
    blocks = []
    for count in pieces:
        blocks.append(refs[:count])
        refs = refs[count:]
    before = None
    if stage:
        before, refs = refs[0], refs[1:]
    if stage == 3:
        kept, sent, refs = refs[0], refs[1:4], refs[4:]
        kept[...] = before[0]
    else:
        asks, refs = refs[0], refs[1:]
    ents, tall, queries, marks, totals, *held = refs
    if stage == 2:
        asks[:2] = before[:2]
    number = len(blocks)
    base = 2 if stage > 1 else 0
    width = SPAN
    tiles = SPAN // LANES

    x, y, z, core = coords_of(me[0])
    if stage == 1:
        core = 1 - core
    spots = [
        flat_of((x + dx) % 4, (y + ((0,) + FAR)[part]) % 4, z, core)
        for part in parts
        for dx in (0,) + FAR
    ]
    for k, part in enumerate(parts):
        wide = jnp.concatenate(
            [
                slab[:, part * SPAN : (part + 1) * SPAN].astype(F32),
                jnp.zeros((WIDE - depth, SPAN), F32),
            ],
            axis=0,
        )
        tall[k * SPAN : (k + 1) * SPAN, :] = wide.T.astype(BF16)
    within = lax.broadcasted_iota(jnp.int32, (LANES, width), 0)
    for b in range(number):
        query = jnp.concatenate([piece[...] for piece in blocks[b]], axis=1).astype(F32)
        queries[b] = jnp.concatenate(
            [query[:depth, :], jnp.zeros((WIDE - depth, width), F32)], axis=0
        ).astype(BF16)
        digits = query[depth:, :].astype(jnp.int32)
        marked = jnp.zeros((LANES, width), jnp.int32)
        for t in range(digits.shape[0] // 2):
            owner = digits[2 * t : 2 * t + 1, :]
            low = digits[2 * t + 1 : 2 * t + 2, :]
            bit = jnp.zeros(owner.shape, jnp.int32)
            for k, spot in enumerate(spots):
                bit = jnp.where(owner == spot, 1 << k, bit)
            marked = marked | jnp.where(within == low, bit, 0)
        marks[b] = marked

    def residual_of(step):
        k, b = step // number, step % number
        score = jnp.dot(
            tall[k * SPAN : (k + 1) * SPAN, :], queries[b], preferred_element_type=F32
        )
        marked = marks[b]
        for j in range(tiles):
            hit = (marked & (1 << (k * tiles + j))) != 0
            label = jnp.where(hit, struck_value, plain)
            at = slice(j * LANES, (j + 1) * LANES)
            held[step % 2][at, :] = (jnp.tanh(score[at, :]) + label).astype(BF16)

    def use(step):
        k, b = step // number, step % number
        first = parts[k] * SPAN
        residual = held[step % 2][...]
        ent = lax.dot_general(
            residual, queries[b], (((1,), (1,)), ((), ())), preferred_element_type=F32
        )
        ask = jnp.dot(slab[:, first : first + SPAN], residual, preferred_element_type=F32)
        if b:
            ent = totals[...] + ent
        if b < number - 1:
            totals[...] = ent
        else:
            ents[:, k * SPAN : (k + 1) * SPAN] = ent.T[:depth, :].astype(ents.dtype)
        if k:
            ask = asks[base + b] + ask
        elif stage > 1 or stage == 1 and b < 2:
            ask = before[base + b] + ask
        if stage == 3 and b:
            sent[1][...] = ask.astype(BF16)
        elif stage == 3:
            half = width // 2
            for out, at in ((sent[0], slice(0, half)), (sent[2], slice(half, width))):
                out[:, :half] = before[1, :, at].astype(BF16)
                out[:, half:] = ask[:, at].astype(BF16)
        else:
            asks[base + b] = ask

    steps = number * len(parts)
    residual_of(0)
    for step in range(steps):
        if step + 1 < steps:
            residual_of(step + 1)
        use(step)


def score(me, slab, blocks, parts, stage, total_entities, before=None):
    depth = slab.shape[0]
    plain = 1.0 - 2.0 * (0.1 / total_entities)
    shape = jax.ShapeDtypeStruct
    number = len(blocks)
    outs = [pltpu.VMEM((4 if stage else 2, depth, SPAN), F32)]
    if stage == 3:
        outs = [shape((depth, SPAN), F32)] + [shape((depth, SPAN), BF16)] * 3
    outs.append(shape((depth, len(parts) * SPAN), BF16 if stage == 1 else F32))
    scratch = [
        pltpu.VMEM((len(parts) * SPAN, WIDE), BF16),
        pltpu.VMEM((number, WIDE, SPAN), BF16),
        pltpu.VMEM((number, LANES, SPAN), jnp.int32),
        pltpu.VMEM((SPAN, WIDE), F32),
        pltpu.VMEM((SPAN, SPAN), BF16),
        pltpu.VMEM((SPAN, SPAN), BF16),
    ]
    whole = pl.BlockSpec(memory_space=pltpu.VMEM)
    given = [piece for block in blocks for piece in block] + ([before] if stage else [])
    return pl.pallas_call(
        functools.partial(
            score_kernel, plain, plain - 1.8, depth, parts, [len(b) for b in blocks], stage
        ),
        in_specs=[pl.BlockSpec(memory_space=pltpu.SMEM)] + [whole] * (1 + len(given)),
        out_specs=[whole] * len(outs),
        out_shape=outs,
        input_output_aliases={1 + len(given): 0} if stage == 2 else {},
        scratch_shapes=scratch,
        compiler_params=pltpu.CompilerParams(vmem_limit_bytes=VMEM_BYTES),
    )(me, slab, *given)


def body(
    anchor_ids,
    relation_ids,
    head_anchors,
    head_relations,
    query_relation,
    targets,
    anchor_table,
    relation_table,
    enc_weight,
    fc_weight,
):
    width = anchor_ids.shape[0]
    entities = width * 128
    queries = head_anchors.shape[0] * 128
    scale = 0.5 * float(anchor_table.shape[1]) ** (-0.5)
    me = (lax.axis_index("ent") * 16 + lax.axis_index("qry")).astype(jnp.int32)[None]
    ids = jnp.concatenate([anchor_ids.T.reshape(-1), head_anchors.T.reshape(-1)]) * 2
    own_cols, *shared = encode_entities(
        ids,
        anchor_ids.shape[1],
        relation_ids,
        anchor_table,
        relation_table,
        enc_weight,
        scale,
    )
    heads = (head_relations.T, query_relation[None, :], targets.T, fc_weight)
    sent = [moved(own_cols, dx=d) for d in FAR]
    early, own_cols, *shared = encode_heads(0, ids, *heads, own_cols, *shared)
    row = jnp.concatenate([own_cols] + sent, axis=1)
    first = [moved(early, dz=d) for d in (1, 2)]
    sent = [moved(row, dy=d) for d in FAR]
    late, row, query, *shared = encode_heads(1, ids, *heads, row, *shared, early)
    late, query, row, *first = lax.optimization_barrier((late, query, row, *first))
    slab = jnp.concatenate([row] + sent, axis=1)
    other = moved(slab, dcore=1)
    second = [moved(late, dz=d) for d in (1, 2)]
    asks, own_ents = score(me, slab, [[query], first], (0, 1, 2, 3), 0, entities)
    asks, own_ents, last, *second = lax.optimization_barrier(
        (asks, own_ents, moved(query, dz=3), *second)
    )
    blocks = [[query], first, second, [last]]
    asks, away = score(me, other, blocks, (0, 1, 2, 3), 1, entities, asks)
    back = moved(away, dcore=1)
    asks, ents = score(me, slab, blocks[2:], (1, 2, 3), 2, entities, asks)
    span = slab.shape[1] // 4

    def slab_sum(part, k):
        at = slice(k * span, (k + 1) * span)
        return part + own_ents[:, at] + back[:, at].astype(F32)

    ents = [ents[:, k * span : (k + 1) * span] for k in range(3)]
    ents = [slab_sum(part, k + 1).astype(BF16) for k, part in enumerate(ents)]
    ents = [moved(part, dy=-d) for d, part in zip((3, 1, 2), (ents[1], ents[0], ents[2]))]
    query_total, *sums, ent_row = score(me, slab, blocks[2:], (0,), 3, entities, asks)
    ent_row = slab_sum(ent_row, 0)
    for ent in ents:
        ent_row = ent_row + ent.astype(F32)
    for d, part in zip((1, 2, 3), (sums[0], sums[2], sums[1])):
        query_total = query_total + moved(part, dz=-d).astype(F32)
    ent_share = ent_row[:, :width]
    for k, d in ((2, 2), (0, 1), (1, 3)):
        block = ent_row[:, (k + 1) * width : (k + 2) * width].astype(BF16)
        ent_share = ent_share + moved(block, dx=-d).astype(F32)
    return (
        ent_share * (0.5 / math.sqrt(queries)),
        query_total.T * (0.5 / scale / math.sqrt(entities)),
    )


def solution(mesh):
    spread = P(AXES, None)
    placed = (spread, spread, spread, spread, P(AXES), spread, P(), P(), P(), P())
    return jax.shard_map(
        body,
        mesh=mesh,
        in_specs=placed,
        out_specs=(P(None, AXES), spread),
        check_vma=False,
    )
```
